32 devices in a mesh: rows: 8 (over z, core), cols: 4 (over y, x).
Axes of the slice: x: 2, y: 2, z: 4, core: 2. Of those that a mesh axis runs over, the one named last changes fastest.
Arguments:
- inputs: bfloat16 [10240, 512], P('rows'), may hold values from -6 to 6
- reset_flags: int32 [10240], P('rows'), may hold values 0 or 1
- gate_weight: bfloat16 [2, 1024, 4, 4096], P(None, None, None, 'cols'), may hold values from -0.1875 to 0.1875
- gate_bias: float32 [2, 4, 4096], P(None, None, 'cols'), may hold values from -3 to 3
- proj_weight: bfloat16 [2, 4096, 512], P(None, 'cols'), may hold values from -0.25 to 0.25
- grad_out: bfloat16 [10240, 2, 512], P('rows'), may hold values from -6 to 6
Outputs:
- layer_out: bfloat16 [10240, 2, 512], P('rows')
- input_grad: bfloat16 [10240, 512], P('rows', 'cols')
- gate_weight_grad: float32 [2, 1024, 4, 4096], P(None, 'rows', None, 'cols')
- gate_bias_grad: float32 [2, 4, 4096], P(None, None, 'cols')
- proj_weight_grad: float32 [2, 4096, 512], P(None, 'cols', 'rows')
The draws below stay inside these ranges and needn't reach their ends.
Inputs may be any that keep to these rules, and one draw needn't show every extreme that they name: `reset_flags`: 1 marks the first position of a document.
All inputs are finite; a program needn't handle non-finite values. No bound on the sum of `reset_flags` on one device may be relied on, other than what follows from the above.
Results may differ from the reference program's by a relative error of at most 0.017.
Values may be sent and summed in bfloat16 or wider, within the bound.
No kernel may reach another device: no remote copies, remote signals or barrier semaphores. Data moves between devices by JAX's collectives and lax.ppermute only.
A program may use at most 384 MiB of HBM per device.

```python
import jax
import jax.numpy as jnp
from jax import lax

HID = 512
CELL = 4096
STEPS = 20
WIN_DEV = 64
TOKENS = 10240
N_ROWS = 8


def place_ends(values, key, smallest, high):
    longest = values.shape.index(max(values.shape))
    spots = []
    for shift in (0, 1):
        where = [jax.random.randint(jax.random.fold_in(key, axis), (), 0, length) for axis, length in enumerate(values.shape)]
        where[longest] = (where[longest] + shift) % values.shape[longest]
        spots.append(tuple(where))
    return values.at[spots[0]].set(smallest).at[spots[1]].set(high)


def spiked(values, key, source, target, shards_of, factor):
    def block_of(dim):
        return (jnp.arange(values.shape[dim]) // (values.shape[dim] // shards_of)).reshape((-1,) + (1,) * (values.ndim - 1 - dim))

    first = jax.random.permutation(key, shards_of)[block_of(target)]
    other_side = (block_of(target) + shards_of // 2) % shards_of
    return jnp.where((block_of(source) == first) | (block_of(source) == other_side), factor * values, values)


def block_scale(own_key, shape, shards, low, high):
    loudness, own = 1.0, jax.random.fold_in(own_key, 6)
    for dim, parts in shards:
        draws = jnp.exp(jax.random.uniform(jax.random.fold_in(own, dim), (parts,), jnp.float32, low / len(shards), high / len(shards)))
        loudness = loudness * jnp.repeat(draws, shape[dim] // parts).reshape([-1 if axis == dim else 1 for axis in range(len(shape))])
    return loudness


def gaussian(rng, shape, width, limit, cuts=(), kind=jnp.bfloat16):
    loudness = block_scale(rng, shape, cuts, -0.22, 0.18) if cuts else 1.0
    entries = jax.random.normal(rng, shape, jnp.float32) * width * loudness
    return jnp.minimum(jnp.maximum(entries, -limit), limit).astype(kind)


def noise_with(rng, shape, scale, most, split, heavy, kind=jnp.bfloat16):
    entries = scale * jax.random.normal(rng, shape, jnp.float32)
    if split:
        entries = entries * block_scale(rng, shape, split, -0.22, 0.18)
    return jnp.clip(spiked(entries, jax.random.fold_in(rng, 3), *heavy), -most, most).astype(kind)


def setup_inputs(seed: int = 0) -> dict:
    keys = jax.random.split(jax.random.key(seed), 7)
    return {
        "inputs": noise_with(keys[0], (TOKENS, HID), 1.0, 6.0, ((0, 8),), (0, 1, 8, 2.0)),
        "reset_flags": place_ends((jax.random.randint(keys[1], (TOKENS,), 0, 6) < 1).astype(jnp.int32), jax.random.fold_in(keys[1], 1), 0, 1),
        "gate_weight": gaussian(keys[2], (2, 2 * HID, 4, CELL), (2 * HID) ** -0.5, 0.1875, ((3, 4),)),
        "gate_bias": gaussian(keys[3], (2, 4, CELL), 0.5, 3.0, ((2, 4),), jnp.float32),
        "proj_weight": gaussian(keys[4], (2, CELL, HID), (CELL // 8) ** -0.5, 0.25, ((1, 4),)),
        "grad_out": noise_with(keys[5], (TOKENS, 2, HID), 1.0, 6.0, ((0, 8),), (0, 2, 8, 2.0)),
    }


HIGHEST = lax.Precision.HIGHEST

@jax.custom_vjp
def low(v):
    return lax.optimization_barrier(v.astype(jnp.bfloat16)).astype(jnp.float32)

@jax.custom_vjp
def low_back(v):
    return v

def low_keep(v):
    return (low(v), None)

def low_pass(kept, grad):
    return (grad,)

def back_keep(v):
    return (v, None)

def back_low(kept, grad):
    return (low(grad),)
low.defvjp(low_keep, low_pass)
low_back.defvjp(back_keep, back_low)

def soft_clip(amount):
    return 3.0 * jnp.tanh(amount / 3.0)

def one_direction(x_steps, keep_steps, weight, bias_row, proj_matrix):
    w_input = weight[:HID]
    w_recur = weight[HID:]
    batch_rows = x_steps.shape[1]

    def advance(state_pair, pieces):
        hidden, cell_prev = state_pair
        step_input, keep_step = pieces
        kept_hidden = hidden * keep_step
        gate_pre = jnp.dot(step_input, w_input, precision=HIGHEST) + jnp.dot(kept_hidden, w_recur, precision=HIGHEST) + bias_row
        gate_pre = low_back(gate_pre)
        in_gate = jax.nn.sigmoid(gate_pre[:, :CELL])
        forget = jax.nn.sigmoid(gate_pre[:, CELL:2 * CELL])
        update = jnp.tanh(gate_pre[:, 2 * CELL:3 * CELL])
        out_gate = jax.nn.sigmoid(gate_pre[:, 3 * CELL:])
        cell_new = soft_clip(forget * (cell_prev * keep_step) + in_gate * update)
        cell_output = low(out_gate * jnp.tanh(cell_new))
        proj_raw = low_back(jnp.dot(cell_output, proj_matrix, precision=HIGHEST))
        hidden_new = low(soft_clip(proj_raw))
        return ((hidden_new, cell_new), hidden_new)
    init_state = (jnp.zeros((batch_rows, HID), jnp.float32), jnp.zeros((batch_rows, CELL), jnp.float32))
    _, hiddens = lax.scan(advance, init_state, (x_steps, keep_steps))
    return hiddens

def window_block(pieces, weight, bias_row, proj_matrix):
    x_block, keep_ahead, keep_behind = pieces
    x_steps = jnp.swapaxes(x_block, 0, 1)
    ahead_keep = jnp.swapaxes(keep_ahead, 0, 1)[:, :, None]
    behind_keep = jnp.swapaxes(keep_behind, 0, 1)[:, :, None]
    ahead_hidden = one_direction(x_steps, ahead_keep, weight[0], bias_row[0], proj_matrix[0])
    behind_hidden = one_direction(x_steps[::-1], behind_keep[::-1], weight[1], bias_row[1], proj_matrix[1])[::-1]
    both_outputs = jnp.stack([x_steps + ahead_hidden, x_steps + behind_hidden], axis=2)
    return jnp.swapaxes(both_outputs, 0, 1)

def reference(inputs, reset_flags, gate_weight, gate_bias, proj_weight, grad_out):
    windows = WIN_DEV * N_ROWS
    flag_grid = reset_flags.reshape(windows, STEPS).astype(jnp.float32)
    position = lax.broadcasted_iota(jnp.int32, (windows, STEPS), 1)
    keep_ahead = jnp.where(position > 0, 1.0 - flag_grid, jnp.zeros_like(flag_grid))
    next_flags = jnp.concatenate([flag_grid[:, 1:], jnp.zeros((windows, 1), jnp.float32)], axis=1)
    keep_behind = jnp.where(position < STEPS - 1, 1.0 - next_flags, jnp.zeros_like(flag_grid))
    ahead_blocks = keep_ahead.reshape(N_ROWS, WIN_DEV, STEPS)
    behind_blocks = keep_behind.reshape(N_ROWS, WIN_DEV, STEPS)

    def forward(x_all, weight, bias_row, proj_matrix):
        x_blocks = x_all.reshape(N_ROWS, WIN_DEV, STEPS, HID)
        block_fn = jax.checkpoint(lambda pieces: window_block(pieces, weight, bias_row, proj_matrix))
        result = lax.map(block_fn, (x_blocks, ahead_blocks, behind_blocks))
        return result.reshape(TOKENS, 2, HID)
    x_all = inputs.astype(jnp.float32)
    weight = gate_weight.astype(jnp.float32).reshape(2, 2 * HID, 4 * CELL)
    bias_row = gate_bias.astype(jnp.float32).reshape(2, 4 * CELL)
    proj_matrix = proj_weight.astype(jnp.float32)
    layer_out, pull_back = jax.vjp(forward, x_all, weight, bias_row, proj_matrix)
    back_grads = pull_back(grad_out.astype(jnp.float32))
    input_grad = back_grads[0].astype(jnp.bfloat16)
    weight_grad = back_grads[1].reshape(2, 2 * HID, 4, CELL)
    bias_grad = back_grads[2].reshape(2, 4, CELL)
    proj_grad = back_grads[3]
    return (layer_out.astype(jnp.bfloat16), input_grad, weight_grad, bias_grad, proj_grad)
```

```python
import functools

import jax
import jax.numpy as jnp
from jax import lax
from jax.experimental import pallas as pl
from jax.experimental.pallas import tpu as pltpu
from jax.sharding import PartitionSpec as P

STEPS = 20
BF16 = jnp.bfloat16
F32 = jnp.float32
THIRD = 1.0 / 3.0
LANES = 128
BLOCKS = 4
PARTS = 4


def soft_clip(amount):
    return 3.0 * jnp.tanh(amount / 3.0)


def clip_slope(amount):
    tangent = jnp.tanh(amount / 3.0)
    return 1.0 - tangent * tangent


def shared_cells(inputs, reset_flags, gate_weight, gate_bias, proj_weight, grad_out):
    tok_rows, model_width = inputs.shape
    windows = tok_rows // STEPS
    cell_cols = gate_weight.shape[3]
    gate_width = 4 * cell_cols
    share_width = model_width // lax.axis_size("cols")
    column = lax.axis_index("cols") * share_width
    weight = gate_weight.reshape(2, 2 * model_width, gate_width)
    w_input = weight[:, :model_width]
    w_recur = weight[:, model_width:]
    bias_row = gate_bias.reshape(2, 1, gate_width)
    sequence = jnp.swapaxes(inputs.reshape(windows, STEPS, model_width), 0, 1)
    x_stack = jnp.stack([sequence, sequence[::-1]], axis=1)
    flag_grid = jnp.swapaxes(reset_flags.reshape(windows, STEPS), 0, 1).astype(jnp.float32)
    position = lax.broadcasted_iota(jnp.int32, (STEPS, windows), 0)
    keep_ahead = jnp.where(position > 0, 1.0 - flag_grid, 0.0)
    next_flags = jnp.concatenate([flag_grid[1:], jnp.zeros((1, windows), jnp.float32)], axis=0)
    keep_behind = jnp.where(position < STEPS - 1, 1.0 - next_flags, 0.0)
    keep_stack = jnp.stack([keep_ahead, keep_behind[::-1]], axis=1)[..., None]
    input_gates = jnp.einsum("sdwh,dhg->sdwg", x_stack, w_input, preferred_element_type=jnp.float32)

    def forward_step(state_pair, pieces):
        hidden, cell_prev = state_pair
        gates_in, keep_step = pieces
        kept_hidden = hidden * keep_step.astype(jnp.bfloat16)
        gate_pre = (
            gates_in
            + jnp.einsum("dwh,dhg->dwg", kept_hidden, w_recur, preferred_element_type=jnp.float32)
            + bias_row
        )
        in_gate = jax.nn.sigmoid(gate_pre[..., :cell_cols])
        forget = jax.nn.sigmoid(gate_pre[..., cell_cols : 2 * cell_cols])
        update = jnp.tanh(gate_pre[..., 2 * cell_cols : 3 * cell_cols])
        out_gate = jax.nn.sigmoid(gate_pre[..., 3 * cell_cols :])
        kept_cell = cell_prev * keep_step
        cell_new = soft_clip(forget * kept_cell + in_gate * update)
        cell_output = (out_gate * jnp.tanh(cell_new)).astype(jnp.bfloat16)
        partial_raw = jnp.einsum(
            "dwc,dch->dwh", cell_output, proj_weight, preferred_element_type=jnp.float32
        )
        proj_raw = lax.psum(partial_raw, "cols")
        new_hidden = soft_clip(proj_raw).astype(jnp.bfloat16)
        return (
            (new_hidden, cell_new),
            (kept_hidden, gate_pre, kept_cell, cell_new, cell_output, proj_raw, new_hidden),
        )

    init_state = (
        jnp.zeros((2, windows, model_width), jnp.bfloat16),
        jnp.zeros((2, windows, cell_cols), jnp.float32),
    )
    _, fwd_saved = lax.scan(forward_step, init_state, (input_gates, keep_stack))
    kept_all, pre_all, kept_cells, cell_states, cell_outputs, proj_raws, hiddens = fwd_saved
    ahead_hidden = hiddens[:, 0]
    behind_hidden = hiddens[::-1, 1]
    both_outputs = jnp.stack([ahead_hidden, behind_hidden], axis=2).astype(jnp.float32) + sequence[
        :, :, None, :
    ].astype(jnp.float32)
    block_out = (
        jnp.swapaxes(both_outputs, 0, 1).reshape(tok_rows, 2, model_width).astype(jnp.bfloat16)
    )
    out_grid = jnp.transpose(grad_out.reshape(windows, STEPS, 2, model_width), (1, 2, 0, 3))
    grad_stack = jnp.stack([out_grid[:, 0], out_grid[::-1, 1]], axis=1)

    def backward_step(state_pair, pieces):
        recur_part, cell_grad = state_pair
        gate_pre, kept_cell, cell_new, cell_output, proj_raw, grad_step, keep_step = pieces
        recur_sum = lax.psum(recur_part, "cols")
        hidden_grad = grad_step.astype(jnp.float32) + recur_sum
        raw_grad = (hidden_grad * clip_slope(proj_raw)).astype(jnp.bfloat16)
        emit_grad = jnp.einsum(
            "dwh,dch->dwc", raw_grad, proj_weight, preferred_element_type=jnp.float32
        )
        in_gate = jax.nn.sigmoid(gate_pre[..., :cell_cols])
        forget = jax.nn.sigmoid(gate_pre[..., cell_cols : 2 * cell_cols])
        update = jnp.tanh(gate_pre[..., 2 * cell_cols : 3 * cell_cols])
        out_gate = jax.nn.sigmoid(gate_pre[..., 3 * cell_cols :])
        tanh_cell = jnp.tanh(cell_new)
        cell_total = cell_grad + emit_grad * out_gate * (1.0 - tanh_cell * tanh_cell)
        cell_third = cell_new / 3.0
        cell_raw_grad = cell_total * (1.0 - cell_third * cell_third)
        pre_grad = jnp.concatenate(
            [
                cell_raw_grad * update * in_gate * (1.0 - in_gate),
                cell_raw_grad * kept_cell * forget * (1.0 - forget),
                cell_raw_grad * in_gate * (1.0 - update * update),
                emit_grad * tanh_cell * out_gate * (1.0 - out_gate),
            ],
            axis=-1,
        ).astype(jnp.bfloat16)
        recur_next = (
            jnp.einsum("dwg,dhg->dwh", pre_grad, w_recur, preferred_element_type=jnp.float32)
            * keep_step
        )
        cell_next = cell_raw_grad * forget * keep_step
        return ((recur_next, cell_next), (pre_grad, raw_grad))

    zero_state = (
        jnp.zeros((2, windows, model_width), jnp.float32),
        jnp.zeros((2, windows, cell_cols), jnp.float32),
    )
    _, back_saved = lax.scan(
        backward_step,
        zero_state,
        (pre_all, kept_cells, cell_states, cell_outputs, proj_raws, grad_stack, keep_stack),
        reverse=True,
    )
    pre_grads, raw_grads = back_saved
    input_part = jnp.einsum(
        "sdwg,dhg->sdwh", pre_grads, w_input, preferred_element_type=jnp.float32
    )
    input_sum = jnp.swapaxes(input_part[:, 0] + input_part[::-1, 1], 0, 1).reshape(
        tok_rows, model_width
    )
    input_share = lax.psum_scatter(
        input_sum.astype(jnp.bfloat16), "cols", scatter_dimension=1, tiled=True
    ).astype(jnp.float32)
    residual_grad = grad_out[:, 0].astype(jnp.float32) + grad_out[:, 1].astype(jnp.float32)
    input_grad = (
        input_share + lax.dynamic_slice_in_dim(residual_grad, column, share_width, 1)
    ).astype(jnp.bfloat16)
    input_weight_grad = jnp.einsum(
        "sdwh,sdwg->dhg", x_stack, pre_grads, preferred_element_type=jnp.float32
    )
    recur_weight_grad = jnp.einsum(
        "sdwh,sdwg->dhg", kept_all, pre_grads, preferred_element_type=jnp.float32
    )
    weight_grad = jnp.concatenate([input_weight_grad, recur_weight_grad], axis=1).reshape(
        2, 2 * model_width, 4, cell_cols
    )
    proj_grad = jnp.einsum(
        "sdwc,sdwh->dch", cell_outputs, raw_grads, preferred_element_type=jnp.float32
    )
    bias_grad = jnp.sum(pre_grads, axis=(0, 2), dtype=jnp.float32).reshape(2, 4, cell_cols)
    weight_share, proj_share = (
        lax.psum_scatter(
            weight_grad.astype(jnp.bfloat16), "rows", scatter_dimension=1, tiled=True
        ).astype(jnp.float32),
        lax.psum_scatter(
            proj_grad.astype(jnp.bfloat16), "rows", scatter_dimension=2, tiled=True
        ).astype(jnp.float32),
    )
    bias_total = lax.psum(bias_grad, "rows")
    return (block_out, input_grad, weight_share, bias_total, proj_share)


def sigmoid(amount):
    return 0.5 * jnp.tanh(0.5 * amount) + 0.5


def whole(shape):
    return pl.BlockSpec(shape, lambda *_: (0,) * len(shape), pipeline_mode=pl.Buffered(1))


def matmul(a, b):
    return jnp.dot(a, b, preferred_element_type=F32)


def input_kernel(x_ref, w0, w1, w2, w3, bias_ref, out_ref):
    width = w0.shape[1]
    for n, w_ref in enumerate((w0, w1, w2, w3)):
        at = n * width
        out_ref[:, at : at + width] = (matmul(x_ref[...], w_ref[...]) + bias_ref[:, at : at + width]).astype(BF16)


def input_gates(x, weights, bias):
    rows, model = x.shape
    width = weights[0].shape[1]
    tile = rows // 4
    return pl.pallas_call(
        input_kernel,
        grid=(4,),
        out_shape=jax.ShapeDtypeStruct((rows, PARTS * width), BF16),
        in_specs=[pl.BlockSpec((tile, model), lambda n: (n, 0))]
        + [whole(w.shape) for w in weights]
        + [whole(bias.shape)],
        out_specs=pl.BlockSpec((tile, PARTS * width), lambda n: (n, 0)),
        compiler_params=pltpu.CompilerParams(vmem_limit_bytes=32 * 2**20),
        cost_estimate=pl.CostEstimate(
            flops=2 * rows * model * PARTS * width,
            bytes_accessed=2 * (rows + model) * PARTS * width,
            transcendentals=0,
        ),
        name="input_gates",
    )(x, *weights, bias)


def forward_kernel(*refs):
    px_refs, keep_ref = refs[:BLOCKS], refs[BLOCKS]
    w_refs = refs[BLOCKS + 1 : BLOCKS + 1 + BLOCKS * PARTS]
    p_refs = refs[BLOCKS + 1 + BLOCKS * PARTS : BLOCKS + 1 + 2 * BLOCKS * PARTS]
    outs = refs[BLOCKS + 1 + 2 * BLOCKS * PARTS :]
    pre_out, cell_out, emit_own, emit_far, raw_out, kept_out, hid_out, c_scr, h_scr = outs
    step = pl.program_id(0)
    piece, hidden = p_refs[0].shape
    cells = piece * PARTS
    tiles = piece // LANES
    width = 4 * piece
    half = cells // 2
    rows = keep_ref.shape[1]

    @pl.when(step == 0)
    def _():
        c_scr[...] = jnp.zeros_like(c_scr)
        h_scr[...] = jnp.zeros_like(h_scr)

    keep = keep_ref[0][:, :1]
    kept = (h_scr[...] * keep).astype(BF16)
    kept_out[0] = kept
    raw = jnp.zeros((rows, hidden), F32)
    for b in range(BLOCKS):
        parts = []
        for s in range(PARTS):
            pre = px_refs[b][0, :, s * width : (s + 1) * width].astype(F32) + matmul(kept, w_refs[b * PARTS + s][...])
            at = b * 4 * cells + s * width
            pre_out[0, :, at : at + width] = pre.astype(BF16)
            parts.append(pre)
        gates = [
            jnp.concatenate(
                [part[:, (u * 4 + q) * LANES : (u * 4 + q + 1) * LANES] for part in parts for u in range(tiles)], axis=1
            )
            for q in range(4)
        ]
        i, f, u, o = sigmoid(gates[0]), sigmoid(gates[1]), jnp.tanh(gates[2]), sigmoid(gates[3])
        at = b * cells
        kept_cell = c_scr[:, at : at + cells] * keep
        cell = 3.0 * jnp.tanh((f * kept_cell + i * u) * THIRD)
        emit = (o * jnp.tanh(cell)).astype(BF16)
        c_scr[:, at : at + cells] = cell
        cell_out[0, :, at : at + cells] = cell
        emit_own[0, :, b * half : (b + 1) * half] = emit[:, :half]
        emit_far[0, :, b * half : (b + 1) * half] = emit[:, half:]
        proj = jnp.concatenate([p_refs[b * PARTS + s][...] for s in range(PARTS)], axis=0)
        raw = raw + matmul(emit, proj)
    raw_out[0] = raw
    hid = 3.0 * jnp.tanh(raw * THIRD)
    h_scr[...] = hid.astype(BF16).astype(F32)
    hid_out[0] = hid.astype(BF16)


def run_forward(px, keep, weights, projs):
    steps, rows, wide = px[0].shape
    hidden = projs[0].shape[1]
    total = BLOCKS * wide // 4
    block = lambda n: pl.BlockSpec((1, rows, n), lambda t: (t, 0, 0))
    sizes = (4 * total, total, total // 2, total // 2, hidden, hidden, hidden)
    kinds = (BF16, F32, BF16, BF16, F32, BF16, BF16)
    return pl.pallas_call(
        forward_kernel,
        grid=(steps,),
        out_shape=tuple(jax.ShapeDtypeStruct((steps, rows, n), kind) for n, kind in zip(sizes, kinds)),
        in_specs=[block(wide)] * BLOCKS + [block(LANES)] + [whole(w.shape) for w in weights + projs],
        out_specs=tuple(block(n) for n in sizes),
        scratch_shapes=[pltpu.VMEM((rows, total), F32), pltpu.VMEM((rows, hidden), F32)],
        compiler_params=pltpu.CompilerParams(vmem_limit_bytes=48 * 2**20, dimension_semantics=("arbitrary",)),
        cost_estimate=pl.CostEstimate(
            flops=2 * steps * rows * hidden * 5 * total * 8,
            bytes_accessed=steps * rows * total * 24 + 10 * total * hidden,
            transcendentals=steps * rows * total * 6,
        ),
        name="forward_chain",
    )(*px, keep, *weights, *projs)


def backward_kernel(*refs):
    pre_ref, cell_ref, before_ref, raw_ref, grad_ref, keep_ref = refs[:6]
    wt_refs, pt_refs = refs[6 : 6 + BLOCKS * PARTS], refs[6 + BLOCKS * PARTS : 6 + 2 * BLOCKS * PARTS]
    outs = refs[6 + 2 * BLOCKS * PARTS :]
    slabs, draw_out, bias_out, dc_scr, dk_scr = outs[: 4 * BLOCKS], *outs[4 * BLOCKS :]
    step = pl.program_id(0)
    hidden, piece = pt_refs[0].shape
    cells = piece * PARTS
    tiles = piece // LANES
    width = 4 * piece
    chunk = 4 * LANES
    rows = keep_ref.shape[1]

    @pl.when(step == 0)
    def _():
        dc_scr[...] = jnp.zeros_like(dc_scr)
        dk_scr[...] = jnp.zeros_like(dk_scr)
        bias_out[...] = jnp.zeros_like(bias_out)

    keep = keep_ref[0][:, :1]
    tangent = jnp.tanh(raw_ref[0] * THIRD)
    draw = ((grad_ref[0].astype(F32) + dk_scr[...]) * (1.0 - tangent * tangent)).astype(BF16)
    draw_out[0] = draw
    dk = jnp.zeros((rows, hidden), F32)
    for b in range(BLOCKS):
        at = b * cells
        demit = matmul(draw, jnp.concatenate([pt_refs[b * PARTS + s][...] for s in range(PARTS)], axis=1))
        gates = [
            jnp.concatenate(
                [
                    pre_ref[0, :, 4 * at + s * width + (u * 4 + q) * LANES : 4 * at + s * width + (u * 4 + q + 1) * LANES]
                    for s in range(PARTS)
                    for u in range(tiles)
                ],
                axis=1,
            ).astype(F32)
            for q in range(4)
        ]
        i, f, u, o = sigmoid(gates[0]), sigmoid(gates[1]), jnp.tanh(gates[2]), sigmoid(gates[3])
        cell = cell_ref[0, :, at : at + cells]
        kept_cell = before_ref[0, :, at : at + cells] * keep
        tanh_cell = jnp.tanh(cell)
        third = cell * THIRD
        dcell = (dc_scr[:, at : at + cells] + demit * o * (1.0 - tanh_cell * tanh_cell)) * (1.0 - third * third)
        dgates = (
            dcell * u * i * (1.0 - i),
            dcell * kept_cell * f * (1.0 - f),
            dcell * i * (1.0 - u * u),
            demit * tanh_cell * o * (1.0 - o),
        )
        dc_scr[:, at : at + cells] = dcell * f * keep
        for q in range(4):
            folded = dgates[q][:8]
            for r in range(8, rows, 8):
                folded = folded + dgates[q][r : r + 8]
            bias_out[:, (b * 4 + q) * cells : (b * 4 + q + 1) * cells] += folded
        dgates = [dgate.astype(BF16) for dgate in dgates]
        for s in range(PARTS):
            part = jnp.concatenate(
                [
                    dgates[q][:, s * piece + u * LANES : s * piece + (u + 1) * LANES]
                    for u in range(tiles)
                    for q in range(4)
                ],
                axis=1,
            )
            side, quarter = s // 2, s % 2
            for u in range(tiles):
                slabs[(b * 2 + side) * 2 + u][0, :, quarter * chunk : (quarter + 1) * chunk] = part[
                    :, u * chunk : (u + 1) * chunk
                ]
            dk = dk + matmul(part, wt_refs[b * PARTS + s][...])
    dk_scr[...] = dk * keep


def run_backward(pre, cell, raw, grad, keep, weights, projs):
    steps, rows, gates = pre.shape
    total = gates // 4
    hidden, piece = projs[0].shape
    width = 4 * piece
    block = lambda n: pl.BlockSpec((1, rows, n), lambda s: (steps - 1 - s, 0, 0))
    before = pl.BlockSpec((1, rows, total), lambda s: (jnp.maximum(steps - 2 - s, 0), 0, 0))
    shape = lambda n: jax.ShapeDtypeStruct((steps, rows, n), BF16)
    out = pl.pallas_call(
        backward_kernel,
        grid=(steps,),
        out_shape=tuple([shape(width)] * (4 * BLOCKS) + [shape(hidden), jax.ShapeDtypeStruct((8, gates), F32)]),
        in_specs=[block(gates), block(total), before, block(hidden), block(hidden), block(LANES)]
        + [whole(w.shape) for w in weights + projs],
        out_specs=tuple([block(width)] * (4 * BLOCKS) + [block(hidden), pl.BlockSpec((8, gates), lambda s: (0, 0))]),
        scratch_shapes=[pltpu.VMEM((rows, total), F32), pltpu.VMEM((rows, hidden), F32)],
        compiler_params=pltpu.CompilerParams(vmem_limit_bytes=48 * 2**20, dimension_semantics=("arbitrary",)),
        cost_estimate=pl.CostEstimate(
            flops=2 * steps * rows * hidden * 5 * total * 8,
            bytes_accessed=steps * rows * total * 24 + 10 * total * hidden,
            transcendentals=steps * rows * total * 6,
        ),
        name="backward_chain",
    )(pre, cell, cell, raw, grad, keep, *weights, *projs)
    slabs = [[[out[(b * 2 + side) * 2 + u] for u in range(2)] for side in range(2)] for b in range(BLOCKS)]
    return slabs, out[4 * BLOCKS], out[4 * BLOCKS + 1]


def slab_kernel(split, left_ref, draw_ref, own_ref, far_ref, e00, e01, e10, e11, *outs):
    rows = own_ref.shape[0]
    blocks = outs[0].shape[0] * (2 if split else 1)
    depth = left_ref.shape[0] // blocks
    lines = draw_ref.shape[0] // blocks
    group = lines // 4
    chunk = 4 * LANES
    for quarter, (own_emit, far_emit) in enumerate(((e00, e10), (e01, e11))):
        columns = slice(quarter * chunk, (quarter + 1) * chunk)
        dw = matmul(left_ref[:, :rows], own_ref[:, columns]) + matmul(left_ref[:, rows:], far_ref[:, columns])
        dp = matmul(draw_ref[:, :rows], own_emit[...]) + matmul(draw_ref[:, rows:], far_emit[...])
        dw, dp = dw.astype(BF16), dp.astype(BF16)
        for r in range(blocks):
            if split:
                out, to = outs[quarter * 2 + r // (blocks // 2)], r % (blocks // 2)
            else:
                out, to = outs[quarter], r
            out[to, :depth, :] = dw[r * depth : (r + 1) * depth]
            for g in range(4):
                at = r * lines + g * group
                out[to, depth : depth + group, g * LANES : (g + 1) * LANES] = dp[at : at + group]


def slab_grads(split, left, draw, own, far, emit_own, emit_far, b, u):
    rows, wide = own.shape
    chunk = wide // 2
    blocks = 8
    lines = left.shape[0] // blocks + draw.shape[0] // blocks // 4
    at = lambda quarter: (b * 2 + quarter) * 2 + u
    emit = lambda quarter: pl.BlockSpec((rows, LANES), lambda n, quarter=quarter: (0, at(quarter)))
    count = blocks // 2 if split else blocks
    shape = (count, lines, chunk)
    outs = 4 if split else 2
    return pl.pallas_call(
        functools.partial(slab_kernel, split),
        grid=(1,),
        out_shape=[jax.ShapeDtypeStruct(shape, BF16)] * outs,
        in_specs=[whole(left.shape), whole(draw.shape), whole(own.shape), whole(far.shape)]
        + [emit(0), emit(1), emit(0), emit(1)],
        out_specs=[whole(shape)] * outs,
        compiler_params=pltpu.CompilerParams(vmem_limit_bytes=40 * 2**20),
        cost_estimate=pl.CostEstimate(
            flops=4 * rows * wide * left.shape[0], bytes_accessed=4 * rows * wide + 4 * left.size, transcendentals=0
        ),
        name="weight_gradients",
    )(left, draw, own, far, emit_own, emit_own, emit_far, emit_far)


def input_grad_kernel(has_sum, *refs):
    slab_refs, w_refs, out_ref = refs[:4], refs[4:8], refs[-1]
    chunk = 4 * LANES
    total = refs[8][...] if has_sum else None
    for side in range(2):
        for u in range(2):
            for quarter in range(2):
                part = lax.dot_general(
                    slab_refs[side * 2 + u][:, quarter * chunk : (quarter + 1) * chunk],
                    w_refs[side * 2 + quarter][:, u * chunk : (u + 1) * chunk],
                    (((1,), (1,)), ((), ())),
                    preferred_element_type=F32,
                )
                total = part if total is None else total + part
    out_ref[...] = total


def add_input_grad(slabs, weights, total):
    rows = slabs[0].shape[0]
    model, width = weights[0].shape
    tile = rows // 4
    operands = [*slabs, *weights] + ([] if total is None else [total])
    lines = lambda n: pl.BlockSpec((tile, n), lambda s: (s, 0))
    return pl.pallas_call(
        functools.partial(input_grad_kernel, total is not None),
        grid=(4,),
        out_shape=jax.ShapeDtypeStruct((rows, model), F32),
        in_specs=[lines(width)] * 4
        + [whole(w.shape) for w in weights]
        + ([] if total is None else [lines(model)]),
        out_specs=lines(model),
        compiler_params=pltpu.CompilerParams(vmem_limit_bytes=32 * 2**20),
        cost_estimate=pl.CostEstimate(
            flops=8 * rows * width * model, bytes_accessed=8 * rows * width, transcendentals=0
        ),
        name="input_gradient",
    )(*operands)


def after(value, *others):
    return lax.optimization_barrier((value, *others))[0]


def one_direction(inputs, reset_flags, gate_weight, gate_bias, proj_weight, grad_out):
    row, col = lax.axis_index("rows"), lax.axis_index("cols")
    layer, core = row // 2, row % 2
    direction, pair = layer // 2, layer % 2
    model = inputs.shape[1]
    local = inputs.shape[0] // STEPS
    share = local // 4
    rows = 2 * share
    cells = gate_weight.shape[3]
    piece = cells // PARTS
    width = 4 * piece
    tiles = piece // LANES

    def mask_of(r, near):
        odd = (r // 2) % 2
        return (2 if odd else 1) if near else (1 if odd else 2)

    def over_chips(value, near):
        pairs = [(r * 4 + j, r * 4 + (j ^ mask_of(r, near))) for r in range(8) for j in range(4)]
        return lax.ppermute(value, ("rows", "cols"), pairs)

    def over_rows(value, mask):
        return lax.ppermute(value, "rows", [(r, r ^ mask) for r in range(8)])

    core_swap = functools.partial(over_rows, mask=1)
    pair_swap = functools.partial(over_rows, mask=2)
    half_swap = functools.partial(over_rows, mask=4)
    near_mask = jnp.where(pair == 0, 1, 2)
    block_at = [col, col ^ near_mask, col ^ (3 - near_mask), col ^ 3]
    by_dir = lambda pair_of: jnp.where(direction == 0, pair_of[0], pair_of[1])
    by_other = lambda pair_of: jnp.where(direction == 0, pair_of[1], pair_of[0])
    in_run = lambda value: jnp.where(direction == 0, value, value[::-1])

    def cell_of(part):
        return (core ^ (part // 2)) * (2 * piece) + (pair ^ (part % 2)) * piece

    def own_gates(part, first):
        w = lax.dynamic_slice(gate_weight, (direction, first, 0, cell_of(part)), (1, model, 4, piece))
        w = w.reshape(model, 4, tiles, LANES)
        return jnp.swapaxes(w, 1, 2).reshape(model, width)

    w_in = [[None] * PARTS for _ in range(BLOCKS)]
    w_rec = [[None] * PARTS for _ in range(BLOCKS)]
    w_proj = [[None] * PARTS for _ in range(BLOCKS)]
    for part in range(PARTS):
        w_in[0][part] = own_gates(part, 0)
        w_rec[0][part] = own_gates(part, model)
        w_proj[0][part] = lax.dynamic_slice(proj_weight, (direction, cell_of(part), 0), (1, piece, model))[0]
    for store in (w_in, w_rec, w_proj):
        first = w_in is store
        mine = store[0][0]
        store[1][0] = over_chips(mine, True)
        store[2][0] = over_chips(mine if first else after(mine, w_in[2][0]), False)
        store[3][0] = over_chips(store[1][0], False)
        store[1][1] = over_chips(after(store[0][1], store[1][0]), True)
        store[2][1] = pair_swap(store[1][0])
        store[3][1] = pair_swap(store[3][0])
        for b in range(1, BLOCKS):
            for part in range(2):
                store[b][2 + part] = core_swap(store[b][part])

    keep_grid = reset_flags.reshape(local, STEPS).astype(F32)
    position = lax.broadcasted_iota(jnp.int32, (local, STEPS), 1)
    keep_ahead = jnp.where(position > 0, 1.0 - keep_grid, 0.0)
    next_flags = jnp.concatenate([keep_grid[:, 1:], jnp.zeros((local, 1), F32)], axis=1)
    keep_behind = jnp.where(position < STEPS - 1, 1.0 - next_flags, 0.0)
    mine = lambda value: lax.dynamic_slice_in_dim(value, col * share, share, 0)
    steps_first = lambda value: jnp.swapaxes(value, 0, 1)
    x_mine = steps_first(mine(inputs.reshape(local, STEPS, model)))
    g_mine = mine(grad_out.reshape(local, STEPS, 2, model))
    g_dirs = (steps_first(g_mine[:, :, 0]), steps_first(g_mine[:, :, 1]))
    keep_dirs = (steps_first(mine(keep_ahead)), steps_first(mine(keep_behind)))
    keep_wide = [jnp.broadcast_to(k[..., None], (STEPS, share, LANES)).astype(BF16) for k in keep_dirs]
    xk_here = jnp.concatenate([x_mine, by_dir(keep_wide)], axis=2)
    xk_sent = jnp.concatenate([x_mine, by_other(keep_wide)], axis=2)
    xk = in_run(jnp.concatenate([xk_here, half_swap(xk_sent)], axis=1))
    x_run, keep_run = xk[..., :model], xk[..., model:].astype(F32)
    g_run = in_run(jnp.concatenate([by_dir(g_dirs), half_swap(after(by_other(g_dirs), xk))], axis=1))
    x_flat = x_run.reshape(STEPS * rows, model)

    bias_own = lax.dynamic_index_in_dim(gate_bias, direction, 0, keepdims=False)
    bias_near = over_chips(bias_own, True)
    bias_all = (bias_own, bias_near, over_chips(bias_own, False), over_chips(bias_near, False))

    def bias_block(b):
        tiled = bias_all[b].reshape(4, cells // LANES, LANES)
        tiled = jnp.swapaxes(tiled, 0, 1).reshape(1, 4 * cells)
        parts = [lax.dynamic_slice(tiled, (0, 4 * cell_of(part)), (1, width)) for part in range(PARTS)]
        return jnp.concatenate(parts, axis=1)

    px = [input_gates(x_flat, w_in[b], bias_block(b)).reshape(STEPS, rows, PARTS * width) for b in range(BLOCKS)]
    ordered = lambda store: [store[b][part] for b in range(BLOCKS) for part in range(PARTS)]
    turned = lambda store: [jnp.swapaxes(w, 0, 1) for w in ordered(store)]
    pre, cell, emit_own, emit_far, raw, kept, hid = run_forward(px, keep_run, ordered(w_rec), ordered(w_proj))

    hid_time = in_run(hid)
    hid_here, hid_there = hid_time[:, :share], half_swap(hid_time[:, share:])
    hid_both = (by_dir((hid_here, hid_there)), by_other((hid_here, hid_there)))
    x_wide = x_mine.astype(F32)
    out_mine = jnp.stack([(x_wide + h.astype(F32)).astype(BF16) for h in hid_both], axis=2)
    out_mine = jnp.swapaxes(out_mine, 0, 1).reshape(share * STEPS, 2 * model)
    out_near = over_chips(out_mine, True)
    out_parts = (out_mine, out_near, over_chips(out_mine, False), over_chips(out_near, False))

    def by_column(parts):
        whole_rows = jnp.zeros((BLOCKS * parts[0].shape[0], parts[0].shape[1]), parts[0].dtype)
        for b, value in enumerate(parts):
            whole_rows = lax.dynamic_update_slice(whole_rows, value, (block_at[b] * value.shape[0], 0))
        return whole_rows

    block_out = by_column(out_parts).reshape(local * STEPS, 2, model)

    flat = lambda value: value.reshape(STEPS * rows, value.shape[-1])
    row_at = [
        (((half ^ direction) * 2 + (layer_of ^ pair)) * 2 + (side ^ core))
        for layer_of in range(2)
        for half in range(2)
        for side in range(2)
    ]

    def turned_rows(value):
        both = jnp.concatenate([value, core_swap(value)], axis=0)
        blocked = jnp.swapaxes(both, 0, 1).reshape(8, value.shape[1] // 8, 2 * value.shape[0])
        picked = [lax.dynamic_index_in_dim(blocked, at, 0, keepdims=False) for at in row_at]
        return jnp.concatenate(picked, axis=0)

    left = turned_rows(jnp.concatenate([x_flat, flat(kept)], axis=1))
    emit_own, emit_far = flat(emit_own), core_swap(flat(emit_far))

    slabs, draw, bias_sums = run_backward(pre, cell, raw, g_run, keep_run, turned(w_rec), turned(w_proj))

    slabs = [[[flat(value) for value in side] for side in block] for block in slabs]
    draw_turned = turned_rows(flat(draw))
    moved = [[core_swap(slabs[b][1][u]) for u in range(2)] for b in range(BLOCKS)]

    def grads(b, u, split):
        return slab_grads(split, left, draw_turned, slabs[b][0][u], moved[b][u], emit_own, emit_far, b, u)

    def add(first, *others):
        total = first.astype(F32)
        for other in others:
            total = total + other.astype(F32)
        return total.astype(BF16)

    def pair_sums(mine_a, sent_a, mine_b, sent_b, met=None):
        met = (mine_a, sent_a, mine_b, sent_b) if met is None else met
        return add(mine_a, pair_swap(met[3])), add(mine_b, pair_swap(met[1]))

    def chip_sums(opposite, near, other, own):
        relay_a = over_chips(opposite[0], True)
        relay_b = over_chips(opposite[1], False)
        near_a = over_chips(near[0], True)
        other_a = over_chips(add(other[0], relay_a), False)
        near_b = over_chips(add(near[1], relay_b), True)
        other_b = over_chips(other[1], False)
        return (own[0], near_a, other_a), (own[1], near_b, other_b)

    tile0 = [grads(b, 0, False) for b in (3, 1, 2, 0)]
    sums0 = [add(*parts) for parts in chip_sums(*tile0)]
    count = sums0[0].shape[0] // 2
    sums0 = pair_sums(sums0[0][:count], sums0[0][count:], sums0[1][:count], sums0[1][count:])
    opposite, near, other, own = [grads(b, 1, True) for b in (3, 1, 2, 0)]
    tile1 = [pair_sums(*opposite), pair_sums(*near, met=other), pair_sums(*other, met=near), pair_sums(*own)]
    sums1 = [add(*parts) for parts in chip_sums(*tile1)]

    final = [[None] * 2 for _ in range(2)]
    for u, sums in enumerate((sums0, sums1)):
        for quarter in range(2):
            value = sums[quarter]
            here, there = value[:2], half_swap(value[2:])
            both = jnp.stack([by_dir((here, there)), by_other((here, there))], axis=1)
            kept_part, got_part = both[0], core_swap(both[1])
            sides = [jnp.where(core == which, kept_part, got_part) for which in range(2)]
            final[quarter][u] = jnp.stack(sides, axis=2)
    depth = 2 * model // 8
    quarters = [jnp.stack(final[quarter], axis=3) for quarter in range(2)]
    ordered_quarters = (
        jnp.where(pair == 0, quarters[0], quarters[1]),
        jnp.where(pair == 0, quarters[1], quarters[0]),
    )
    full = jnp.stack(ordered_quarters, axis=3).reshape(2, -1, 2, 2, 2, 4, LANES)
    weight_share = jnp.transpose(full[:, :depth], (0, 1, 5, 2, 3, 4, 6)).reshape(2, depth, 4, cells).astype(F32)
    proj_share = jnp.transpose(full[:, depth:], (0, 2, 3, 4, 6, 5, 1)).reshape(2, cells, model // 8).astype(F32)

    bias_parts = jnp.sum(bias_sums, axis=0).reshape(BLOCKS, 4, 2, 2 * piece)
    bias_half = bias_parts[:, :, 0] + core_swap(bias_parts[:, :, 1])
    bias_near = over_chips(bias_half[1], True)
    bias_other = over_chips(bias_half[2], False)
    bias_far = lax.ppermute(bias_half[3], "cols", [(j, j ^ 3) for j in range(4)])
    bias_half = bias_half[0] + bias_near + bias_other + bias_far
    bias_half = jnp.where(pair == 0, bias_half, jnp.concatenate([bias_half[:, piece:], bias_half[:, :piece]], axis=1))
    bias_half = bias_half + pair_swap(bias_half)
    bias_there = half_swap(bias_half)
    bias_half = jnp.stack([by_dir((bias_half, bias_there)), by_other((bias_half, bias_there))])
    bias_side = core_swap(bias_half)
    bias_total = jnp.concatenate(
        [jnp.where(core == which, bias_half, bias_side) for which in range(2)], axis=2
    )

    wide = None
    for b in range(BLOCKS):
        wide = add_input_grad([slabs[b][side][u] for side in range(2) for u in range(2)], w_in[b], wide)
    dx = in_run(wide.reshape(STEPS, rows, model))
    dx = dx[:, :share] + half_swap(dx[:, share:].astype(BF16)).astype(F32)
    dx = (dx + g_dirs[0].astype(F32) + g_dirs[1].astype(F32)).astype(BF16)
    dx = jnp.swapaxes(dx, 0, 1).reshape(share * STEPS, model)
    slice_for = lambda at: lax.dynamic_slice_in_dim(dx, at * (model // 4), model // 4, 1)
    dx_parts = (
        slice_for(block_at[0]),
        over_chips(slice_for(block_at[1]), True),
        over_chips(slice_for(block_at[2]), False),
        lax.ppermute(slice_for(block_at[3]), "cols", [(j, j ^ 3) for j in range(4)]),
    )
    input_grad = by_column(dx_parts)
    return (block_out, input_grad, weight_share, bias_total, proj_share)


def solution(mesh):
    placed = (
        P("rows", None),
        P("rows"),
        P(None, None, None, "cols"),
        P(None, None, "cols"),
        P(None, "cols", None),
        P("rows", None, None),
    )
    plan = one_direction if (mesh.shape["rows"], mesh.shape["cols"]) == (8, 4) else shared_cells
    return jax.shard_map(
        plan,
        mesh=mesh,
        in_specs=placed,
        out_specs=(
            P("rows", None, None),
            P("rows", "cols"),
            P(None, "rows", None, "cols"),
            P(None, None, "cols"),
            P(None, "cols", "rows"),
        ),
        check_vma=False,
    )
```

```python
import functools

import jax
import jax.numpy as jnp
from jax import lax
from jax.experimental import pallas as pl
from jax.experimental.pallas import tpu as pltpu
from jax.sharding import PartitionSpec as P

STEPS = 20
BF16 = jnp.bfloat16
F32 = jnp.float32
THIRD = 1.0 / 3.0
LANES = 128
BLOCKS = 4
LIGHT = pl.CostEstimate(flops=1, bytes_accessed=1, transcendentals=0)
PARTS = 4


def soft_clip(amount):
    return 3.0 * jnp.tanh(amount / 3.0)


def clip_slope(amount):
    tangent = jnp.tanh(amount / 3.0)
    return 1.0 - tangent * tangent


def shared_cells(inputs, reset_flags, gate_weight, gate_bias, proj_weight, grad_out):
    tok_rows, model_width = inputs.shape
    windows = tok_rows // STEPS
    cell_cols = gate_weight.shape[3]
    gate_width = 4 * cell_cols
    share_width = model_width // lax.axis_size("cols")
    column = lax.axis_index("cols") * share_width
    weight = gate_weight.reshape(2, 2 * model_width, gate_width)
    w_input = weight[:, :model_width]
    w_recur = weight[:, model_width:]
    bias_row = gate_bias.reshape(2, 1, gate_width)
    sequence = jnp.swapaxes(inputs.reshape(windows, STEPS, model_width), 0, 1)
    x_stack = jnp.stack([sequence, sequence[::-1]], axis=1)
    flag_grid = jnp.swapaxes(reset_flags.reshape(windows, STEPS), 0, 1).astype(jnp.float32)
    position = lax.broadcasted_iota(jnp.int32, (STEPS, windows), 0)
    keep_ahead = jnp.where(position > 0, 1.0 - flag_grid, 0.0)
    next_flags = jnp.concatenate([flag_grid[1:], jnp.zeros((1, windows), jnp.float32)], axis=0)
    keep_behind = jnp.where(position < STEPS - 1, 1.0 - next_flags, 0.0)
    keep_stack = jnp.stack([keep_ahead, keep_behind[::-1]], axis=1)[..., None]
    input_gates = jnp.einsum("sdwh,dhg->sdwg", x_stack, w_input, preferred_element_type=jnp.float32)

    def forward_step(state_pair, pieces):
        hidden, cell_prev = state_pair
        gates_in, keep_step = pieces
        kept_hidden = hidden * keep_step.astype(jnp.bfloat16)
        gate_pre = (
            gates_in
            + jnp.einsum("dwh,dhg->dwg", kept_hidden, w_recur, preferred_element_type=jnp.float32)
            + bias_row
        )
        in_gate = jax.nn.sigmoid(gate_pre[..., :cell_cols])
        forget = jax.nn.sigmoid(gate_pre[..., cell_cols : 2 * cell_cols])
        update = jnp.tanh(gate_pre[..., 2 * cell_cols : 3 * cell_cols])
        out_gate = jax.nn.sigmoid(gate_pre[..., 3 * cell_cols :])
        kept_cell = cell_prev * keep_step
        cell_new = soft_clip(forget * kept_cell + in_gate * update)
        cell_output = (out_gate * jnp.tanh(cell_new)).astype(jnp.bfloat16)
        partial_raw = jnp.einsum(
            "dwc,dch->dwh", cell_output, proj_weight, preferred_element_type=jnp.float32
        )
        proj_raw = lax.psum(partial_raw, "cols")
        new_hidden = soft_clip(proj_raw).astype(jnp.bfloat16)
        return (
            (new_hidden, cell_new),
            (kept_hidden, gate_pre, kept_cell, cell_new, cell_output, proj_raw, new_hidden),
        )

    init_state = (
        jnp.zeros((2, windows, model_width), jnp.bfloat16),
        jnp.zeros((2, windows, cell_cols), jnp.float32),
    )
    _, fwd_saved = lax.scan(forward_step, init_state, (input_gates, keep_stack))
    kept_all, pre_all, kept_cells, cell_states, cell_outputs, proj_raws, hiddens = fwd_saved
    ahead_hidden = hiddens[:, 0]
    behind_hidden = hiddens[::-1, 1]
    both_outputs = jnp.stack([ahead_hidden, behind_hidden], axis=2).astype(jnp.float32) + sequence[
        :, :, None, :
    ].astype(jnp.float32)
    block_out = (
        jnp.swapaxes(both_outputs, 0, 1).reshape(tok_rows, 2, model_width).astype(jnp.bfloat16)
    )
    out_grid = jnp.transpose(grad_out.reshape(windows, STEPS, 2, model_width), (1, 2, 0, 3))
    grad_stack = jnp.stack([out_grid[:, 0], out_grid[::-1, 1]], axis=1)

    def backward_step(state_pair, pieces):
        recur_part, cell_grad = state_pair
        gate_pre, kept_cell, cell_new, cell_output, proj_raw, grad_step, keep_step = pieces
        recur_sum = lax.psum(recur_part, "cols")
        hidden_grad = grad_step.astype(jnp.float32) + recur_sum
        raw_grad = (hidden_grad * clip_slope(proj_raw)).astype(jnp.bfloat16)
        emit_grad = jnp.einsum(
            "dwh,dch->dwc", raw_grad, proj_weight, preferred_element_type=jnp.float32
        )
        in_gate = jax.nn.sigmoid(gate_pre[..., :cell_cols])
        forget = jax.nn.sigmoid(gate_pre[..., cell_cols : 2 * cell_cols])
        update = jnp.tanh(gate_pre[..., 2 * cell_cols : 3 * cell_cols])
        out_gate = jax.nn.sigmoid(gate_pre[..., 3 * cell_cols :])
        tanh_cell = jnp.tanh(cell_new)
        cell_total = cell_grad + emit_grad * out_gate * (1.0 - tanh_cell * tanh_cell)
        cell_third = cell_new / 3.0
        cell_raw_grad = cell_total * (1.0 - cell_third * cell_third)
        pre_grad = jnp.concatenate(
            [
                cell_raw_grad * update * in_gate * (1.0 - in_gate),
                cell_raw_grad * kept_cell * forget * (1.0 - forget),
                cell_raw_grad * in_gate * (1.0 - update * update),
                emit_grad * tanh_cell * out_gate * (1.0 - out_gate),
            ],
            axis=-1,
        ).astype(jnp.bfloat16)
        recur_next = (
            jnp.einsum("dwg,dhg->dwh", pre_grad, w_recur, preferred_element_type=jnp.float32)
            * keep_step
        )
        cell_next = cell_raw_grad * forget * keep_step
        return ((recur_next, cell_next), (pre_grad, raw_grad))

    zero_state = (
        jnp.zeros((2, windows, model_width), jnp.float32),
        jnp.zeros((2, windows, cell_cols), jnp.float32),
    )
    _, back_saved = lax.scan(
        backward_step,
        zero_state,
        (pre_all, kept_cells, cell_states, cell_outputs, proj_raws, grad_stack, keep_stack),
        reverse=True,
    )
    pre_grads, raw_grads = back_saved
    input_part = jnp.einsum(
        "sdwg,dhg->sdwh", pre_grads, w_input, preferred_element_type=jnp.float32
    )
    input_sum = jnp.swapaxes(input_part[:, 0] + input_part[::-1, 1], 0, 1).reshape(
        tok_rows, model_width
    )
    input_share = lax.psum_scatter(
        input_sum.astype(jnp.bfloat16), "cols", scatter_dimension=1, tiled=True
    ).astype(jnp.float32)
    residual_grad = grad_out[:, 0].astype(jnp.float32) + grad_out[:, 1].astype(jnp.float32)
    input_grad = (
        input_share + lax.dynamic_slice_in_dim(residual_grad, column, share_width, 1)
    ).astype(jnp.bfloat16)
    input_weight_grad = jnp.einsum(
        "sdwh,sdwg->dhg", x_stack, pre_grads, preferred_element_type=jnp.float32
    )
    recur_weight_grad = jnp.einsum(
        "sdwh,sdwg->dhg", kept_all, pre_grads, preferred_element_type=jnp.float32
    )
    weight_grad = jnp.concatenate([input_weight_grad, recur_weight_grad], axis=1).reshape(
        2, 2 * model_width, 4, cell_cols
    )
    proj_grad = jnp.einsum(
        "sdwc,sdwh->dch", cell_outputs, raw_grads, preferred_element_type=jnp.float32
    )
    bias_grad = jnp.sum(pre_grads, axis=(0, 2), dtype=jnp.float32).reshape(2, 4, cell_cols)
    weight_share, proj_share = (
        lax.psum_scatter(
            weight_grad.astype(jnp.bfloat16), "rows", scatter_dimension=1, tiled=True
        ).astype(jnp.float32),
        lax.psum_scatter(
            proj_grad.astype(jnp.bfloat16), "rows", scatter_dimension=2, tiled=True
        ).astype(jnp.float32),
    )
    bias_total = lax.psum(bias_grad, "rows")
    return (block_out, input_grad, weight_share, bias_total, proj_share)


def sigmoid(amount):
    return 0.5 * jnp.tanh(0.5 * amount) + 0.5


def whole(shape):
    return pl.BlockSpec(shape, lambda *_: (0,) * len(shape), pipeline_mode=pl.Buffered(1))


def matmul(a, b):
    return jnp.dot(a, b, preferred_element_type=F32)


def own_piece_kernel(order_ref, w_ref, extra_ref, out_ref):
    step = pl.program_id(0)
    lines = w_ref.shape[1]
    model, width = extra_ref.shape[-1] if extra_ref.shape[1] > 4 else None, out_ref.shape[1]
    for u in range(2):
        for q in range(4):
            to = (u * 4 + q) * LANES
            out_ref[pl.ds(step * lines, lines), to : to + LANES] = w_ref[0, :, q, u * LANES : (u + 1) * LANES]
    base = width // 2

    @pl.when(step == 0)
    def _():
        if model is None:
            rest = jnp.concatenate(
                [extra_ref[0, q : q + 1, u * LANES : (u + 1) * LANES] for u in range(2) for q in range(4)], axis=1
            )
            parts = []
            for _ in range(3):
                parts.append(rest.astype(BF16).astype(F32))
                rest = rest - parts[-1]
            parts.append(jnp.zeros((13, width), F32))
            out_ref[base:, :] = jnp.concatenate(parts, axis=0).astype(BF16)
        else:
            half = extra_ref.shape[1] // 2
            out_ref[base:, :model] = extra_ref[0, :half, :]
            out_ref[base:, model:] = extra_ref[0, half:, :]


def own_piece(place, gate_weight, extra, recurrent, memory=16):
    model, piece = gate_weight.shape[1] // 2, gate_weight.shape[3] // PARTS
    cut = model // 4
    first = 4 if recurrent else 0
    if recurrent:
        extra_spec = pl.BlockSpec((1, piece, model), lambda n, p: (p[0], p[1], 0))
    else:
        extra_spec = pl.BlockSpec((1, 4, piece), lambda n, p: (p[0], 0, p[1]))
    lines = model + (piece // 2 if recurrent else 16)
    return pl.pallas_call(
        own_piece_kernel,
        grid_spec=pltpu.PrefetchScalarGridSpec(
            num_scalar_prefetch=1,
            grid=(4,),
            in_specs=[pl.BlockSpec((1, cut, 4, piece), lambda n, p: (p[0], n + first, 0, p[1])), extra_spec],
            out_specs=pl.BlockSpec((lines, 4 * piece), lambda n, p: (0, 0)),
        ),
        out_shape=jax.ShapeDtypeStruct((lines, 4 * piece), BF16),
        compiler_params=pltpu.CompilerParams(vmem_limit_bytes=memory * 2**20, dimension_semantics=("arbitrary",)),
        cost_estimate=LIGHT,
        name="own_piece",
    )(place, gate_weight, extra)


def input_kernel(x_ref, w0, w1, w2, w3, out_ref):
    model, width = x_ref.shape[1], w0.shape[1]
    for n, w_ref in enumerate((w0, w1, w2, w3)):
        bias = jnp.sum(w_ref[model:, :].astype(F32), axis=0, keepdims=True)
        out_ref[:, n * width : (n + 1) * width] = (matmul(x_ref[...], w_ref[:model, :]) + bias).astype(BF16)


def input_gates(x, weights):
    rows, model = x.shape
    width = weights[0].shape[1]
    tile = rows // 2
    return pl.pallas_call(
        input_kernel,
        grid=(2,),
        out_shape=jax.ShapeDtypeStruct((rows, PARTS * width), BF16),
        in_specs=[pl.BlockSpec((tile, model), lambda n: (n, 0))] + [whole(w.shape) for w in weights],
        out_specs=pl.BlockSpec((tile, PARTS * width), lambda n: (n, 0)),
        compiler_params=pltpu.CompilerParams(vmem_limit_bytes=20 * 2**20),
        cost_estimate=LIGHT,
        name="input_gates",
    )(x, *weights)


def forward_kernel(*refs):
    px_refs, keep_ref = refs[:BLOCKS], refs[BLOCKS]
    w_refs = refs[BLOCKS + 1 : BLOCKS + 1 + BLOCKS * PARTS]
    pre_out, cell_out, emit_own, emit_far, raw_out, kept_out, hid_out, c_scr, h_scr = refs[BLOCKS + 1 + BLOCKS * PARTS :]
    step = pl.program_id(0)
    width = w_refs[0].shape[1]
    hidden = width // 2
    piece = width // 4
    cells = piece * PARTS
    tiles = piece // LANES
    half = cells // 2
    rows = keep_ref.shape[1]

    @pl.when(step == 0)
    def _():
        c_scr[...] = jnp.zeros_like(c_scr)
        h_scr[...] = jnp.zeros_like(h_scr)

    keep = keep_ref[0][:, :1]
    kept = (h_scr[...] * keep).astype(BF16)
    kept_out[0] = kept
    raw = jnp.zeros((rows, hidden), F32)
    for b in range(BLOCKS):
        parts, proj = [], []
        for s in range(PARTS):
            w_ref = w_refs[b * PARTS + s]
            pre = px_refs[b][0, :, s * width : (s + 1) * width].astype(F32) + matmul(kept, w_ref[:hidden, :])
            at = b * 4 * cells + s * width
            pre_out[0, :, at : at + width] = pre.astype(BF16)
            parts.append(pre)
            proj += [w_ref[hidden:, :hidden], w_ref[hidden:, hidden:]]
        gates = [
            jnp.concatenate(
                [part[:, (u * 4 + q) * LANES : (u * 4 + q + 1) * LANES] for part in parts for u in range(tiles)], axis=1
            )
            for q in range(4)
        ]
        i, f, u, o = sigmoid(gates[0]), sigmoid(gates[1]), jnp.tanh(gates[2]), sigmoid(gates[3])
        at = b * cells
        kept_cell = c_scr[:, at : at + cells] * keep
        cell = 3.0 * jnp.tanh((f * kept_cell + i * u) * THIRD)
        emit = (o * jnp.tanh(cell)).astype(BF16)
        c_scr[:, at : at + cells] = cell
        cell_out[0, :, at : at + cells] = cell
        emit_own[0, :, b * half : (b + 1) * half] = emit[:, :half]
        emit_far[0, :, b * half : (b + 1) * half] = emit[:, half:]
        raw = raw + matmul(emit, jnp.concatenate(proj, axis=0))
    raw_out[0] = raw
    hid = 3.0 * jnp.tanh(raw * THIRD)
    h_scr[...] = hid.astype(BF16).astype(F32)
    hid_out[0] = hid.astype(BF16)


def run_forward(px, keep, weights):
    steps, rows, wide = px[0].shape
    hidden = weights[0].shape[1] // 2
    total = BLOCKS * wide // 4
    block = lambda n: pl.BlockSpec((1, rows, n), lambda t: (t, 0, 0))
    sizes = (4 * total, total, total // 2, total // 2, hidden, hidden, hidden)
    kinds = (BF16, F32, BF16, BF16, F32, BF16, BF16)
    return pl.pallas_call(
        forward_kernel,
        grid=(steps,),
        out_shape=tuple(jax.ShapeDtypeStruct((steps, rows, n), kind) for n, kind in zip(sizes, kinds)),
        in_specs=[block(wide)] * BLOCKS + [block(LANES)] + [whole(w.shape) for w in weights],
        out_specs=tuple(block(n) for n in sizes),
        scratch_shapes=[pltpu.VMEM((rows, total), F32), pltpu.VMEM((rows, hidden), F32)],
        compiler_params=pltpu.CompilerParams(vmem_limit_bytes=48 * 2**20, dimension_semantics=("arbitrary",)),
        cost_estimate=pl.CostEstimate(
            flops=2 * steps * rows * hidden * 5 * total * 8,
            bytes_accessed=steps * rows * total * 24 + 10 * total * hidden,
            transcendentals=steps * rows * total * 6,
        ),
        name="forward_chain",
    )(*px, keep, *weights)


def backward_kernel(*refs):
    pre_ref, cell_ref, before_ref, raw_ref, grad_ref, keep_ref = refs[:6]
    wt_refs, pt_refs = refs[6 : 6 + BLOCKS * PARTS], refs[6 + BLOCKS * PARTS : 6 + 2 * BLOCKS * PARTS]
    outs = refs[6 + 2 * BLOCKS * PARTS :]
    slabs, draw_out, bias_out, dc_scr, dk_scr = outs[: 2 * BLOCKS], *outs[2 * BLOCKS :]
    step = pl.program_id(0)
    hidden, piece = pt_refs[0].shape
    cells = piece * PARTS
    tiles = piece // LANES
    width = 4 * piece
    chunk = 4 * LANES
    rows = keep_ref.shape[1]

    @pl.when(step == 0)
    def _():
        dc_scr[...] = jnp.zeros_like(dc_scr)
        dk_scr[...] = jnp.zeros_like(dk_scr)
        bias_out[...] = jnp.zeros_like(bias_out)

    keep = keep_ref[0][:, :1]
    tangent = jnp.tanh(raw_ref[0] * THIRD)
    draw = ((grad_ref[0].astype(F32) + dk_scr[...]) * (1.0 - tangent * tangent)).astype(BF16)
    draw_out[0] = draw
    dk = jnp.zeros((rows, hidden), F32)
    for b in range(BLOCKS):
        at = b * cells
        demit = matmul(draw, jnp.concatenate([pt_refs[b * PARTS + s][...] for s in range(PARTS)], axis=1))
        gates = [
            jnp.concatenate(
                [
                    pre_ref[0, :, 4 * at + s * width + (u * 4 + q) * LANES : 4 * at + s * width + (u * 4 + q + 1) * LANES]
                    for s in range(PARTS)
                    for u in range(tiles)
                ],
                axis=1,
            ).astype(F32)
            for q in range(4)
        ]
        i, f, u, o = sigmoid(gates[0]), sigmoid(gates[1]), jnp.tanh(gates[2]), sigmoid(gates[3])
        cell = cell_ref[0, :, at : at + cells]
        kept_cell = before_ref[0, :, at : at + cells] * keep
        tanh_cell = jnp.tanh(cell)
        third = cell * THIRD
        dcell = (dc_scr[:, at : at + cells] + demit * o * (1.0 - tanh_cell * tanh_cell)) * (1.0 - third * third)
        dgates = (
            dcell * u * i * (1.0 - i),
            dcell * kept_cell * f * (1.0 - f),
            dcell * i * (1.0 - u * u),
            demit * tanh_cell * o * (1.0 - o),
        )
        dc_scr[:, at : at + cells] = dcell * f * keep
        for q in range(4):
            folded = dgates[q][:8]
            for r in range(8, rows, 8):
                folded = folded + dgates[q][r : r + 8]
            bias_out[:, (b * 4 + q) * cells : (b * 4 + q + 1) * cells] += folded
        dgates = [dgate.astype(BF16) for dgate in dgates]
        for s in range(PARTS):
            part = jnp.concatenate(
                [
                    dgates[q][:, s * piece + u * LANES : s * piece + (u + 1) * LANES]
                    for u in range(tiles)
                    for q in range(4)
                ],
                axis=1,
            )
            side, quarter = s // 2, s % 2
            for u in range(tiles):
                to = (u * 2 + quarter) * chunk
                slabs[b * 2 + side][0, :, to : to + chunk] = part[:, u * chunk : (u + 1) * chunk]
            dk = dk + matmul(part, wt_refs[b * PARTS + s][...])
    dk_scr[...] = dk * keep


def run_backward(pre, cell, raw, grad, keep, weights, projs):
    steps, rows, gates = pre.shape
    total = gates // 4
    hidden, piece = projs[0].shape
    half = PARTS * piece * 2
    block = lambda n: pl.BlockSpec((1, rows, n), lambda s: (steps - 1 - s, 0, 0))
    before = pl.BlockSpec((1, rows, total), lambda s: (jnp.maximum(steps - 2 - s, 0), 0, 0))
    shape = lambda n: jax.ShapeDtypeStruct((steps, rows, n), BF16)
    out = pl.pallas_call(
        backward_kernel,
        grid=(steps,),
        out_shape=tuple([shape(half)] * (2 * BLOCKS) + [shape(hidden), jax.ShapeDtypeStruct((8, gates), F32)]),
        in_specs=[block(gates), block(total), before, block(hidden), block(hidden), block(LANES)]
        + [whole(w.shape) for w in [*weights, *projs]],
        out_specs=tuple([block(half)] * (2 * BLOCKS) + [block(hidden), pl.BlockSpec((8, gates), lambda s: (0, 0))]),
        scratch_shapes=[pltpu.VMEM((rows, total), F32), pltpu.VMEM((rows, hidden), F32)],
        compiler_params=pltpu.CompilerParams(vmem_limit_bytes=48 * 2**20, dimension_semantics=("arbitrary",)),
        cost_estimate=pl.CostEstimate(
            flops=2 * steps * rows * hidden * 5 * total * 8,
            bytes_accessed=steps * rows * total * 24 + 10 * total * hidden,
            transcendentals=steps * rows * total * 6,
        ),
        name="backward_chain",
    )(pre, cell, cell, raw, grad, keep, *weights, *projs)
    return [out[b * 2 : b * 2 + 2] for b in range(BLOCKS)], out[2 * BLOCKS], out[2 * BLOCKS + 1]


def block_kernel(order_ref, x_ref, kept_ref, draw_ref, own_ref, far_ref, own_emit, far_emit, *refs):
    first_a, first_b, second_here, second_there, right, emit = refs
    rows = own_ref.shape[0]
    tile, step = pl.program_id(0), pl.program_id(1)
    depth, lines = x_ref.shape[0] // 4, draw_ref.shape[0] // 8
    group = lines // 4
    chunk = 4 * LANES
    first = order_ref[1]
    here, half = (step // 2) ^ order_ref[2], (step % 2) ^ order_ref[0]

    @pl.when(step == 0)
    def _():
        right[:rows, :], right[rows:, :] = own_ref[...], far_ref[...]
        for u in range(2):

            @pl.when(tile == u)
            def _():
                for quarter in range(2):
                    to, at = quarter * LANES, (quarter * 2 + u) * LANES
                    emit[:rows, to : to + LANES] = own_emit[:, at : at + LANES]
                    emit[rows:, to : to + LANES] = far_emit[:, at : at + LANES]

    def body(left_ref):
        left = left_ref[pl.ds(here * (2 * depth), 2 * depth), :]
        dp = matmul(draw_ref[pl.ds((half * 2 + here) * (2 * lines), 2 * lines), :], emit[...]).astype(BF16)
        for quarter in range(2):
            dw = matmul(left, right[:, quarter * chunk : (quarter + 1) * chunk]).astype(BF16)

            def store(out):
                for side in range(2):
                    to = side ^ first
                    out[to, :depth, :] = dw[side * depth : (side + 1) * depth]
                    for g in range(4):
                        at = side * lines + g * group
                        out[to, depth : depth + group, g * LANES : (g + 1) * LANES] = dp[
                            at : at + group, quarter * LANES : (quarter + 1) * LANES
                        ]

            pl.when(tile == 0)(lambda: store((first_a, first_b)[quarter]))
            pl.when((tile == 1) & (step < 2))(lambda: store(second_here.at[quarter]))
            pl.when((tile == 1) & (step >= 2))(lambda: store(second_there.at[quarter]))

    pl.when(half == 0)(lambda: body(x_ref))
    pl.when(half == 1)(lambda: body(kept_ref))


def block_grads(order, x_turned, kept_turned, draw_turned, own, far, emit_own, emit_far, b):
    rows = own.shape[0]
    chunk = 4 * LANES
    depth, lines = x_turned.shape[0] // 4, draw_turned.shape[0] // 8
    high = depth + lines // 4
    emit = pl.BlockSpec((rows, 4 * LANES), lambda u, n, o: (0, b))
    slab = pl.BlockSpec((rows, 2 * chunk), lambda u, n, o: (0, u))
    left = pl.BlockSpec(memory_space=pltpu.VMEM)
    first = pl.BlockSpec((2, high, chunk), lambda u, n, o: (jnp.where(u == 0, n, 3), 0, 0))
    here = pl.BlockSpec((2, 2, high, chunk), lambda u, n, o: (0, jnp.where(u == 0, 0, jnp.minimum(n, 1)), 0, 0))
    there = pl.BlockSpec((2, 2, high, chunk), lambda u, n, o: (0, jnp.where(u == 0, 0, jnp.maximum(n - 2, 0)), 0, 0))
    return pl.pallas_call(
        block_kernel,
        grid_spec=pltpu.PrefetchScalarGridSpec(
            num_scalar_prefetch=1,
            grid=(2, 4),
            in_specs=[left, left, left, slab, slab, emit, emit],
            out_specs=[first, first, here, there],
            scratch_shapes=[pltpu.VMEM((2 * rows, 2 * chunk), BF16), pltpu.VMEM((2 * rows, 2 * LANES), BF16)],
        ),
        out_shape=[jax.ShapeDtypeStruct((8, high, chunk), BF16)] * 2
        + [jax.ShapeDtypeStruct((2, 4, high, chunk), BF16)] * 2,
        compiler_params=pltpu.CompilerParams(vmem_limit_bytes=28 * 2**20, dimension_semantics=("arbitrary",) * 2),
        cost_estimate=LIGHT,
        name="weight_gradients",
    )(order, x_turned, kept_turned, draw_turned, own, far, emit_own, emit_far)


def layer_kernel(col_ref, x_ref, *refs):
    hid_refs, out_ref = refs[:4], refs[4]
    model = x_ref.shape[1]
    mask = pl.program_id(0) ^ col_ref[0]
    x = x_ref[...].astype(F32)

    def body(hid_ref):
        for d in range(2):
            out_ref[:, d, :] = (x + hid_ref[:, d * model : (d + 1) * model].astype(F32)).astype(BF16)

    for n in range(4):
        pl.when(mask == n)(functools.partial(body, hid_refs[n]))


def layer_sum(col, x, hiddens):
    rows, wide = hiddens[0].shape
    model = x.shape[1]
    return pl.pallas_call(
        layer_kernel,
        grid_spec=pltpu.PrefetchScalarGridSpec(
            num_scalar_prefetch=1,
            grid=(4,),
            in_specs=[pl.BlockSpec((rows, model), lambda n, c: (n, 0))] + [whole((rows, wide))] * 4,
            out_specs=pl.BlockSpec((rows, 2, model), lambda n, c: (n, 0, 0)),
        ),
        out_shape=jax.ShapeDtypeStruct((x.shape[0], 2, model), BF16),
        compiler_params=pltpu.CompilerParams(vmem_limit_bytes=16 * 2**20),
        cost_estimate=LIGHT,
        name="layer_sum",
    )(col.reshape(1).astype(jnp.int32), x, *hiddens)


def turn_rows_kernel(own_ref, met_ref, out_ref):
    rows = own_ref.shape[0]
    out_ref[:, :rows] = jnp.swapaxes(own_ref[...], 0, 1)
    out_ref[:, rows:] = jnp.swapaxes(met_ref[...], 0, 1)


def turn_rows(own, met):
    rows, wide = own.shape
    return pl.pallas_call(
        turn_rows_kernel,
        grid=(2,),
        out_shape=jax.ShapeDtypeStruct((wide, 2 * rows), BF16),
        in_specs=[pl.BlockSpec((rows, wide // 2), lambda n: (0, n))] * 2,
        out_specs=pl.BlockSpec((wide // 2, 2 * rows), lambda n: (n, 0)),
        compiler_params=pltpu.CompilerParams(vmem_limit_bytes=16 * 2**20),
        cost_estimate=LIGHT,
        name="turn_rows",
    )(own, met)


def turn_kernel(*refs):
    w_refs, p_refs, wt_refs, pt_refs = (refs[n * PARTS : (n + 1) * PARTS] for n in range(4))
    for source, target in zip(w_refs, wt_refs):
        target[...] = jnp.swapaxes(source[...], 0, 1)

    @pl.when(pl.program_id(0) == 0)
    def _():
        for source, target in zip(p_refs, pt_refs):
            lines, hidden = source.shape[0], source.shape[1] // 2
            target[:, :lines] = jnp.swapaxes(source[:, :hidden], 0, 1)
            target[:, lines:] = jnp.swapaxes(source[:, hidden:], 0, 1)


def turn(pieces):
    width = pieces[0].shape[1]
    hidden, piece = width // 2, width // 4
    cut = width // 4
    results = pl.pallas_call(
        turn_kernel,
        grid=(4,),
        out_shape=[jax.ShapeDtypeStruct((width, hidden), BF16)] * PARTS
        + [jax.ShapeDtypeStruct((hidden, piece), BF16)] * PARTS,
        in_specs=[pl.BlockSpec((hidden, cut), lambda n: (0, n))] * PARTS
        + [pl.BlockSpec((piece // 2, width), lambda n: (2 * hidden // piece, 0))] * PARTS,
        out_specs=[pl.BlockSpec((cut, hidden), lambda n: (n, 0))] * PARTS
        + [pl.BlockSpec((hidden, piece), lambda n: (0, 0))] * PARTS,
        compiler_params=pltpu.CompilerParams(vmem_limit_bytes=20 * 2**20, dimension_semantics=("arbitrary",)),
        cost_estimate=LIGHT,
        name="turn_pieces",
    )(*pieces, *pieces)
    return results[:PARTS], results[PARTS:]


def assemble_kernel(order_ref, *refs):
    weight_out, proj_out = refs[4:]
    depth = weight_out.shape[1]
    group = refs[0].shape[-2] - depth

    def body(tiles):
        for u, tile_ref in enumerate(tiles):
            value = tile_ref[0, 0].astype(F32)
            lanes = slice(u * LANES, (u + 1) * LANES)
            for q in range(4):
                columns = slice(q * LANES, (q + 1) * LANES)
                weight_out[0, :, q, lanes] = value[:depth, columns]
                proj_out[0, q * group : (q + 1) * group, lanes] = value[depth:, columns]

    far = (pl.program_id(1) // 2) ^ order_ref[1]
    pl.when(far == 0)(lambda: body(refs[:2]))
    pl.when(far == 1)(lambda: body(refs[2:4]))


def assemble(order, own0, own1, far0, far1, depth):
    lines = own0.shape[2]
    group = lines - depth
    cells = 8 * LANES
    piece = pl.BlockSpec((1, 1, lines, 4 * LANES), lambda d, n, o: (d ^ o[0], (n % 2) ^ o[2], 0, 0))
    return pl.pallas_call(
        assemble_kernel,
        grid_spec=pltpu.PrefetchScalarGridSpec(
            num_scalar_prefetch=1,
            grid=(2, 4),
            in_specs=[piece] * 4,
            out_specs=[
                pl.BlockSpec((1, depth, 4, 2 * LANES), lambda d, n, o: (d, 0, 0, n)),
                pl.BlockSpec((1, 4 * group, 2 * LANES), lambda d, n, o: (d, 0, n)),
            ],
        ),
        out_shape=[
            jax.ShapeDtypeStruct((2, depth, 4, cells), F32),
            jax.ShapeDtypeStruct((2, 4 * group, cells), F32),
        ],
        compiler_params=pltpu.CompilerParams(vmem_limit_bytes=16 * 2**20),
        cost_estimate=LIGHT,
        name="assemble_gradients",
    )(order, own0, own1, far0, far1)


def input_grad_kernel(has_sum, *refs):
    slab_refs, w_refs, out_ref = refs[:2], refs[2:6], refs[-1]
    chunk = 4 * LANES
    model = out_ref.shape[1]
    total = refs[6][...] if has_sum else None
    for side in range(2):
        for u in range(2):
            for quarter in range(2):
                at = (u * 2 + quarter) * chunk
                part = lax.dot_general(
                    slab_refs[side][:, at : at + chunk],
                    w_refs[side * 2 + quarter][:model, u * chunk : (u + 1) * chunk],
                    (((1,), (1,)), ((), ())),
                    preferred_element_type=F32,
                )
                total = part if total is None else total + part
    out_ref[...] = total


def add_input_grad(slabs, weights, total):
    rows, half = slabs[0].shape
    model = weights[0].shape[1] // 2
    tile = rows // 2
    operands = [*slabs, *weights] + ([] if total is None else [total])
    lines = lambda n: pl.BlockSpec((tile, n), lambda s: (s, 0))
    return pl.pallas_call(
        functools.partial(input_grad_kernel, total is not None),
        grid=(2,),
        out_shape=jax.ShapeDtypeStruct((rows, model), F32),
        in_specs=[lines(half)] * 2
        + [whole(w.shape) for w in weights]
        + ([] if total is None else [lines(model)]),
        out_specs=lines(model),
        compiler_params=pltpu.CompilerParams(vmem_limit_bytes=24 * 2**20),
        cost_estimate=LIGHT,
        name="input_gradient",
    )(*operands)


def after(values):
    return lax.optimization_barrier(values)


def one_direction(inputs, reset_flags, gate_weight, gate_bias, proj_weight, grad_out):
    row, col = lax.axis_index("rows"), lax.axis_index("cols")
    layer, core = row // 2, row % 2
    direction, pair = layer // 2, layer % 2
    model = inputs.shape[1]
    local = inputs.shape[0] // STEPS
    share = local // 4
    rows = 2 * share
    cells = gate_weight.shape[3]
    piece = cells // PARTS
    width = 4 * piece
    tiles = piece // LANES

    def mask_of(r, near):
        odd = (r // 2) % 2
        return (2 if odd else 1) if near else (1 if odd else 2)

    def over_chips(value, near):
        pairs = [(r * 4 + j, r * 4 + (j ^ mask_of(r, near))) for r in range(8) for j in range(4)]
        return lax.ppermute(value, ("rows", "cols"), pairs)

    def over_rows(value, mask):
        return lax.ppermute(value, "rows", [(r, r ^ mask) for r in range(8)])

    core_swap = functools.partial(over_rows, mask=1)
    pair_swap = functools.partial(over_rows, mask=2)
    half_swap = functools.partial(over_rows, mask=4)
    near_mask = jnp.where(pair == 0, 1, 2)
    block_at = [col, col ^ near_mask, col ^ (3 - near_mask), col ^ 3]
    by_dir = lambda pair_of: jnp.where(direction == 0, pair_of[0], pair_of[1])
    by_other = lambda pair_of: jnp.where(direction == 0, pair_of[1], pair_of[0])
    in_run = lambda value: jnp.where(direction == 0, value, value[::-1])

    order = jnp.stack([direction, core, pair]).astype(jnp.int32)

    def place_of(part):
        return jnp.stack([direction, (core ^ (part // 2)) * 2 + (pair ^ (part % 2))]).astype(jnp.int32)

    places = [place_of(part) for part in range(PARTS)]
    input_piece = lambda part: own_piece(places[part], gate_weight, gate_bias, False)
    recurrent_piece = lambda part: own_piece(places[part], gate_weight, proj_weight, True)

    local_windows = lambda value: lax.dynamic_slice_in_dim(value, col * share, share, 0)
    steps_first = lambda value: jnp.swapaxes(value, 0, 1)
    by_side = lambda k, there: [jnp.where(core == which, k, there) for which in range(2)]

    w_in = {(0, 0): own_piece(places[0], gate_weight, gate_bias, False, memory=60)}
    w_rec = {}
    w_in[1, 0] = over_chips(w_in[0, 0], True)
    w_in[2, 0] = over_chips(w_in[0, 0], False)
    w_rec[0, 0] = recurrent_piece(0)

    keep_grid = local_windows(reset_flags.reshape(local, STEPS)).astype(F32)
    position = lax.broadcasted_iota(jnp.int32, (share, STEPS), 1)
    keep_ahead = jnp.where(position > 0, 1.0 - keep_grid, 0.0)
    next_flags = jnp.concatenate([keep_grid[:, 1:], jnp.zeros((share, 1), F32)], axis=1)
    keep_behind = jnp.where(position < STEPS - 1, 1.0 - next_flags, 0.0)
    own_tokens = share * STEPS
    x_mine = lax.dynamic_slice_in_dim(inputs, col * own_tokens, own_tokens, 0).reshape(share, STEPS, model)
    x_mine = steps_first(x_mine)
    keep_dirs = (steps_first(keep_ahead), steps_first(keep_behind))
    keep_wide = [jnp.broadcast_to(k[..., None], (STEPS, share, LANES)).astype(BF16) for k in keep_dirs]
    xk_here = jnp.concatenate([x_mine, by_dir(keep_wide)], axis=2)
    xk_sent = jnp.concatenate([x_mine, by_other(keep_wide)], axis=2)
    xk_met = half_swap(xk_sent)
    w_in[0, 1] = input_piece(1)
    g_mine = lax.dynamic_slice_in_dim(grad_out, col * own_tokens, own_tokens, 0).reshape(share, STEPS, 2, model)
    g_dirs = (steps_first(g_mine[:, :, 0]), steps_first(g_mine[:, :, 1]))
    w_in, w_rec, xk_here, xk_met, g_dirs, places = after((w_in, w_rec, xk_here, xk_met, g_dirs, places))

    w_rec[1, 0] = over_chips(w_rec[0, 0], True)
    w_in[3, 0] = over_chips(w_in[1, 0], False)
    w_in[2, 1] = pair_swap(w_in[1, 0])
    for b in (1, 2):
        w_in[b, 2] = core_swap(w_in[b, 0])
    w_rec[0, 1], w_in[0, 2], w_in[0, 3] = recurrent_piece(1), input_piece(2), input_piece(3)
    xk = in_run(jnp.concatenate([xk_here, xk_met], axis=1))
    x_run, keep_run = xk[..., :model], xk[..., model:].astype(F32)
    x_flat = x_run.reshape(STEPS * rows, model)
    w_in, w_rec, x_flat, keep_run, g_dirs, places = after((w_in, w_rec, x_flat, keep_run, g_dirs, places))

    gates_of = lambda b: input_gates(x_flat, [w_in[b, part] for part in range(PARTS)])
    turn_of = lambda b: turn([w_rec[b, part] for part in range(PARTS)])
    w_in[1, 1] = over_chips(w_in[0, 1], True)
    w_rec[3, 0] = over_chips(w_rec[1, 0], False)
    w_in[3, 1] = pair_swap(w_in[3, 0])
    w_rec[1, 2], w_in[3, 2] = core_swap(w_rec[1, 0]), core_swap(w_in[3, 0])
    w_rec[0, 2], w_rec[0, 3] = recurrent_piece(2), recurrent_piece(3)
    px, turned = {0: gates_of(0)}, {}
    w_in, w_rec, px, x_flat = after((w_in, w_rec, px, x_flat))

    w_rec[1, 1] = over_chips(w_rec[0, 1], True)
    w_rec[2, 0] = over_chips(w_rec[0, 0], False)
    w_rec[2, 1] = pair_swap(w_rec[1, 0])
    for b in (1, 2, 3):
        w_in[b, 3] = core_swap(w_in[b, 1])
    turned[0] = turn_of(0)
    for b in (1, 2, 3):
        px[b] = gates_of(b)
    w_in, w_rec, px, turned, x_flat = after((w_in, w_rec, px, turned, x_flat))

    last_half = w_rec[3, 0].shape[0] // 2
    last_piece = [pair_swap(w_rec[3, 0][:last_half]), over_chips(w_rec[1, 1][last_half:], False)]
    w_rec[1, 3], w_rec[2, 2] = core_swap(w_rec[1, 1]), core_swap(w_rec[2, 0])
    w_rec[2, 3], w_rec[3, 2] = core_swap(w_rec[2, 1]), core_swap(w_rec[3, 0])
    x_met = core_swap(x_flat)
    turned[1], turned[2] = turn_of(1), turn_of(2)
    w_rec, turned, last_piece, x_met = after((w_rec, turned, last_piece, x_met))

    w_rec[3, 1] = jnp.concatenate(last_piece, axis=0)
    w_rec[3, 3] = core_swap(w_rec[3, 1])
    x_turned = turn_rows(x_flat, x_met)
    g_sent = by_other(g_dirs)
    w_rec, turned, x_turned, g_sent = after((w_rec, turned, x_turned, g_sent))

    g_met = half_swap(g_sent)
    px = [px[b].reshape(STEPS, rows, PARTS * width) for b in range(BLOCKS)]
    pre, cell, emit_own, emit_far, raw, kept, hid = run_forward(
        px, keep_run, [w_rec[b, part] for b in range(BLOCKS) for part in range(PARTS)]
    )

    pre, cell, emit_own, emit_far, raw, kept, hid, g_met = after((pre, cell, emit_own, emit_far, raw, kept, hid, g_met))
    g_run = in_run(jnp.concatenate([by_dir(g_dirs), g_met], axis=1))

    flat = lambda value: value.reshape(STEPS * rows, value.shape[-1])
    hid_time = in_run(hid)
    hid_here, hid_there = hid_time[:, :share], half_swap(hid_time[:, share:])
    emit_met = core_swap(flat(emit_far))
    kept = flat(kept)
    kept_met = core_swap(kept)
    turned[3] = turn_of(3)
    hid_here, hid_there, kept, kept_met, emit_met, turned, chain = after(
        (hid_here, hid_there, kept, kept_met, emit_met, turned, (pre, cell, raw))
    )

    def over_cols(value, mask):
        return lax.ppermute(value, "cols", [(j, j ^ mask) for j in range(4)])

    hid_both = jnp.concatenate([by_dir((hid_here, hid_there)), by_other((hid_here, hid_there))], axis=2)
    hid_parts = [hid_both] + [over_cols(hid_both, mask) for mask in (1, 2, 3)]

    kept_turned = turn_rows(kept, kept_met)
    slabs, draw, bias_sums = run_backward(
        *chain,
        g_run,
        keep_run,
        [w for b in range(BLOCKS) for w in turned[b][0]],
        [p for b in range(BLOCKS) for p in turned[b][1]],
    )
    hid_parts, kept_turned, slabs, draw, bias_sums, emit_own, emit_met = after(
        (hid_parts, kept_turned, slabs, draw, bias_sums, emit_own, emit_met)
    )

    slabs = [[flat(value) for value in block] for block in slabs]
    emit_own, draw = flat(emit_own), flat(draw)
    far = {3: core_swap(slabs[3][1])}
    draw_met = core_swap(draw)
    bias_parts = jnp.sum(bias_sums, axis=0).reshape(BLOCKS, 4, 2, 2 * piece)
    bias_half = bias_parts[:, :, 0] + core_swap(bias_parts[:, :, 1])
    far, draw_met, slabs, bias_half = after((far, draw_met, slabs, bias_half))

    def grads(b):
        left = (x_turned, kept_turned, draw_turned)
        return block_grads(order, *left, slabs[b][0], far[b], emit_own, emit_met, b)

    def add(first, *others):
        total = first.astype(F32)
        for other in others:
            total = total + other.astype(F32)
        return total.astype(BF16)

    def flip(value):
        return jnp.concatenate([value[1:], value[:1]], axis=0)

    draw_turned = turn_rows(draw, draw_met)
    opposite = grads(3)
    for b in (1, 2):
        far[b] = core_swap(slabs[b][1])
    bias_met = [over_chips(bias_half[1], True), over_chips(bias_half[2], False), over_cols(bias_half[3], 3)]
    far, opposite, draw_turned, slabs, bias_half, bias_met = after(
        (far, opposite, draw_turned, slabs, bias_half, bias_met)
    )

    relay_a, relay_b = over_chips(opposite[0], True), over_chips(opposite[1], False)
    met = pair_swap(opposite[3])
    far[0] = core_swap(slabs[0][1])
    bias_half = bias_half[0] + bias_met[0] + bias_met[1] + bias_met[2]
    bias_half = jnp.where(pair == 0, bias_half, jnp.concatenate([bias_half[:, piece:], bias_half[:, :piece]], axis=1))
    bias_half = bias_half + pair_swap(bias_half)
    near, other = grads(1), grads(2)
    far, relay_a, relay_b, met, near, other, slabs, bias_half = after(
        (far, relay_a, relay_b, met, near, other, slabs, bias_half)
    )

    near_a, other_b = over_chips(near[0], True), over_chips(other[1], False)
    other_met = pair_swap(near[3])
    opposite1 = add(opposite[2], flip(met))
    near_b, other_a = add(near[1], relay_b), add(other[0], relay_a)
    own = grads(0)
    near1, other1, own0, own1 = near[2:], other[2:], own[:2], own[2:]
    bias_there = half_swap(bias_half)
    bias_half = jnp.stack([by_dir((bias_half, bias_there)), by_other((bias_half, bias_there))])
    near_a, other_b, other_met, opposite1, near_b, other_a, other1, own0, own1, slabs, bias_half, hid_parts = after(
        (near_a, other_b, other_met, opposite1, near_b, other_a, other1, own0, own1, slabs, bias_half, hid_parts)
    )

    near_b, other_a = over_chips(near_b, True), over_chips(other_a, False)
    near_met = pair_swap(other1[1])
    wide = None
    for b in range(BLOCKS):
        wide = add_input_grad(slabs[b], [w_in[b, part] for part in range(PARTS)], wide)
    bias_total = jnp.concatenate(by_side(bias_half, core_swap(bias_half)), axis=2)
    near_b, other_a, near_met, wide, own1, bias_total, hid_parts = after(
        (near_b, other_a, near_met, wide, own1, bias_total, hid_parts)
    )

    relay_a, relay_b = over_chips(opposite1[0], True), over_chips(opposite1[1], False)
    sums0 = jnp.stack([add(own0[0], near_a, other_a), add(own0[1], near_b, other_b)])
    count = sums0.shape[1] // 2
    sums0_met = pair_swap(sums0[:, count:])
    dx = in_run(wide.reshape(STEPS, rows, model))
    dx, dx_met = dx[:, :share], half_swap(dx[:, share:].astype(BF16))
    hid_parts = [steps_first(value).reshape(own_tokens, 2 * model) for value in hid_parts]
    relay_a, relay_b, sums0, sums0_met, dx, dx_met, own1, hid_parts = after(
        (relay_a, relay_b, sums0, sums0_met, dx, dx_met, own1, hid_parts)
    )

    near1 = add(near1[0], flip(near_met), jnp.stack([jnp.zeros_like(relay_b), relay_b]))
    other1 = add(other1[0], flip(other_met), jnp.stack([relay_a, jnp.zeros_like(relay_a)]))
    near_met, other_met = over_chips(near1, True), over_chips(other1, False)
    own_met = pair_swap(own1[1])
    by_half = lambda value: value.reshape(2, 2, 2, *value.shape[2:])
    sums0 = by_half(add(sums0[:, :count], flip(sums0_met)))
    sums0_met = half_swap(sums0[:, 1])
    dx = dx + dx_met.astype(F32) + g_dirs[0].astype(F32) + g_dirs[1].astype(F32)
    dx = steps_first(dx.astype(BF16)).reshape(own_tokens, model)
    def by_column(parts):
        whole_rows = jnp.zeros((BLOCKS * parts[0].shape[0], parts[0].shape[1]), parts[0].dtype)
        for mask, value in enumerate(parts):
            whole_rows = lax.dynamic_update_slice(whole_rows, value, ((col ^ mask) * value.shape[0], 0))
        return whole_rows

    block_out = layer_sum(col, inputs, hid_parts)
    near_met, other_met, own_met, sums0, sums0_met, dx, own1, block_out = after(
        (near_met, other_met, own_met, sums0, sums0_met, dx, own1, block_out)
    )

    sums1 = by_half(add(own1[0], flip(own_met), near_met, other_met))
    sums1_met = half_swap(sums1[:, 1])

    def two_directions(here, there):
        both = jnp.stack([here, there])
        return both[:, :, 0], both[:, :, 1]

    kept0, sent0 = two_directions(sums0[:, 0], sums0_met)
    met0 = core_swap(sent0)
    slice_for = lambda at: lax.dynamic_slice_in_dim(dx, at * (model // 4), model // 4, 1)
    dx_parts = [slice_for(col ^ mask) for mask in range(4)]
    dx_parts = [dx_parts[0]] + [over_cols(dx_parts[mask], mask) for mask in (1, 2, 3)]

    sums1, sums1_met, kept0, met0, dx_parts = after((sums1, sums1_met, kept0, met0, dx_parts))

    kept1, sent1 = two_directions(sums1[:, 0], sums1_met)
    met1 = core_swap(sent1)
    weight_share, proj_share = assemble(order, kept0, kept1, met0, met1, 2 * model // 8)
    proj_share = jnp.swapaxes(proj_share, 1, 2)
    input_grad = by_column(dx_parts)
    return (block_out, input_grad, weight_share, bias_total, proj_share)


def solution(mesh):
    placed = (
        P("rows", None),
        P("rows"),
        P(None, None, None, "cols"),
        P(None, None, "cols"),
        P(None, "cols", None),
        P("rows", None, None),
    )
    plan = one_direction if (mesh.shape["rows"], mesh.shape["cols"]) == (8, 4) else shared_cells
    return jax.shard_map(
        plan,
        mesh=mesh,
        in_specs=placed,
        out_specs=(
            P("rows", None, None),
            P("rows", "cols"),
            P(None, "rows", None, "cols"),
            P(None, None, "cols"),
            P(None, "cols", "rows"),
        ),
        check_vma=False,
    )
```

```python
import functools

import jax
import jax.numpy as jnp
from jax import lax
from jax.experimental import pallas as pl
from jax.experimental.pallas import tpu as pltpu
from jax.sharding import PartitionSpec as P

STEPS = 20
BF16 = jnp.bfloat16
F32 = jnp.float32
THIRD = 1.0 / 3.0
LANES = 128
BLOCKS = 4
LIGHT = pl.CostEstimate(flops=1, bytes_accessed=1, transcendentals=0)
PARTS = 4


def soft_clip(amount):
    return 3.0 * jnp.tanh(amount / 3.0)


def clip_slope(amount):
    tangent = jnp.tanh(amount / 3.0)
    return 1.0 - tangent * tangent


def shared_cells(inputs, reset_flags, gate_weight, gate_bias, proj_weight, grad_out):
    tok_rows, model_width = inputs.shape
    windows = tok_rows // STEPS
    cell_cols = gate_weight.shape[3]
    gate_width = 4 * cell_cols
    share_width = model_width // lax.axis_size("cols")
    column = lax.axis_index("cols") * share_width
    weight = gate_weight.reshape(2, 2 * model_width, gate_width)
    w_input = weight[:, :model_width]
    w_recur = weight[:, model_width:]
    bias_row = gate_bias.reshape(2, 1, gate_width)
    sequence = jnp.swapaxes(inputs.reshape(windows, STEPS, model_width), 0, 1)
    x_stack = jnp.stack([sequence, sequence[::-1]], axis=1)
    flag_grid = jnp.swapaxes(reset_flags.reshape(windows, STEPS), 0, 1).astype(jnp.float32)
    position = lax.broadcasted_iota(jnp.int32, (STEPS, windows), 0)
    keep_ahead = jnp.where(position > 0, 1.0 - flag_grid, 0.0)
    next_flags = jnp.concatenate([flag_grid[1:], jnp.zeros((1, windows), jnp.float32)], axis=0)
    keep_behind = jnp.where(position < STEPS - 1, 1.0 - next_flags, 0.0)
    keep_stack = jnp.stack([keep_ahead, keep_behind[::-1]], axis=1)[..., None]
    input_gates = jnp.einsum("sdwh,dhg->sdwg", x_stack, w_input, preferred_element_type=jnp.float32)

    def forward_step(state_pair, pieces):
        hidden, cell_prev = state_pair
        gates_in, keep_step = pieces
        kept_hidden = hidden * keep_step.astype(jnp.bfloat16)
        gate_pre = (
            gates_in
            + jnp.einsum("dwh,dhg->dwg", kept_hidden, w_recur, preferred_element_type=jnp.float32)
            + bias_row
        )
        in_gate = jax.nn.sigmoid(gate_pre[..., :cell_cols])
        forget = jax.nn.sigmoid(gate_pre[..., cell_cols : 2 * cell_cols])
        update = jnp.tanh(gate_pre[..., 2 * cell_cols : 3 * cell_cols])
        out_gate = jax.nn.sigmoid(gate_pre[..., 3 * cell_cols :])
        kept_cell = cell_prev * keep_step
        cell_new = soft_clip(forget * kept_cell + in_gate * update)
        cell_output = (out_gate * jnp.tanh(cell_new)).astype(jnp.bfloat16)
        partial_raw = jnp.einsum(
            "dwc,dch->dwh", cell_output, proj_weight, preferred_element_type=jnp.float32
        )
        proj_raw = lax.psum(partial_raw, "cols")
        new_hidden = soft_clip(proj_raw).astype(jnp.bfloat16)
        return (
            (new_hidden, cell_new),
            (kept_hidden, gate_pre, kept_cell, cell_new, cell_output, proj_raw, new_hidden),
        )

    init_state = (
        jnp.zeros((2, windows, model_width), jnp.bfloat16),
        jnp.zeros((2, windows, cell_cols), jnp.float32),
    )
    _, fwd_saved = lax.scan(forward_step, init_state, (input_gates, keep_stack))
    kept_all, pre_all, kept_cells, cell_states, cell_outputs, proj_raws, hiddens = fwd_saved
    ahead_hidden = hiddens[:, 0]
    behind_hidden = hiddens[::-1, 1]
    both_outputs = jnp.stack([ahead_hidden, behind_hidden], axis=2).astype(jnp.float32) + sequence[
        :, :, None, :
    ].astype(jnp.float32)
    block_out = (
        jnp.swapaxes(both_outputs, 0, 1).reshape(tok_rows, 2, model_width).astype(jnp.bfloat16)
    )
    out_grid = jnp.transpose(grad_out.reshape(windows, STEPS, 2, model_width), (1, 2, 0, 3))
    grad_stack = jnp.stack([out_grid[:, 0], out_grid[::-1, 1]], axis=1)

    def backward_step(state_pair, pieces):
        recur_part, cell_grad = state_pair
        gate_pre, kept_cell, cell_new, cell_output, proj_raw, grad_step, keep_step = pieces
        recur_sum = lax.psum(recur_part, "cols")
        hidden_grad = grad_step.astype(jnp.float32) + recur_sum
        raw_grad = (hidden_grad * clip_slope(proj_raw)).astype(jnp.bfloat16)
        emit_grad = jnp.einsum(
            "dwh,dch->dwc", raw_grad, proj_weight, preferred_element_type=jnp.float32
        )
        in_gate = jax.nn.sigmoid(gate_pre[..., :cell_cols])
        forget = jax.nn.sigmoid(gate_pre[..., cell_cols : 2 * cell_cols])
        update = jnp.tanh(gate_pre[..., 2 * cell_cols : 3 * cell_cols])
        out_gate = jax.nn.sigmoid(gate_pre[..., 3 * cell_cols :])
        tanh_cell = jnp.tanh(cell_new)
        cell_total = cell_grad + emit_grad * out_gate * (1.0 - tanh_cell * tanh_cell)
        cell_third = cell_new / 3.0
        cell_raw_grad = cell_total * (1.0 - cell_third * cell_third)
        pre_grad = jnp.concatenate(
            [
                cell_raw_grad * update * in_gate * (1.0 - in_gate),
                cell_raw_grad * kept_cell * forget * (1.0 - forget),
                cell_raw_grad * in_gate * (1.0 - update * update),
                emit_grad * tanh_cell * out_gate * (1.0 - out_gate),
            ],
            axis=-1,
        ).astype(jnp.bfloat16)
        recur_next = (
            jnp.einsum("dwg,dhg->dwh", pre_grad, w_recur, preferred_element_type=jnp.float32)
            * keep_step
        )
        cell_next = cell_raw_grad * forget * keep_step
        return ((recur_next, cell_next), (pre_grad, raw_grad))

    zero_state = (
        jnp.zeros((2, windows, model_width), jnp.float32),
        jnp.zeros((2, windows, cell_cols), jnp.float32),
    )
    _, back_saved = lax.scan(
        backward_step,
        zero_state,
        (pre_all, kept_cells, cell_states, cell_outputs, proj_raws, grad_stack, keep_stack),
        reverse=True,
    )
    pre_grads, raw_grads = back_saved
    input_part = jnp.einsum(
        "sdwg,dhg->sdwh", pre_grads, w_input, preferred_element_type=jnp.float32
    )
    input_sum = jnp.swapaxes(input_part[:, 0] + input_part[::-1, 1], 0, 1).reshape(
        tok_rows, model_width
    )
    input_share = lax.psum_scatter(
        input_sum.astype(jnp.bfloat16), "cols", scatter_dimension=1, tiled=True
    ).astype(jnp.float32)
    residual_grad = grad_out[:, 0].astype(jnp.float32) + grad_out[:, 1].astype(jnp.float32)
    input_grad = (
        input_share + lax.dynamic_slice_in_dim(residual_grad, column, share_width, 1)
    ).astype(jnp.bfloat16)
    input_weight_grad = jnp.einsum(
        "sdwh,sdwg->dhg", x_stack, pre_grads, preferred_element_type=jnp.float32
    )
    recur_weight_grad = jnp.einsum(
        "sdwh,sdwg->dhg", kept_all, pre_grads, preferred_element_type=jnp.float32
    )
    weight_grad = jnp.concatenate([input_weight_grad, recur_weight_grad], axis=1).reshape(
        2, 2 * model_width, 4, cell_cols
    )
    proj_grad = jnp.einsum(
        "sdwc,sdwh->dch", cell_outputs, raw_grads, preferred_element_type=jnp.float32
    )
    bias_grad = jnp.sum(pre_grads, axis=(0, 2), dtype=jnp.float32).reshape(2, 4, cell_cols)
    weight_share, proj_share = (
        lax.psum_scatter(
            weight_grad.astype(jnp.bfloat16), "rows", scatter_dimension=1, tiled=True
        ).astype(jnp.float32),
        lax.psum_scatter(
            proj_grad.astype(jnp.bfloat16), "rows", scatter_dimension=2, tiled=True
        ).astype(jnp.float32),
    )
    bias_total = lax.psum(bias_grad, "rows")
    return (block_out, input_grad, weight_share, bias_total, proj_share)


def sigmoid(amount):
    return 0.5 * jnp.tanh(0.5 * amount) + 0.5


def whole(shape):
    return pl.BlockSpec(shape, lambda *_: (0,) * len(shape), pipeline_mode=pl.Buffered(1))


def matmul(a, b):
    return jnp.dot(a, b, preferred_element_type=F32)


def own_piece_kernel(order_ref, w_ref, extra_ref, out_ref):
    step = pl.program_id(0)
    lines = w_ref.shape[1]
    model, width = extra_ref.shape[-1] if extra_ref.shape[1] > 4 else None, out_ref.shape[1]
    for u in range(2):
        for q in range(4):
            to = (u * 4 + q) * LANES
            out_ref[pl.ds(step * lines, lines), to : to + LANES] = w_ref[0, :, q, u * LANES : (u + 1) * LANES]
    base = width // 2

    @pl.when(step == 0)
    def _():
        if model is None:
            rest = jnp.concatenate(
                [extra_ref[0, q : q + 1, u * LANES : (u + 1) * LANES] for u in range(2) for q in range(4)], axis=1
            )
            parts = []
            for _ in range(3):
                parts.append(rest.astype(BF16).astype(F32))
                rest = rest - parts[-1]
            parts.append(jnp.zeros((13, width), F32))
            out_ref[base:, :] = jnp.concatenate(parts, axis=0).astype(BF16)
        else:
            half = extra_ref.shape[1] // 2
            out_ref[base:, :model] = extra_ref[0, :half, :]
            out_ref[base:, model:] = extra_ref[0, half:, :]


def own_piece(place, gate_weight, extra, recurrent, memory=16):
    model, piece = gate_weight.shape[1] // 2, gate_weight.shape[3] // PARTS
    cut = model // 4
    first = 4 if recurrent else 0
    if recurrent:
        extra_spec = pl.BlockSpec((1, piece, model), lambda n, p: (p[0], p[1], 0))
    else:
        extra_spec = pl.BlockSpec((1, 4, piece), lambda n, p: (p[0], 0, p[1]))
    lines = model + (piece // 2 if recurrent else 16)
    return pl.pallas_call(
        own_piece_kernel,
        grid_spec=pltpu.PrefetchScalarGridSpec(
            num_scalar_prefetch=1,
            grid=(4,),
            in_specs=[pl.BlockSpec((1, cut, 4, piece), lambda n, p: (p[0], n + first, 0, p[1])), extra_spec],
            out_specs=pl.BlockSpec((lines, 4 * piece), lambda n, p: (0, 0)),
        ),
        out_shape=jax.ShapeDtypeStruct((lines, 4 * piece), BF16),
        compiler_params=pltpu.CompilerParams(vmem_limit_bytes=memory * 2**20, dimension_semantics=("arbitrary",)),
        cost_estimate=LIGHT,
        name="own_piece",
    )(place, gate_weight, extra)


def input_kernel(x_ref, w0, w1, w2, w3, out_ref):
    model, width = x_ref.shape[1], w0.shape[1]
    for n, w_ref in enumerate((w0, w1, w2, w3)):
        bias = jnp.sum(w_ref[model:, :].astype(F32), axis=0, keepdims=True)
        out_ref[:, n * width : (n + 1) * width] = (matmul(x_ref[...], w_ref[:model, :]) + bias).astype(BF16)


def input_gates(x, weights):
    rows, model = x.shape
    width = weights[0].shape[1]
    tile = rows // 2
    return pl.pallas_call(
        input_kernel,
        grid=(2,),
        out_shape=jax.ShapeDtypeStruct((rows, PARTS * width), BF16),
        in_specs=[pl.BlockSpec((tile, model), lambda n: (n, 0))] + [whole(w.shape) for w in weights],
        out_specs=pl.BlockSpec((tile, PARTS * width), lambda n: (n, 0)),
        compiler_params=pltpu.CompilerParams(vmem_limit_bytes=20 * 2**20),
        cost_estimate=LIGHT,
        name="input_gates",
    )(x, *weights)


def forward_kernel(*refs):
    px_refs, keep_ref = refs[:BLOCKS], refs[BLOCKS]
    w_refs = refs[BLOCKS + 1 : BLOCKS + 1 + BLOCKS * PARTS]
    pre_out, cell_out, emit_own, emit_far, raw_out, kept_out, hid_out, c_scr, h_scr = refs[BLOCKS + 1 + BLOCKS * PARTS :]
    step = pl.program_id(0)
    width = w_refs[0].shape[1]
    hidden = width // 2
    piece = width // 4
    cells = piece * PARTS
    tiles = piece // LANES
    half = cells // 2
    rows = keep_ref.shape[1]

    @pl.when(step == 0)
    def _():
        c_scr[...] = jnp.zeros_like(c_scr)
        h_scr[...] = jnp.zeros_like(h_scr)

    keep = keep_ref[0][:, :1]
    kept = (h_scr[...] * keep).astype(BF16)
    kept_out[0] = kept
    raw = jnp.zeros((rows, hidden), F32)
    for b in range(BLOCKS):
        parts, proj = [], []
        for s in range(PARTS):
            w_ref = w_refs[b * PARTS + s]
            pre = px_refs[b][0, :, s * width : (s + 1) * width].astype(F32) + matmul(kept, w_ref[:hidden, :])
            at = b * 4 * cells + s * width
            pre_out[0, :, at : at + width] = pre.astype(BF16)
            parts.append(pre)
            proj += [w_ref[hidden:, :hidden], w_ref[hidden:, hidden:]]
        gates = [
            jnp.concatenate(
                [part[:, (u * 4 + q) * LANES : (u * 4 + q + 1) * LANES] for part in parts for u in range(tiles)], axis=1
            )
            for q in range(4)
        ]
        i, f, u, o = sigmoid(gates[0]), sigmoid(gates[1]), jnp.tanh(gates[2]), sigmoid(gates[3])
        at = b * cells
        kept_cell = c_scr[:, at : at + cells] * keep
        cell = 3.0 * jnp.tanh((f * kept_cell + i * u) * THIRD)
        emit = (o * jnp.tanh(cell)).astype(BF16)
        c_scr[:, at : at + cells] = cell
        cell_out[0, :, at : at + cells] = cell
        emit_own[0, :, b * half : (b + 1) * half] = emit[:, :half]
        emit_far[0, :, b * half : (b + 1) * half] = emit[:, half:]
        raw = raw + matmul(emit, jnp.concatenate(proj, axis=0))
    raw_out[0] = raw
    hid = 3.0 * jnp.tanh(raw * THIRD)
    h_scr[...] = hid.astype(BF16).astype(F32)
    hid_out[0] = hid.astype(BF16)


def run_forward(px, keep, weights):
    steps, rows, wide = px[0].shape
    hidden = weights[0].shape[1] // 2
    total = BLOCKS * wide // 4
    block = lambda n: pl.BlockSpec((1, rows, n), lambda t: (t, 0, 0))
    sizes = (4 * total, total, total // 2, total // 2, hidden, hidden, hidden)
    kinds = (BF16, F32, BF16, BF16, F32, BF16, BF16)
    return pl.pallas_call(
        forward_kernel,
        grid=(steps,),
        out_shape=tuple(jax.ShapeDtypeStruct((steps, rows, n), kind) for n, kind in zip(sizes, kinds)),
        in_specs=[block(wide)] * BLOCKS + [block(LANES)] + [whole(w.shape) for w in weights],
        out_specs=tuple(block(n) for n in sizes),
        scratch_shapes=[pltpu.VMEM((rows, total), F32), pltpu.VMEM((rows, hidden), F32)],
        compiler_params=pltpu.CompilerParams(vmem_limit_bytes=48 * 2**20, dimension_semantics=("arbitrary",)),
        cost_estimate=pl.CostEstimate(
            flops=2 * steps * rows * hidden * 5 * total * 8,
            bytes_accessed=steps * rows * total * 24 + 10 * total * hidden,
            transcendentals=steps * rows * total * 6,
        ),
        name="forward_chain",
    )(*px, keep, *weights)


def backward_kernel(*refs):
    pre_ref, cell_ref, before_ref, raw_ref, grad_ref, keep_ref = refs[:6]
    wt_refs, pt_refs = refs[6 : 6 + BLOCKS * PARTS], refs[6 + BLOCKS * PARTS : 6 + 2 * BLOCKS * PARTS]
    outs = refs[6 + 2 * BLOCKS * PARTS :]
    slabs, draw_out, bias_out, dc_scr, dk_scr = outs[: 2 * BLOCKS], *outs[2 * BLOCKS :]
    step = pl.program_id(0)
    hidden, piece = pt_refs[0].shape
    cells = piece * PARTS
    tiles = piece // LANES
    width = 4 * piece
    chunk = 4 * LANES
    rows = keep_ref.shape[1]

    @pl.when(step == 0)
    def _():
        dc_scr[...] = jnp.zeros_like(dc_scr)
        dk_scr[...] = jnp.zeros_like(dk_scr)
        bias_out[...] = jnp.zeros_like(bias_out)

    keep = keep_ref[0][:, :1]
    tangent = jnp.tanh(raw_ref[0] * THIRD)
    draw = ((grad_ref[0].astype(F32) + dk_scr[...]) * (1.0 - tangent * tangent)).astype(BF16)
    draw_out[0] = draw
    dk = jnp.zeros((rows, hidden), F32)
    for b in range(BLOCKS):
        at = b * cells
        demit = matmul(draw, jnp.concatenate([pt_refs[b * PARTS + s][...] for s in range(PARTS)], axis=1))
        gates = [
            jnp.concatenate(
                [
                    pre_ref[0, :, 4 * at + s * width + (u * 4 + q) * LANES : 4 * at + s * width + (u * 4 + q + 1) * LANES]
                    for s in range(PARTS)
                    for u in range(tiles)
                ],
                axis=1,
            ).astype(F32)
            for q in range(4)
        ]
        i, f, u, o = sigmoid(gates[0]), sigmoid(gates[1]), jnp.tanh(gates[2]), sigmoid(gates[3])
        cell = cell_ref[0, :, at : at + cells]
        kept_cell = before_ref[0, :, at : at + cells] * keep
        tanh_cell = jnp.tanh(cell)
        third = cell * THIRD
        dcell = (dc_scr[:, at : at + cells] + demit * o * (1.0 - tanh_cell * tanh_cell)) * (1.0 - third * third)
        dgates = (
            dcell * u * i * (1.0 - i),
            dcell * kept_cell * f * (1.0 - f),
            dcell * i * (1.0 - u * u),
            demit * tanh_cell * o * (1.0 - o),
        )
        dc_scr[:, at : at + cells] = dcell * f * keep
        for q in range(4):
            folded = dgates[q][:8]
            for r in range(8, rows, 8):
                folded = folded + dgates[q][r : r + 8]
            bias_out[:, (b * 4 + q) * cells : (b * 4 + q + 1) * cells] += folded
        dgates = [dgate.astype(BF16) for dgate in dgates]
        for s in range(PARTS):
            part = jnp.concatenate(
                [
                    dgates[q][:, s * piece + u * LANES : s * piece + (u + 1) * LANES]
                    for u in range(tiles)
                    for q in range(4)
                ],
                axis=1,
            )
            side, quarter = s // 2, s % 2
            for u in range(tiles):
                to = (u * 2 + quarter) * chunk
                slabs[b * 2 + side][0, :, to : to + chunk] = part[:, u * chunk : (u + 1) * chunk]
            dk = dk + matmul(part, wt_refs[b * PARTS + s][...])
    dk_scr[...] = dk * keep


def run_backward(pre, cell, raw, grad, keep, weights, projs):
    steps, rows, gates = pre.shape
    total = gates // 4
    hidden, piece = projs[0].shape
    half = PARTS * piece * 2
    block = lambda n: pl.BlockSpec((1, rows, n), lambda s: (steps - 1 - s, 0, 0))
    before = pl.BlockSpec((1, rows, total), lambda s: (jnp.maximum(steps - 2 - s, 0), 0, 0))
    shape = lambda n: jax.ShapeDtypeStruct((steps, rows, n), BF16)
    out = pl.pallas_call(
        backward_kernel,
        grid=(steps,),
        out_shape=tuple([shape(half)] * (2 * BLOCKS) + [shape(hidden), jax.ShapeDtypeStruct((8, gates), F32)]),
        in_specs=[block(gates), block(total), before, block(hidden), block(hidden), block(LANES)]
        + [whole(w.shape) for w in [*weights, *projs]],
        out_specs=tuple([block(half)] * (2 * BLOCKS) + [block(hidden), pl.BlockSpec((8, gates), lambda s: (0, 0))]),
        scratch_shapes=[pltpu.VMEM((rows, total), F32), pltpu.VMEM((rows, hidden), F32)],
        compiler_params=pltpu.CompilerParams(vmem_limit_bytes=48 * 2**20, dimension_semantics=("arbitrary",)),
        cost_estimate=pl.CostEstimate(
            flops=2 * steps * rows * hidden * 5 * total * 8,
            bytes_accessed=steps * rows * total * 24 + 10 * total * hidden,
            transcendentals=steps * rows * total * 6,
        ),
        name="backward_chain",
    )(pre, cell, cell, raw, grad, keep, *weights, *projs)
    return [out[b * 2 : b * 2 + 2] for b in range(BLOCKS)], out[2 * BLOCKS], out[2 * BLOCKS + 1]


def block_kernel(order_ref, x_ref, kept_ref, draw_ref, own_ref, far_ref, own_emit, far_emit, *refs):
    first_a, first_b, second_here, second_there, right, emit = refs
    rows = own_ref.shape[0]
    tile, step = pl.program_id(0), pl.program_id(1)
    depth, lines = x_ref.shape[0] // 4, draw_ref.shape[0] // 8
    group = lines // 4
    chunk = 4 * LANES
    first = order_ref[1]
    here, half = (step // 2) ^ order_ref[2], (step % 2) ^ order_ref[0]

    @pl.when(step == 0)
    def _():
        right[:rows, :], right[rows:, :] = own_ref[...], far_ref[...]
        for u in range(2):

            @pl.when(tile == u)
            def _():
                for quarter in range(2):
                    to, at = quarter * LANES, (quarter * 2 + u) * LANES
                    emit[:rows, to : to + LANES] = own_emit[:, at : at + LANES]
                    emit[rows:, to : to + LANES] = far_emit[:, at : at + LANES]

    def body(left_ref):
        left = left_ref[pl.ds(here * (2 * depth), 2 * depth), :]
        dp = matmul(draw_ref[pl.ds((half * 2 + here) * (2 * lines), 2 * lines), :], emit[...]).astype(BF16)
        for quarter in range(2):
            dw = matmul(left, right[:, quarter * chunk : (quarter + 1) * chunk]).astype(BF16)

            def store(out):
                for side in range(2):
                    to = side ^ first
                    out[to, :depth, :] = dw[side * depth : (side + 1) * depth]
                    for g in range(4):
                        at = side * lines + g * group
                        out[to, depth : depth + group, g * LANES : (g + 1) * LANES] = dp[
                            at : at + group, quarter * LANES : (quarter + 1) * LANES
                        ]

            pl.when(tile == 0)(lambda: store((first_a, first_b)[quarter]))
            pl.when((tile == 1) & (step < 2))(lambda: store(second_here.at[quarter]))
            pl.when((tile == 1) & (step >= 2))(lambda: store(second_there.at[quarter]))

    pl.when(half == 0)(lambda: body(x_ref))
    pl.when(half == 1)(lambda: body(kept_ref))


def block_grads(order, x_turned, kept_turned, draw_turned, own, far, emit_own, emit_far, b):
    rows = own.shape[0]
    chunk = 4 * LANES
    depth, lines = x_turned.shape[0] // 4, draw_turned.shape[0] // 8
    high = depth + lines // 4
    emit = pl.BlockSpec((rows, 4 * LANES), lambda u, n, o: (0, b))
    slab = pl.BlockSpec((rows, 2 * chunk), lambda u, n, o: (0, u))
    left = pl.BlockSpec(memory_space=pltpu.VMEM)
    first = pl.BlockSpec((2, high, chunk), lambda u, n, o: (jnp.where(u == 0, n, 3), 0, 0))
    here = pl.BlockSpec((2, 2, high, chunk), lambda u, n, o: (0, jnp.where(u == 0, 0, jnp.minimum(n, 1)), 0, 0))
    there = pl.BlockSpec((2, 2, high, chunk), lambda u, n, o: (0, jnp.where(u == 0, 0, jnp.maximum(n - 2, 0)), 0, 0))
    return pl.pallas_call(
        block_kernel,
        grid_spec=pltpu.PrefetchScalarGridSpec(
            num_scalar_prefetch=1,
            grid=(2, 4),
            in_specs=[left, left, left, slab, slab, emit, emit],
            out_specs=[first, first, here, there],
            scratch_shapes=[pltpu.VMEM((2 * rows, 2 * chunk), BF16), pltpu.VMEM((2 * rows, 2 * LANES), BF16)],
        ),
        out_shape=[jax.ShapeDtypeStruct((8, high, chunk), BF16)] * 2
        + [jax.ShapeDtypeStruct((2, 4, high, chunk), BF16)] * 2,
        compiler_params=pltpu.CompilerParams(vmem_limit_bytes=54 * 2**20, dimension_semantics=("arbitrary",) * 2),
        cost_estimate=LIGHT,
        name="weight_gradients",
    )(order, x_turned, kept_turned, draw_turned, own, far, emit_own, emit_far)


def layer_kernel(col_ref, x_ref, *refs):
    hid_refs, out_ref = refs[:4], refs[4]
    model = x_ref.shape[1]
    mask = pl.program_id(0) ^ col_ref[0]
    x = x_ref[...].astype(F32)

    def body(hid_ref):
        for d in range(2):
            out_ref[:, d, :] = (x + hid_ref[:, d * model : (d + 1) * model].astype(F32)).astype(BF16)

    for n in range(4):
        pl.when(mask == n)(functools.partial(body, hid_refs[n]))


def layer_sum(col, x, hiddens):
    rows, wide = hiddens[0].shape
    model = x.shape[1]
    return pl.pallas_call(
        layer_kernel,
        grid_spec=pltpu.PrefetchScalarGridSpec(
            num_scalar_prefetch=1,
            grid=(4,),
            in_specs=[pl.BlockSpec((rows, model), lambda n, c: (n, 0))] + [whole((rows, wide))] * 4,
            out_specs=pl.BlockSpec((rows, 2, model), lambda n, c: (n, 0, 0)),
        ),
        out_shape=jax.ShapeDtypeStruct((x.shape[0], 2, model), BF16),
        compiler_params=pltpu.CompilerParams(vmem_limit_bytes=16 * 2**20),
        cost_estimate=LIGHT,
        name="layer_sum",
    )(col.reshape(1).astype(jnp.int32), x, *hiddens)


def turn_rows_kernel(own_ref, met_ref, out_ref):
    rows = own_ref.shape[0]
    out_ref[:, :rows] = jnp.swapaxes(own_ref[...], 0, 1)
    out_ref[:, rows:] = jnp.swapaxes(met_ref[...], 0, 1)


def turn_rows(own, met):
    rows, wide = own.shape
    return pl.pallas_call(
        turn_rows_kernel,
        grid=(2,),
        out_shape=jax.ShapeDtypeStruct((wide, 2 * rows), BF16),
        in_specs=[pl.BlockSpec((rows, wide // 2), lambda n: (0, n))] * 2,
        out_specs=pl.BlockSpec((wide // 2, 2 * rows), lambda n: (n, 0)),
        compiler_params=pltpu.CompilerParams(vmem_limit_bytes=16 * 2**20),
        cost_estimate=LIGHT,
        name="turn_rows",
    )(own, met)


def turn_kernel(*refs):
    w_refs, p_refs, wt_refs, pt_refs = (refs[n * PARTS : (n + 1) * PARTS] for n in range(4))
    for source, target in zip(w_refs, wt_refs):
        target[...] = jnp.swapaxes(source[...], 0, 1)

    @pl.when(pl.program_id(0) == 0)
    def _():
        for source, target in zip(p_refs, pt_refs):
            lines, hidden = source.shape[0], source.shape[1] // 2
            target[:, :lines] = jnp.swapaxes(source[:, :hidden], 0, 1)
            target[:, lines:] = jnp.swapaxes(source[:, hidden:], 0, 1)


def turn(pieces):
    width = pieces[0].shape[1]
    hidden, piece = width // 2, width // 4
    cut = width // 4
    results = pl.pallas_call(
        turn_kernel,
        grid=(4,),
        out_shape=[jax.ShapeDtypeStruct((width, hidden), BF16)] * PARTS
        + [jax.ShapeDtypeStruct((hidden, piece), BF16)] * PARTS,
        in_specs=[pl.BlockSpec((hidden, cut), lambda n: (0, n))] * PARTS
        + [pl.BlockSpec((piece // 2, width), lambda n: (2 * hidden // piece, 0))] * PARTS,
        out_specs=[pl.BlockSpec((cut, hidden), lambda n: (n, 0))] * PARTS
        + [pl.BlockSpec((hidden, piece), lambda n: (0, 0))] * PARTS,
        compiler_params=pltpu.CompilerParams(vmem_limit_bytes=20 * 2**20, dimension_semantics=("arbitrary",)),
        cost_estimate=LIGHT,
        name="turn_pieces",
    )(*pieces, *pieces)
    return results[:PARTS], results[PARTS:]


def assemble_kernel(order_ref, *refs):
    weight_out, proj_out = refs[4:]
    depth = weight_out.shape[1]
    group = refs[0].shape[-2] - depth

    def body(tiles):
        for u, tile_ref in enumerate(tiles):
            value = tile_ref[0, 0].astype(F32)
            lanes = slice(u * LANES, (u + 1) * LANES)
            for q in range(4):
                columns = slice(q * LANES, (q + 1) * LANES)
                weight_out[0, :, q, lanes] = value[:depth, columns]
                proj_out[0, q * group : (q + 1) * group, lanes] = value[depth:, columns]

    far = (pl.program_id(1) // 2) ^ order_ref[1]
    pl.when(far == 0)(lambda: body(refs[:2]))
    pl.when(far == 1)(lambda: body(refs[2:4]))


def assemble(order, own0, own1, far0, far1, depth):
    lines = own0.shape[2]
    group = lines - depth
    cells = 8 * LANES
    piece = pl.BlockSpec((1, 1, lines, 4 * LANES), lambda d, n, o: (d ^ o[0], (n % 2) ^ o[2], 0, 0))
    return pl.pallas_call(
        assemble_kernel,
        grid_spec=pltpu.PrefetchScalarGridSpec(
            num_scalar_prefetch=1,
            grid=(2, 4),
            in_specs=[piece] * 4,
            out_specs=[
                pl.BlockSpec((1, depth, 4, 2 * LANES), lambda d, n, o: (d, 0, 0, n)),
                pl.BlockSpec((1, 4 * group, 2 * LANES), lambda d, n, o: (d, 0, n)),
            ],
        ),
        out_shape=[
            jax.ShapeDtypeStruct((2, depth, 4, cells), F32),
            jax.ShapeDtypeStruct((2, 4 * group, cells), F32),
        ],
        compiler_params=pltpu.CompilerParams(vmem_limit_bytes=16 * 2**20),
        cost_estimate=LIGHT,
        name="assemble_gradients",
    )(order, own0, own1, far0, far1)


def input_grad_kernel(has_sum, *refs):
    slab_refs, w_refs, out_ref = refs[:2], refs[2:6], refs[-1]
    chunk = 4 * LANES
    model = out_ref.shape[1]
    total = refs[6][...] if has_sum else None
    for side in range(2):
        for u in range(2):
            for quarter in range(2):
                at = (u * 2 + quarter) * chunk
                part = lax.dot_general(
                    slab_refs[side][:, at : at + chunk],
                    w_refs[side * 2 + quarter][:model, u * chunk : (u + 1) * chunk],
                    (((1,), (1,)), ((), ())),
                    preferred_element_type=F32,
                )
                total = part if total is None else total + part
    out_ref[...] = total


def add_input_grad(slabs, weights, total):
    rows, half = slabs[0].shape
    model = weights[0].shape[1] // 2
    tile = rows // 2
    operands = [*slabs, *weights] + ([] if total is None else [total])
    lines = lambda n: pl.BlockSpec((tile, n), lambda s: (s, 0))
    return pl.pallas_call(
        functools.partial(input_grad_kernel, total is not None),
        grid=(2,),
        out_shape=jax.ShapeDtypeStruct((rows, model), F32),
        in_specs=[lines(half)] * 2
        + [whole(w.shape) for w in weights]
        + ([] if total is None else [lines(model)]),
        out_specs=lines(model),
        compiler_params=pltpu.CompilerParams(vmem_limit_bytes=24 * 2**20),
        cost_estimate=LIGHT,
        name="input_gradient",
    )(*operands)


def after(values):
    return lax.optimization_barrier(values)


def one_direction(inputs, reset_flags, gate_weight, gate_bias, proj_weight, grad_out):
    row, col = lax.axis_index("rows"), lax.axis_index("cols")
    layer, core = row // 2, row % 2
    direction, pair = layer // 2, layer % 2
    model = inputs.shape[1]
    local = inputs.shape[0] // STEPS
    share = local // 4
    rows = 2 * share
    cells = gate_weight.shape[3]
    piece = cells // PARTS
    width = 4 * piece
    tiles = piece // LANES

    def mask_of(r, near):
        odd = (r // 2) % 2
        return (2 if odd else 1) if near else (1 if odd else 2)

    def over_chips(value, near):
        pairs = [(r * 4 + j, r * 4 + (j ^ mask_of(r, near))) for r in range(8) for j in range(4)]
        return lax.ppermute(value, ("rows", "cols"), pairs)

    def over_rows(value, mask):
        return lax.ppermute(value, "rows", [(r, r ^ mask) for r in range(8)])

    core_swap = functools.partial(over_rows, mask=1)
    pair_swap = functools.partial(over_rows, mask=2)
    half_swap = functools.partial(over_rows, mask=4)
    near_mask = jnp.where(pair == 0, 1, 2)
    block_at = [col, col ^ near_mask, col ^ (3 - near_mask), col ^ 3]
    by_dir = lambda pair_of: jnp.where(direction == 0, pair_of[0], pair_of[1])
    by_other = lambda pair_of: jnp.where(direction == 0, pair_of[1], pair_of[0])
    in_run = lambda value: jnp.where(direction == 0, value, value[::-1])

    order = jnp.stack([direction, core, pair]).astype(jnp.int32)

    def place_of(part):
        return jnp.stack([direction, (core ^ (part // 2)) * 2 + (pair ^ (part % 2))]).astype(jnp.int32)

    places = [place_of(part) for part in range(PARTS)]
    input_piece = lambda part: own_piece(places[part], gate_weight, gate_bias, False)
    recurrent_piece = lambda part: own_piece(places[part], gate_weight, proj_weight, True)

    local_windows = lambda value: lax.dynamic_slice_in_dim(value, col * share, share, 0)
    steps_first = lambda value: jnp.swapaxes(value, 0, 1)
    by_side = lambda k, there: [jnp.where(core == which, k, there) for which in range(2)]

    w_in = {(0, 0): own_piece(places[0], gate_weight, gate_bias, False, memory=60)}
    w_rec = {}
    w_in[1, 0] = over_chips(w_in[0, 0], True)
    w_in[2, 0] = over_chips(w_in[0, 0], False)
    w_rec[0, 0] = recurrent_piece(0)

    keep_grid = local_windows(reset_flags.reshape(local, STEPS)).astype(F32)
    position = lax.broadcasted_iota(jnp.int32, (share, STEPS), 1)
    keep_ahead = jnp.where(position > 0, 1.0 - keep_grid, 0.0)
    next_flags = jnp.concatenate([keep_grid[:, 1:], jnp.zeros((share, 1), F32)], axis=1)
    keep_behind = jnp.where(position < STEPS - 1, 1.0 - next_flags, 0.0)
    own_tokens = share * STEPS
    x_mine = lax.dynamic_slice_in_dim(inputs, col * own_tokens, own_tokens, 0).reshape(share, STEPS, model)
    x_mine = steps_first(x_mine)
    keep_dirs = (steps_first(keep_ahead), steps_first(keep_behind))
    keep_wide = [jnp.broadcast_to(k[..., None], (STEPS, share, LANES)).astype(BF16) for k in keep_dirs]
    xk_here = jnp.concatenate([x_mine, by_dir(keep_wide)], axis=2)
    xk_sent = jnp.concatenate([x_mine, by_other(keep_wide)], axis=2)
    xk_met = half_swap(xk_sent)
    w_in[0, 1] = input_piece(1)
    g_mine = lax.dynamic_slice_in_dim(grad_out, col * own_tokens, own_tokens, 0).reshape(share, STEPS, 2, model)
    g_dirs = (steps_first(g_mine[:, :, 0]), steps_first(g_mine[:, :, 1]))
    w_in, w_rec, xk_here, xk_met, g_dirs, places = after((w_in, w_rec, xk_here, xk_met, g_dirs, places))

    w_rec[1, 0] = over_chips(w_rec[0, 0], True)
    w_in[3, 0] = over_chips(w_in[1, 0], False)
    w_in[2, 1] = pair_swap(w_in[1, 0])
    for b in (1, 2):
        w_in[b, 2] = core_swap(w_in[b, 0])
    w_rec[0, 1], w_in[0, 2], w_in[0, 3] = recurrent_piece(1), input_piece(2), input_piece(3)
    xk = in_run(jnp.concatenate([xk_here, xk_met], axis=1))
    x_run, keep_run = xk[..., :model], xk[..., model:].astype(F32)
    x_flat = x_run.reshape(STEPS * rows, model)
    w_in, w_rec, x_flat, keep_run, g_dirs, places = after((w_in, w_rec, x_flat, keep_run, g_dirs, places))

    gates_of = lambda b: input_gates(x_flat, [w_in[b, part] for part in range(PARTS)])
    turn_of = lambda b: turn([w_rec[b, part] for part in range(PARTS)])
    w_in[1, 1] = over_chips(w_in[0, 1], True)
    w_rec[3, 0] = over_chips(w_rec[1, 0], False)
    w_in[3, 1] = pair_swap(w_in[3, 0])
    w_rec[1, 2], w_in[3, 2] = core_swap(w_rec[1, 0]), core_swap(w_in[3, 0])
    w_rec[0, 2], w_rec[0, 3] = recurrent_piece(2), recurrent_piece(3)
    px, turned = {0: gates_of(0)}, {}
    w_in, w_rec, px, x_flat = after((w_in, w_rec, px, x_flat))

    w_rec[1, 1] = over_chips(w_rec[0, 1], True)
    w_rec[2, 0] = over_chips(w_rec[0, 0], False)
    w_rec[2, 1] = pair_swap(w_rec[1, 0])
    for b in (1, 2, 3):
        w_in[b, 3] = core_swap(w_in[b, 1])
    turned[0] = turn_of(0)
    for b in (1, 2, 3):
        px[b] = gates_of(b)
    w_in, w_rec, px, turned, x_flat = after((w_in, w_rec, px, turned, x_flat))

    last_half = w_rec[3, 0].shape[0] // 2
    last_piece = [pair_swap(w_rec[3, 0][:last_half]), over_chips(w_rec[1, 1][last_half:], False)]
    w_rec[1, 3], w_rec[2, 2] = core_swap(w_rec[1, 1]), core_swap(w_rec[2, 0])
    w_rec[2, 3], w_rec[3, 2] = core_swap(w_rec[2, 1]), core_swap(w_rec[3, 0])
    x_met = core_swap(x_flat)
    turned[1], turned[2] = turn_of(1), turn_of(2)
    w_rec, turned, last_piece, x_met = after((w_rec, turned, last_piece, x_met))

    w_rec[3, 1] = jnp.concatenate(last_piece, axis=0)
    w_rec[3, 3] = core_swap(w_rec[3, 1])
    turned[3] = turn_of(3)
    x_turned = turn_rows(x_flat, x_met)
    g_sent = by_other(g_dirs)
    w_rec, turned, x_turned, g_sent = after((w_rec, turned, x_turned, g_sent))

    g_met = half_swap(g_sent)
    px = [px[b].reshape(STEPS, rows, PARTS * width) for b in range(BLOCKS)]
    pre, cell, emit_own, emit_far, raw, kept, hid = run_forward(
        px, keep_run, [w_rec[b, part] for b in range(BLOCKS) for part in range(PARTS)]
    )

    pre, cell, emit_own, emit_far, raw, kept, hid, g_met = after((pre, cell, emit_own, emit_far, raw, kept, hid, g_met))
    g_run = in_run(jnp.concatenate([by_dir(g_dirs), g_met], axis=1))

    flat = lambda value: value.reshape(STEPS * rows, value.shape[-1])
    hid_time = in_run(hid)
    hid_here, hid_there = hid_time[:, :share], half_swap(hid_time[:, share:])
    emit_met = core_swap(flat(emit_far))
    kept = flat(kept)
    kept_met = core_swap(kept)

    def over_cols(value, mask):
        return lax.ppermute(value, "cols", [(j, j ^ mask) for j in range(4)])

    slabs, draw, bias_sums = run_backward(
        pre,
        cell,
        raw,
        g_run,
        keep_run,
        [w for b in range(BLOCKS) for w in turned[b][0]],
        [p for b in range(BLOCKS) for p in turned[b][1]],
    )
    hid_here, hid_there, kept, kept_met, slabs, draw, bias_sums, emit_own, emit_met = after(
        (hid_here, hid_there, kept, kept_met, slabs, draw, bias_sums, emit_own, emit_met)
    )

    slabs = [[flat(value) for value in block] for block in slabs]
    emit_own, draw = flat(emit_own), flat(draw)
    bias_parts = jnp.sum(bias_sums, axis=0).reshape(BLOCKS, 4, 2, 2 * piece)
    bias_half = bias_parts[:, :, 0] + core_swap(bias_parts[:, :, 1])
    draw_met, far = core_swap(draw), {3: core_swap(slabs[3][1])}
    far[1] = core_swap(after((slabs[1][1], draw_met))[0])
    kept_turned, draw_turned = turn_rows(kept, kept_met), turn_rows(draw, draw_met)

    def grads(b):
        left = (x_turned, kept_turned, draw_turned)
        return block_grads(order, *left, slabs[b][0], far[b], emit_own, emit_met, b)

    def add(first, *others):
        total = first.astype(F32)
        for other in others:
            total = total + other.astype(F32)
        return total.astype(BF16)

    def flip(value):
        return jnp.concatenate([value[1:], value[:1]], axis=0)

    opposite = grads(3)
    far, opposite, kept_turned, draw_turned, slabs, bias_half = after(
        (far, opposite, kept_turned, draw_turned, slabs, bias_half)
    )

    relay_a, relay_b = over_chips(opposite[0], True), over_chips(opposite[1], False)
    met = pair_swap(opposite[3])
    far[2] = core_swap(slabs[2][1])
    bias_met = [over_chips(bias_half[1], True), over_chips(bias_half[2], False)]
    near = grads(1)
    other = grads(2)
    hid_both = jnp.concatenate([by_dir((hid_here, hid_there)), by_other((hid_here, hid_there))], axis=2)
    hid_both = steps_first(hid_both).reshape(own_tokens, 2 * model)
    far, relay_a, relay_b, met, near, other, slabs, bias_met, hid_both = after(
        (far, relay_a, relay_b, met, near, other, slabs, bias_met, hid_both)
    )

    near_a, other_b = over_chips(near[0], True), over_chips(other[1], False)
    other_met = pair_swap(near[3])
    far[0] = core_swap(slabs[0][1])
    bias_met = bias_met + [over_cols(bias_half[3], 3)]
    near_b, other_a = add(near[1], relay_b), add(other[0], relay_a)
    opposite1 = add(opposite[2], flip(met))
    own = grads(0)
    near1, other1, own0, own1 = near[2:], other[2:], own[:2], own[2:]
    near_a, other_b, other_met, opposite1, near_b, other_a, other1, own0, own1, slabs, bias_met = after(
        (near_a, other_b, other_met, opposite1, near_b, other_a, other1, own0, own1, slabs, bias_met)
    )

    near_b, other_a = over_chips(near_b, True), over_chips(other_a, False)
    near_met = pair_swap(other1[1])
    wide = None
    for b in range(BLOCKS):
        wide = add_input_grad(slabs[b], [w_in[b, part] for part in range(PARTS)], wide)
    bias_half = bias_half[0] + bias_met[0] + bias_met[1] + bias_met[2]
    bias_half = jnp.where(pair == 0, bias_half, jnp.concatenate([bias_half[:, piece:], bias_half[:, :piece]], axis=1))
    bias_met = pair_swap(bias_half)
    own0 = [add(own0[0], near_a), add(own0[1], other_b)]
    other_a1, other_b1 = add(other1[0][0], other_met[1]), add(other1[0][1], other_met[0])
    dx = in_run(wide.reshape(STEPS, rows, model))
    dx, dx_sent = dx[:, :share], dx[:, share:].astype(BF16)
    near_b, other_a, near_met, dx, dx_sent, own0, own1, bias_met, other_a1, other_b1 = after(
        (near_b, other_a, near_met, dx, dx_sent, own0, own1, bias_met, other_a1, other_b1)
    )

    relay_a, relay_b = over_chips(opposite1[0], True), over_chips(opposite1[1], False)
    near_a1, near_b1 = add(near1[0][0], near_met[1]), add(near1[0][1], near_met[0])
    near_a1, other_b1 = over_chips(near_a1, True), over_chips(other_b1, False)
    count = own0[0].shape[0] // 2
    sums0_met = pair_swap(jnp.stack([add(own0[0][count:], other_a[count:]), add(own0[1][count:], near_b[count:])]))
    sums0 = [add(own0[0][:count], other_a[:count]), add(own0[1][:count], near_b[:count])]
    bias_half = bias_half + bias_met
    lines, rest = [], bias_half
    for _ in range(3):
        lines.append(lax.reduce_precision(rest, 8, 7))
        rest = rest - lines[-1]
    lines = jnp.concatenate(lines + [jnp.zeros_like(rest)], axis=0).astype(BF16)
    dx_met = half_swap(jnp.concatenate([dx_sent.reshape(own_tokens, model), lines], axis=0))
    near_a1, near_b1, other_a1, other_b1, relay_a, relay_b, sums0, sums0_met, dx, dx_met, own1, bias_half = after(
        (near_a1, near_b1, other_a1, other_b1, relay_a, relay_b, sums0, sums0_met, dx, dx_met, own1, bias_half)
    )

    near_b1, other_a1 = over_chips(add(near_b1, relay_b), True), over_chips(add(other_a1, relay_a), False)
    own_met = pair_swap(own1[1])
    sums0_sent = jnp.stack([add(sums0[n][2:], sums0_met[1 - n][2:]) for n in range(2)])
    there0 = half_swap(sums0_sent)
    here0 = jnp.stack([add(sums0[n][:2], sums0_met[1 - n][:2]) for n in range(2)])
    bias_there = dx_met[own_tokens:].astype(F32).reshape(4, 4, 2 * piece)
    bias_there = bias_there[0] + bias_there[1] + bias_there[2]
    bias_half = jnp.stack([by_dir((bias_half, bias_there)), by_other((bias_half, bias_there))])
    dx_met = dx_met[:own_tokens].reshape(STEPS, share, model)
    dx = dx + dx_met.astype(F32) + g_dirs[0].astype(F32) + g_dirs[1].astype(F32)
    dx = steps_first(dx.astype(BF16)).reshape(own_tokens, model)
    share_width = model // 4
    slice_for = lambda mask: lax.dynamic_slice_in_dim(dx, (col ^ mask) * share_width, share_width, 1)
    outgoing = [jnp.concatenate([hid_both, slice_for(mask)], axis=1) for mask in range(4)]
    incoming = [outgoing[0], None, None, over_cols(outgoing[3], 3)]
    own_a1, own_b1 = add(own1[0][0], near_a1), add(own1[0][1], other_b1)
    near_b1, other_a1, own_met, here0, there0, own_a1, own_b1, incoming[0], incoming[3], outgoing, bias_half = after(
        (near_b1, other_a1, own_met, here0, there0, own_a1, own_b1, incoming[0], incoming[3], outgoing, bias_half)
    )

    parts1 = ((own_a1, own_met[1], other_a1), (own_b1, own_met[0], near_b1))
    there1 = half_swap(jnp.stack([add(*(value[2:] for value in parts)) for parts in parts1]))
    here1 = jnp.stack([add(*(value[:2] for value in parts)) for parts in parts1])

    def two_directions(here, there):
        both = jnp.stack([here, there])
        return both[:, :, 0], both[:, :, 1]

    kept0, sent0 = two_directions(here0, there0)
    met0 = core_swap(sent0)
    incoming[1], incoming[2] = over_cols(outgoing[1], 1), over_cols(outgoing[2], 2)
    block_out = layer_sum(col, inputs, [value[:, : 2 * model] for value in incoming])
    input_grad = jnp.zeros((BLOCKS * own_tokens, share_width), BF16)
    for mask, value in enumerate(incoming):
        input_grad = lax.dynamic_update_slice(input_grad, value[:, 2 * model :], ((col ^ mask) * own_tokens, 0))
    bias_total = jnp.concatenate(by_side(bias_half, core_swap(bias_half)), axis=2)
    here1, there1, kept0, met0, block_out, input_grad, bias_total = after(
        (here1, there1, kept0, met0, block_out, input_grad, bias_total)
    )

    kept1, sent1 = two_directions(here1, there1)
    met1 = core_swap(sent1)
    weight_share, proj_share = assemble(order, kept0, kept1, met0, met1, 2 * model // 8)
    proj_share = jnp.swapaxes(proj_share, 1, 2)
    return (block_out, input_grad, weight_share, bias_total, proj_share)


def solution(mesh):
    placed = (
        P("rows", None),
        P("rows"),
        P(None, None, None, "cols"),
        P(None, None, "cols"),
        P(None, "cols", None),
        P("rows", None, None),
    )
    plan = one_direction if (mesh.shape["rows"], mesh.shape["cols"]) == (8, 4) else shared_cells
    return jax.shard_map(
        plan,
        mesh=mesh,
        in_specs=placed,
        out_specs=(
            P("rows", None, None),
            P("rows", "cols"),
            P(None, "rows", None, "cols"),
            P(None, None, "cols"),
            P(None, "cols", "rows"),
        ),
        check_vma=False,
    )
```

```python
import functools

import jax
import jax.numpy as jnp
from jax import lax
from jax.experimental import pallas as pl
from jax.experimental.pallas import tpu as pltpu
from jax.sharding import PartitionSpec as P

STEPS = 20
BF16 = jnp.bfloat16
F32 = jnp.float32
THIRD = 1.0 / 3.0
LANES = 128
BLOCKS = 4
LIGHT = pl.CostEstimate(flops=1, bytes_accessed=1, transcendentals=0)
PARTS = 4


def soft_clip(amount):
    return 3.0 * jnp.tanh(amount / 3.0)


def clip_slope(amount):
    tangent = jnp.tanh(amount / 3.0)
    return 1.0 - tangent * tangent


def shared_cells(inputs, reset_flags, gate_weight, gate_bias, proj_weight, grad_out):
    tok_rows, model_width = inputs.shape
    windows = tok_rows // STEPS
    cell_cols = gate_weight.shape[3]
    gate_width = 4 * cell_cols
    share_width = model_width // lax.axis_size("cols")
    column = lax.axis_index("cols") * share_width
    weight = gate_weight.reshape(2, 2 * model_width, gate_width)
    w_input = weight[:, :model_width]
    w_recur = weight[:, model_width:]
    bias_row = gate_bias.reshape(2, 1, gate_width)
    sequence = jnp.swapaxes(inputs.reshape(windows, STEPS, model_width), 0, 1)
    x_stack = jnp.stack([sequence, sequence[::-1]], axis=1)
    flag_grid = jnp.swapaxes(reset_flags.reshape(windows, STEPS), 0, 1).astype(jnp.float32)
    position = lax.broadcasted_iota(jnp.int32, (STEPS, windows), 0)
    keep_ahead = jnp.where(position > 0, 1.0 - flag_grid, 0.0)
    next_flags = jnp.concatenate([flag_grid[1:], jnp.zeros((1, windows), jnp.float32)], axis=0)
    keep_behind = jnp.where(position < STEPS - 1, 1.0 - next_flags, 0.0)
    keep_stack = jnp.stack([keep_ahead, keep_behind[::-1]], axis=1)[..., None]
    input_gates = jnp.einsum("sdwh,dhg->sdwg", x_stack, w_input, preferred_element_type=jnp.float32)

    def forward_step(state_pair, pieces):
        hidden, cell_prev = state_pair
        gates_in, keep_step = pieces
        kept_hidden = hidden * keep_step.astype(jnp.bfloat16)
        gate_pre = (
            gates_in
            + jnp.einsum("dwh,dhg->dwg", kept_hidden, w_recur, preferred_element_type=jnp.float32)
            + bias_row
        )
        in_gate = jax.nn.sigmoid(gate_pre[..., :cell_cols])
        forget = jax.nn.sigmoid(gate_pre[..., cell_cols : 2 * cell_cols])
        update = jnp.tanh(gate_pre[..., 2 * cell_cols : 3 * cell_cols])
        out_gate = jax.nn.sigmoid(gate_pre[..., 3 * cell_cols :])
        kept_cell = cell_prev * keep_step
        cell_new = soft_clip(forget * kept_cell + in_gate * update)
        cell_output = (out_gate * jnp.tanh(cell_new)).astype(jnp.bfloat16)
        partial_raw = jnp.einsum(
            "dwc,dch->dwh", cell_output, proj_weight, preferred_element_type=jnp.float32
        )
        proj_raw = lax.psum(partial_raw, "cols")
        new_hidden = soft_clip(proj_raw).astype(jnp.bfloat16)
        return (
            (new_hidden, cell_new),
            (kept_hidden, gate_pre, kept_cell, cell_new, cell_output, proj_raw, new_hidden),
        )

    init_state = (
        jnp.zeros((2, windows, model_width), jnp.bfloat16),
        jnp.zeros((2, windows, cell_cols), jnp.float32),
    )
    _, fwd_saved = lax.scan(forward_step, init_state, (input_gates, keep_stack))
    kept_all, pre_all, kept_cells, cell_states, cell_outputs, proj_raws, hiddens = fwd_saved
    ahead_hidden = hiddens[:, 0]
    behind_hidden = hiddens[::-1, 1]
    both_outputs = jnp.stack([ahead_hidden, behind_hidden], axis=2).astype(jnp.float32) + sequence[
        :, :, None, :
    ].astype(jnp.float32)
    block_out = (
        jnp.swapaxes(both_outputs, 0, 1).reshape(tok_rows, 2, model_width).astype(jnp.bfloat16)
    )
    out_grid = jnp.transpose(grad_out.reshape(windows, STEPS, 2, model_width), (1, 2, 0, 3))
    grad_stack = jnp.stack([out_grid[:, 0], out_grid[::-1, 1]], axis=1)

    def backward_step(state_pair, pieces):
        recur_part, cell_grad = state_pair
        gate_pre, kept_cell, cell_new, cell_output, proj_raw, grad_step, keep_step = pieces
        recur_sum = lax.psum(recur_part, "cols")
        hidden_grad = grad_step.astype(jnp.float32) + recur_sum
        raw_grad = (hidden_grad * clip_slope(proj_raw)).astype(jnp.bfloat16)
        emit_grad = jnp.einsum(
            "dwh,dch->dwc", raw_grad, proj_weight, preferred_element_type=jnp.float32
        )
        in_gate = jax.nn.sigmoid(gate_pre[..., :cell_cols])
        forget = jax.nn.sigmoid(gate_pre[..., cell_cols : 2 * cell_cols])
        update = jnp.tanh(gate_pre[..., 2 * cell_cols : 3 * cell_cols])
        out_gate = jax.nn.sigmoid(gate_pre[..., 3 * cell_cols :])
        tanh_cell = jnp.tanh(cell_new)
        cell_total = cell_grad + emit_grad * out_gate * (1.0 - tanh_cell * tanh_cell)
        cell_third = cell_new / 3.0
        cell_raw_grad = cell_total * (1.0 - cell_third * cell_third)
        pre_grad = jnp.concatenate(
            [
                cell_raw_grad * update * in_gate * (1.0 - in_gate),
                cell_raw_grad * kept_cell * forget * (1.0 - forget),
                cell_raw_grad * in_gate * (1.0 - update * update),
                emit_grad * tanh_cell * out_gate * (1.0 - out_gate),
            ],
            axis=-1,
        ).astype(jnp.bfloat16)
        recur_next = (
            jnp.einsum("dwg,dhg->dwh", pre_grad, w_recur, preferred_element_type=jnp.float32)
            * keep_step
        )
        cell_next = cell_raw_grad * forget * keep_step
        return ((recur_next, cell_next), (pre_grad, raw_grad))

    zero_state = (
        jnp.zeros((2, windows, model_width), jnp.float32),
        jnp.zeros((2, windows, cell_cols), jnp.float32),
    )
    _, back_saved = lax.scan(
        backward_step,
        zero_state,
        (pre_all, kept_cells, cell_states, cell_outputs, proj_raws, grad_stack, keep_stack),
        reverse=True,
    )
    pre_grads, raw_grads = back_saved
    input_part = jnp.einsum(
        "sdwg,dhg->sdwh", pre_grads, w_input, preferred_element_type=jnp.float32
    )
    input_sum = jnp.swapaxes(input_part[:, 0] + input_part[::-1, 1], 0, 1).reshape(
        tok_rows, model_width
    )
    input_share = lax.psum_scatter(
        input_sum.astype(jnp.bfloat16), "cols", scatter_dimension=1, tiled=True
    ).astype(jnp.float32)
    residual_grad = grad_out[:, 0].astype(jnp.float32) + grad_out[:, 1].astype(jnp.float32)
    input_grad = (
        input_share + lax.dynamic_slice_in_dim(residual_grad, column, share_width, 1)
    ).astype(jnp.bfloat16)
    input_weight_grad = jnp.einsum(
        "sdwh,sdwg->dhg", x_stack, pre_grads, preferred_element_type=jnp.float32
    )
    recur_weight_grad = jnp.einsum(
        "sdwh,sdwg->dhg", kept_all, pre_grads, preferred_element_type=jnp.float32
    )
    weight_grad = jnp.concatenate([input_weight_grad, recur_weight_grad], axis=1).reshape(
        2, 2 * model_width, 4, cell_cols
    )
    proj_grad = jnp.einsum(
        "sdwc,sdwh->dch", cell_outputs, raw_grads, preferred_element_type=jnp.float32
    )
    bias_grad = jnp.sum(pre_grads, axis=(0, 2), dtype=jnp.float32).reshape(2, 4, cell_cols)
    weight_share, proj_share = (
        lax.psum_scatter(
            weight_grad.astype(jnp.bfloat16), "rows", scatter_dimension=1, tiled=True
        ).astype(jnp.float32),
        lax.psum_scatter(
            proj_grad.astype(jnp.bfloat16), "rows", scatter_dimension=2, tiled=True
        ).astype(jnp.float32),
    )
    bias_total = lax.psum(bias_grad, "rows")
    return (block_out, input_grad, weight_share, bias_total, proj_share)


def sigmoid(amount):
    return 0.5 * jnp.tanh(0.5 * amount) + 0.5


def whole(shape):
    return pl.BlockSpec(shape, lambda *_: (0,) * len(shape), pipeline_mode=pl.Buffered(1))


def matmul(a, b):
    return jnp.dot(a, b, preferred_element_type=F32)


def own_piece_kernel(order_ref, w_ref, extra_ref, out_ref):
    step = pl.program_id(0)
    lines = w_ref.shape[1]
    model, width = extra_ref.shape[-1] if extra_ref.shape[1] > 4 else None, out_ref.shape[1]
    for u in range(2):
        for q in range(4):
            to = (u * 4 + q) * LANES
            out_ref[pl.ds(step * lines, lines), to : to + LANES] = w_ref[0, :, q, u * LANES : (u + 1) * LANES]
    base = width // 2

    @pl.when(step == 0)
    def _():
        if model is None:
            rest = jnp.concatenate(
                [extra_ref[0, q : q + 1, u * LANES : (u + 1) * LANES] for u in range(2) for q in range(4)], axis=1
            )
            parts = []
            for _ in range(3):
                parts.append(rest.astype(BF16).astype(F32))
                rest = rest - parts[-1]
            parts.append(jnp.zeros((13, width), F32))
            out_ref[base:, :] = jnp.concatenate(parts, axis=0).astype(BF16)
        else:
            half = extra_ref.shape[1] // 2
            out_ref[base:, :model] = extra_ref[0, :half, :]
            out_ref[base:, model:] = extra_ref[0, half:, :]


def own_piece(place, gate_weight, extra, recurrent, memory=16):
    model, piece = gate_weight.shape[1] // 2, gate_weight.shape[3] // PARTS
    cut = model // 4
    first = 4 if recurrent else 0
    if recurrent:
        extra_spec = pl.BlockSpec((1, piece, model), lambda n, p: (p[0], p[1], 0))
    else:
        extra_spec = pl.BlockSpec((1, 4, piece), lambda n, p: (p[0], 0, p[1]))
    lines = model + (piece // 2 if recurrent else 16)
    return pl.pallas_call(
        own_piece_kernel,
        grid_spec=pltpu.PrefetchScalarGridSpec(
            num_scalar_prefetch=1,
            grid=(4,),
            in_specs=[pl.BlockSpec((1, cut, 4, piece), lambda n, p: (p[0], n + first, 0, p[1])), extra_spec],
            out_specs=pl.BlockSpec((lines, 4 * piece), lambda n, p: (0, 0)),
        ),
        out_shape=jax.ShapeDtypeStruct((lines, 4 * piece), BF16),
        compiler_params=pltpu.CompilerParams(vmem_limit_bytes=memory * 2**20, dimension_semantics=("arbitrary",)),
        cost_estimate=LIGHT,
        name="own_piece",
    )(place, gate_weight, extra)


def input_kernel(x_ref, w0, w1, w2, w3, out_ref):
    model, width = x_ref.shape[1], w0.shape[1]
    for n, w_ref in enumerate((w0, w1, w2, w3)):
        bias = jnp.sum(w_ref[model:, :].astype(F32), axis=0, keepdims=True)
        out_ref[:, n * width : (n + 1) * width] = (matmul(x_ref[...], w_ref[:model, :]) + bias).astype(BF16)


def input_gates(x, weights):
    rows, model = x.shape
    width = weights[0].shape[1]
    tile = rows // 2
    return pl.pallas_call(
        input_kernel,
        grid=(2,),
        out_shape=jax.ShapeDtypeStruct((rows, PARTS * width), BF16),
        in_specs=[pl.BlockSpec((tile, model), lambda n: (n, 0))] + [whole(w.shape) for w in weights],
        out_specs=pl.BlockSpec((tile, PARTS * width), lambda n: (n, 0)),
        compiler_params=pltpu.CompilerParams(vmem_limit_bytes=20 * 2**20),
        cost_estimate=LIGHT,
        name="input_gates",
    )(x, *weights)


def forward_kernel(*refs):
    px_refs, keep_ref = refs[:BLOCKS], refs[BLOCKS]
    w_refs = refs[BLOCKS + 1 : BLOCKS + 1 + BLOCKS * PARTS]
    pre_out, cell_out, emit_own, emit_far, raw_out, kept_out, hid_out, c_scr, h_scr = refs[BLOCKS + 1 + BLOCKS * PARTS :]
    step = pl.program_id(0)
    width = w_refs[0].shape[1]
    hidden = width // 2
    piece = width // 4
    cells = piece * PARTS
    tiles = piece // LANES
    half = cells // 2
    rows = keep_ref.shape[1]

    @pl.when(step == 0)
    def _():
        c_scr[...] = jnp.zeros_like(c_scr)
        h_scr[...] = jnp.zeros_like(h_scr)

    keep = keep_ref[0][:, :1]
    kept = (h_scr[...] * keep).astype(BF16)
    kept_out[0] = kept
    raw = jnp.zeros((rows, hidden), F32)
    for b in range(BLOCKS):
        parts, proj = [], []
        for s in range(PARTS):
            w_ref = w_refs[b * PARTS + s]
            pre = px_refs[b][0, :, s * width : (s + 1) * width].astype(F32) + matmul(kept, w_ref[:hidden, :])
            at = b * 4 * cells + s * width
            pre_out[0, :, at : at + width] = pre.astype(BF16)
            parts.append(pre)
            proj += [w_ref[hidden:, :hidden], w_ref[hidden:, hidden:]]
        gates = [
            jnp.concatenate(
                [part[:, (u * 4 + q) * LANES : (u * 4 + q + 1) * LANES] for part in parts for u in range(tiles)], axis=1
            )
            for q in range(4)
        ]
        i, f, u, o = sigmoid(gates[0]), sigmoid(gates[1]), jnp.tanh(gates[2]), sigmoid(gates[3])
        at = b * cells
        kept_cell = c_scr[:, at : at + cells] * keep
        cell = 3.0 * jnp.tanh((f * kept_cell + i * u) * THIRD)
        emit = (o * jnp.tanh(cell)).astype(BF16)
        c_scr[:, at : at + cells] = cell
        cell_out[0, :, at : at + cells] = cell
        emit_own[0, :, b * half : (b + 1) * half] = emit[:, :half]
        emit_far[0, :, b * half : (b + 1) * half] = emit[:, half:]
        raw = raw + matmul(emit, jnp.concatenate(proj, axis=0))
    raw_out[0] = raw
    hid = 3.0 * jnp.tanh(raw * THIRD)
    h_scr[...] = hid.astype(BF16).astype(F32)
    hid_out[0] = hid.astype(BF16)


def run_forward(px, keep, weights):
    steps, rows, wide = px[0].shape
    hidden = weights[0].shape[1] // 2
    total = BLOCKS * wide // 4
    block = lambda n: pl.BlockSpec((1, rows, n), lambda t: (t, 0, 0))
    sizes = (4 * total, total, total // 2, total // 2, hidden, hidden, hidden)
    kinds = (BF16, F32, BF16, BF16, F32, BF16, BF16)
    return pl.pallas_call(
        forward_kernel,
        grid=(steps,),
        out_shape=tuple(jax.ShapeDtypeStruct((steps, rows, n), kind) for n, kind in zip(sizes, kinds)),
        in_specs=[block(wide)] * BLOCKS + [block(LANES)] + [whole(w.shape) for w in weights],
        out_specs=tuple(block(n) for n in sizes),
        scratch_shapes=[pltpu.VMEM((rows, total), F32), pltpu.VMEM((rows, hidden), F32)],
        compiler_params=pltpu.CompilerParams(vmem_limit_bytes=48 * 2**20, dimension_semantics=("arbitrary",)),
        cost_estimate=pl.CostEstimate(
            flops=2 * steps * rows * hidden * 5 * total * 8,
            bytes_accessed=steps * rows * total * 24 + 10 * total * hidden,
            transcendentals=steps * rows * total * 6,
        ),
        name="forward_chain",
    )(*px, keep, *weights)


def backward_kernel(*refs):
    pre_ref, cell_ref, before_ref, raw_ref, grad_ref, keep_ref = refs[:6]
    wt_refs, pt_refs = refs[6 : 6 + BLOCKS * PARTS], refs[6 + BLOCKS * PARTS : 6 + 2 * BLOCKS * PARTS]
    outs = refs[6 + 2 * BLOCKS * PARTS :]
    slabs, draw_out, bias_out, dc_scr, dk_scr = outs[: 2 * BLOCKS], *outs[2 * BLOCKS :]
    step = pl.program_id(0)
    hidden, piece = pt_refs[0].shape
    cells = piece * PARTS
    tiles = piece // LANES
    width = 4 * piece
    chunk = 4 * LANES
    rows = keep_ref.shape[1]

    @pl.when(step == 0)
    def _():
        dc_scr[...] = jnp.zeros_like(dc_scr)
        dk_scr[...] = jnp.zeros_like(dk_scr)
        bias_out[...] = jnp.zeros_like(bias_out)

    keep = keep_ref[0][:, :1]
    tangent = jnp.tanh(raw_ref[0] * THIRD)
    draw = ((grad_ref[0].astype(F32) + dk_scr[...]) * (1.0 - tangent * tangent)).astype(BF16)
    draw_out[0] = draw
    dk = jnp.zeros((rows, hidden), F32)
    for b in range(BLOCKS):
        at = b * cells
        demit = matmul(draw, jnp.concatenate([pt_refs[b * PARTS + s][...] for s in range(PARTS)], axis=1))
        gates = [
            jnp.concatenate(
                [
                    pre_ref[0, :, 4 * at + s * width + (u * 4 + q) * LANES : 4 * at + s * width + (u * 4 + q + 1) * LANES]
                    for s in range(PARTS)
                    for u in range(tiles)
                ],
                axis=1,
            ).astype(F32)
            for q in range(4)
        ]
        i, f, u, o = sigmoid(gates[0]), sigmoid(gates[1]), jnp.tanh(gates[2]), sigmoid(gates[3])
        cell = cell_ref[0, :, at : at + cells]
        kept_cell = before_ref[0, :, at : at + cells] * keep
        tanh_cell = jnp.tanh(cell)
        third = cell * THIRD
        dcell = (dc_scr[:, at : at + cells] + demit * o * (1.0 - tanh_cell * tanh_cell)) * (1.0 - third * third)
        dgates = (
            dcell * u * i * (1.0 - i),
            dcell * kept_cell * f * (1.0 - f),
            dcell * i * (1.0 - u * u),
            demit * tanh_cell * o * (1.0 - o),
        )
        dc_scr[:, at : at + cells] = dcell * f * keep
        for q in range(4):
            folded = dgates[q][:8]
            for r in range(8, rows, 8):
                folded = folded + dgates[q][r : r + 8]
            bias_out[:, (b * 4 + q) * cells : (b * 4 + q + 1) * cells] += folded
        dgates = [dgate.astype(BF16) for dgate in dgates]
        for s in range(PARTS):
            part = jnp.concatenate(
                [
                    dgates[q][:, s * piece + u * LANES : s * piece + (u + 1) * LANES]
                    for u in range(tiles)
                    for q in range(4)
                ],
                axis=1,
            )
            side, quarter = s // 2, s % 2
            for u in range(tiles):
                to = (u * 2 + quarter) * chunk
                slabs[b * 2 + side][0, :, to : to + chunk] = part[:, u * chunk : (u + 1) * chunk]
            dk = dk + matmul(part, wt_refs[b * PARTS + s][...])
    dk_scr[...] = dk * keep


def run_backward(pre, cell, raw, grad, keep, weights, projs):
    steps, rows, gates = pre.shape
    total = gates // 4
    hidden, piece = projs[0].shape
    half = PARTS * piece * 2
    block = lambda n: pl.BlockSpec((1, rows, n), lambda s: (steps - 1 - s, 0, 0))
    before = pl.BlockSpec((1, rows, total), lambda s: (jnp.maximum(steps - 2 - s, 0), 0, 0))
    shape = lambda n: jax.ShapeDtypeStruct((steps, rows, n), BF16)
    out = pl.pallas_call(
        backward_kernel,
        grid=(steps,),
        out_shape=tuple([shape(half)] * (2 * BLOCKS) + [shape(hidden), jax.ShapeDtypeStruct((8, gates), F32)]),
        in_specs=[block(gates), block(total), before, block(hidden), block(hidden), block(LANES)]
        + [whole(w.shape) for w in [*weights, *projs]],
        out_specs=tuple([block(half)] * (2 * BLOCKS) + [block(hidden), pl.BlockSpec((8, gates), lambda s: (0, 0))]),
        scratch_shapes=[pltpu.VMEM((rows, total), F32), pltpu.VMEM((rows, hidden), F32)],
        compiler_params=pltpu.CompilerParams(vmem_limit_bytes=48 * 2**20, dimension_semantics=("arbitrary",)),
        cost_estimate=pl.CostEstimate(
            flops=2 * steps * rows * hidden * 5 * total * 8,
            bytes_accessed=steps * rows * total * 24 + 10 * total * hidden,
            transcendentals=steps * rows * total * 6,
        ),
        name="backward_chain",
    )(pre, cell, cell, raw, grad, keep, *weights, *projs)
    return [out[b * 2 : b * 2 + 2] for b in range(BLOCKS)], out[2 * BLOCKS], out[2 * BLOCKS + 1]


def block_kernel(order_ref, x_ref, kept_ref, draw_ref, own_ref, far_ref, own_emit, far_emit, *refs):
    first_a, first_b, second_here, second_there, right, emit = refs
    rows = own_ref.shape[0]
    tile, step = pl.program_id(0), pl.program_id(1)
    depth, lines = x_ref.shape[0] // 4, draw_ref.shape[0] // 8
    group = lines // 4
    chunk = 4 * LANES
    here = step ^ order_ref[2]

    @pl.when(step == 0)
    def _():
        right[:rows, :], right[rows:, :] = own_ref[...], far_ref[...]
        for u in range(2):

            @pl.when(tile == u)
            def _():
                for quarter in range(2):
                    to, at = quarter * LANES, (quarter * 2 + u) * LANES
                    emit[:rows, to : to + LANES] = own_emit[:, at : at + LANES]
                    emit[rows:, to : to + LANES] = far_emit[:, at : at + LANES]

    def body(outs):
        for half, left_ref in enumerate((x_ref, kept_ref)):
            left = left_ref[pl.ds(here * (2 * depth), 2 * depth), :]
            dp = matmul(draw_ref[pl.ds((half * 2 + here) * (2 * lines), 2 * lines), :], emit[...]).astype(BF16)
            for quarter, out in enumerate(outs):
                dw = matmul(left, right[:, quarter * chunk : (quarter + 1) * chunk]).astype(BF16)
                for side in range(2):
                    to = (half ^ order_ref[0]) * 2 + (side ^ order_ref[1])
                    out[to, :depth, :] = dw[side * depth : (side + 1) * depth]
                    for g in range(4):
                        at = side * lines + g * group
                        out[to, depth : depth + group, g * LANES : (g + 1) * LANES] = dp[
                            at : at + group, quarter * LANES : (quarter + 1) * LANES
                        ]

    pl.when(tile == 0)(lambda: body((first_a, first_b)))
    pl.when((tile == 1) & (step == 0))(lambda: body((second_here.at[0], second_here.at[1])))
    pl.when((tile == 1) & (step == 1))(lambda: body((second_there.at[0], second_there.at[1])))


def block_grads(order, x_turned, kept_turned, draw_turned, own, far, emit_own, emit_far, b):
    rows = own.shape[0]
    chunk = 4 * LANES
    depth, lines = x_turned.shape[0] // 4, draw_turned.shape[0] // 8
    high = depth + lines // 4
    emit = pl.BlockSpec((rows, 4 * LANES), lambda u, n, o: (0, b))
    slab = pl.BlockSpec((rows, 2 * chunk), lambda u, n, o: (0, u))
    left = pl.BlockSpec(memory_space=pltpu.VMEM)
    first = pl.BlockSpec((4, high, chunk), lambda u, n, o: (jnp.where(u == 0, n, 1), 0, 0))
    second = pl.BlockSpec((2, 4, high, chunk), lambda u, n, o: (0, 0, 0, 0))
    return pl.pallas_call(
        block_kernel,
        grid_spec=pltpu.PrefetchScalarGridSpec(
            num_scalar_prefetch=1,
            grid=(2, 2),
            in_specs=[left, left, left, slab, slab, emit, emit],
            out_specs=[first, first, second, second],
            scratch_shapes=[pltpu.VMEM((2 * rows, 2 * chunk), BF16), pltpu.VMEM((2 * rows, 2 * LANES), BF16)],
        ),
        out_shape=[jax.ShapeDtypeStruct((8, high, chunk), BF16)] * 2
        + [jax.ShapeDtypeStruct((2, 4, high, chunk), BF16)] * 2,
        compiler_params=pltpu.CompilerParams(vmem_limit_bytes=54 * 2**20, dimension_semantics=("arbitrary",) * 2),
        cost_estimate=LIGHT,
        name="weight_gradients",
    )(order, x_turned, kept_turned, draw_turned, own, far, emit_own, emit_far)


def layer_kernel(col_ref, x_ref, *refs):
    hid_refs, out_ref = refs[:4], refs[4]
    model = x_ref.shape[1]
    mask = pl.program_id(0) ^ col_ref[0]
    x = x_ref[...].astype(F32)

    def body(hid_ref):
        for d in range(2):
            out_ref[:, d, :] = (x + hid_ref[:, d * model : (d + 1) * model].astype(F32)).astype(BF16)

    for n in range(4):
        pl.when(mask == n)(functools.partial(body, hid_refs[n]))


def layer_sum(col, x, hiddens):
    rows, wide = hiddens[0].shape
    model = x.shape[1]
    return pl.pallas_call(
        layer_kernel,
        grid_spec=pltpu.PrefetchScalarGridSpec(
            num_scalar_prefetch=1,
            grid=(4,),
            in_specs=[pl.BlockSpec((rows, model), lambda n, c: (n, 0))] + [whole((rows, wide))] * 4,
            out_specs=pl.BlockSpec((rows, 2, model), lambda n, c: (n, 0, 0)),
        ),
        out_shape=jax.ShapeDtypeStruct((x.shape[0], 2, model), BF16),
        compiler_params=pltpu.CompilerParams(vmem_limit_bytes=16 * 2**20),
        cost_estimate=LIGHT,
        name="layer_sum",
    )(col.reshape(1).astype(jnp.int32), x, *hiddens)


def turn_rows_kernel(own_ref, met_ref, out_ref):
    rows = own_ref.shape[0]
    out_ref[:, :rows] = jnp.swapaxes(own_ref[...], 0, 1)
    out_ref[:, rows:] = jnp.swapaxes(met_ref[...], 0, 1)


def turn_rows(own, met):
    rows, wide = own.shape
    return pl.pallas_call(
        turn_rows_kernel,
        grid=(2,),
        out_shape=jax.ShapeDtypeStruct((wide, 2 * rows), BF16),
        in_specs=[pl.BlockSpec((rows, wide // 2), lambda n: (0, n))] * 2,
        out_specs=pl.BlockSpec((wide // 2, 2 * rows), lambda n: (n, 0)),
        compiler_params=pltpu.CompilerParams(vmem_limit_bytes=16 * 2**20),
        cost_estimate=LIGHT,
        name="turn_rows",
    )(own, met)


def turn_kernel(*refs):
    w_refs, p_refs, wt_refs, pt_refs = (refs[n * PARTS : (n + 1) * PARTS] for n in range(4))
    for source, target in zip(w_refs, wt_refs):
        target[...] = jnp.swapaxes(source[...], 0, 1)

    @pl.when(pl.program_id(0) == 0)
    def _():
        for source, target in zip(p_refs, pt_refs):
            lines, hidden = source.shape[0], source.shape[1] // 2
            target[:, :lines] = jnp.swapaxes(source[:, :hidden], 0, 1)
            target[:, lines:] = jnp.swapaxes(source[:, hidden:], 0, 1)


def turn(pieces):
    width = pieces[0].shape[1]
    hidden, piece = width // 2, width // 4
    cut = width // 4
    results = pl.pallas_call(
        turn_kernel,
        grid=(4,),
        out_shape=[jax.ShapeDtypeStruct((width, hidden), BF16)] * PARTS
        + [jax.ShapeDtypeStruct((hidden, piece), BF16)] * PARTS,
        in_specs=[pl.BlockSpec((hidden, cut), lambda n: (0, n))] * PARTS
        + [pl.BlockSpec((piece // 2, width), lambda n: (2 * hidden // piece, 0))] * PARTS,
        out_specs=[pl.BlockSpec((cut, hidden), lambda n: (n, 0))] * PARTS
        + [pl.BlockSpec((hidden, piece), lambda n: (0, 0))] * PARTS,
        compiler_params=pltpu.CompilerParams(vmem_limit_bytes=20 * 2**20, dimension_semantics=("arbitrary",)),
        cost_estimate=LIGHT,
        name="turn_pieces",
    )(*pieces, *pieces)
    return results[:PARTS], results[PARTS:]


def assemble_kernel(order_ref, *refs):
    weight_out, proj_out = refs[4:]
    depth = weight_out.shape[1]
    group = refs[0].shape[-2] - depth

    def body(tiles):
        for u, tile_ref in enumerate(tiles):
            value = tile_ref[0, 0].astype(F32)
            lanes = slice(u * LANES, (u + 1) * LANES)
            for q in range(4):
                columns = slice(q * LANES, (q + 1) * LANES)
                weight_out[0, :, q, lanes] = value[:depth, columns]
                proj_out[0, q * group : (q + 1) * group, lanes] = value[depth:, columns]

    far = (pl.program_id(1) // 2) ^ order_ref[1]
    pl.when(far == 0)(lambda: body(refs[:2]))
    pl.when(far == 1)(lambda: body(refs[2:4]))


def assemble(order, own0, own1, far0, far1, depth):
    lines = own0.shape[2]
    group = lines - depth
    cells = 8 * LANES
    piece = pl.BlockSpec((1, 1, lines, 4 * LANES), lambda d, n, o: (d ^ o[0], (n % 2) ^ o[2], 0, 0))
    return pl.pallas_call(
        assemble_kernel,
        grid_spec=pltpu.PrefetchScalarGridSpec(
            num_scalar_prefetch=1,
            grid=(2, 4),
            in_specs=[piece] * 4,
            out_specs=[
                pl.BlockSpec((1, depth, 4, 2 * LANES), lambda d, n, o: (d, 0, 0, n)),
                pl.BlockSpec((1, 4 * group, 2 * LANES), lambda d, n, o: (d, 0, n)),
            ],
        ),
        out_shape=[
            jax.ShapeDtypeStruct((2, depth, 4, cells), F32),
            jax.ShapeDtypeStruct((2, 4 * group, cells), F32),
        ],
        compiler_params=pltpu.CompilerParams(vmem_limit_bytes=16 * 2**20),
        cost_estimate=LIGHT,
        name="assemble_gradients",
    )(order, own0, own1, far0, far1)


def input_grad_kernel(has_sum, *refs):
    slab_refs, w_refs, out_ref = refs[:2], refs[2:6], refs[-1]
    chunk = 4 * LANES
    model = out_ref.shape[1]
    total = refs[6][...] if has_sum else None
    for side in range(2):
        for u in range(2):
            for quarter in range(2):
                at = (u * 2 + quarter) * chunk
                part = lax.dot_general(
                    slab_refs[side][:, at : at + chunk],
                    w_refs[side * 2 + quarter][:model, u * chunk : (u + 1) * chunk],
                    (((1,), (1,)), ((), ())),
                    preferred_element_type=F32,
                )
                total = part if total is None else total + part
    out_ref[...] = total


def add_input_grad(slabs, weights, total):
    rows, half = slabs[0].shape
    model = weights[0].shape[1] // 2
    tile = rows // 2
    operands = [*slabs, *weights] + ([] if total is None else [total])
    lines = lambda n: pl.BlockSpec((tile, n), lambda s: (s, 0))
    return pl.pallas_call(
        functools.partial(input_grad_kernel, total is not None),
        grid=(2,),
        out_shape=jax.ShapeDtypeStruct((rows, model), F32),
        in_specs=[lines(half)] * 2
        + [whole(w.shape) for w in weights]
        + ([] if total is None else [lines(model)]),
        out_specs=lines(model),
        compiler_params=pltpu.CompilerParams(vmem_limit_bytes=24 * 2**20),
        cost_estimate=LIGHT,
        name="input_gradient",
    )(*operands)


def after(values):
    return lax.optimization_barrier(values)


def one_direction(inputs, reset_flags, gate_weight, gate_bias, proj_weight, grad_out):
    row, col = lax.axis_index("rows"), lax.axis_index("cols")
    layer, core = row // 2, row % 2
    direction, pair = layer // 2, layer % 2
    model = inputs.shape[1]
    local = inputs.shape[0] // STEPS
    share = local // 4
    rows = 2 * share
    cells = gate_weight.shape[3]
    piece = cells // PARTS
    width = 4 * piece
    tiles = piece // LANES

    def mask_of(r, near):
        odd = (r // 2) % 2
        return (2 if odd else 1) if near else (1 if odd else 2)

    def over_chips(value, near):
        pairs = [(r * 4 + j, r * 4 + (j ^ mask_of(r, near))) for r in range(8) for j in range(4)]
        return lax.ppermute(value, ("rows", "cols"), pairs)

    def over_rows(value, mask):
        return lax.ppermute(value, "rows", [(r, r ^ mask) for r in range(8)])

    core_swap = functools.partial(over_rows, mask=1)
    pair_swap = functools.partial(over_rows, mask=2)
    half_swap = functools.partial(over_rows, mask=4)
    near_mask = jnp.where(pair == 0, 1, 2)
    block_at = [col, col ^ near_mask, col ^ (3 - near_mask), col ^ 3]
    by_dir = lambda pair_of: jnp.where(direction == 0, pair_of[0], pair_of[1])
    by_other = lambda pair_of: jnp.where(direction == 0, pair_of[1], pair_of[0])
    in_run = lambda value: jnp.where(direction == 0, value, value[::-1])

    order = jnp.stack([direction, core, pair]).astype(jnp.int32)

    def place_of(part):
        return jnp.stack([direction, (core ^ (part // 2)) * 2 + (pair ^ (part % 2))]).astype(jnp.int32)

    places = [place_of(part) for part in range(PARTS)]
    input_piece = lambda part: own_piece(places[part], gate_weight, gate_bias, False)
    recurrent_piece = lambda part: own_piece(places[part], gate_weight, proj_weight, True)

    local_windows = lambda value: lax.dynamic_slice_in_dim(value, col * share, share, 0)
    steps_first = lambda value: jnp.swapaxes(value, 0, 1)
    by_side = lambda k, there: [jnp.where(core == which, k, there) for which in range(2)]

    w_in = {(0, 0): own_piece(places[0], gate_weight, gate_bias, False, memory=60)}
    w_rec = {}
    w_in[1, 0] = over_chips(w_in[0, 0], True)
    w_in[2, 0] = over_chips(w_in[0, 0], False)
    w_rec[0, 0] = recurrent_piece(0)

    keep_grid = local_windows(reset_flags.reshape(local, STEPS)).astype(F32)
    position = lax.broadcasted_iota(jnp.int32, (share, STEPS), 1)
    keep_ahead = jnp.where(position > 0, 1.0 - keep_grid, 0.0)
    next_flags = jnp.concatenate([keep_grid[:, 1:], jnp.zeros((share, 1), F32)], axis=1)
    keep_behind = jnp.where(position < STEPS - 1, 1.0 - next_flags, 0.0)
    own_tokens = share * STEPS
    x_mine = lax.dynamic_slice_in_dim(inputs, col * own_tokens, own_tokens, 0).reshape(share, STEPS, model)
    x_mine = steps_first(x_mine)
    keep_dirs = (steps_first(keep_ahead), steps_first(keep_behind))
    keep_wide = [jnp.broadcast_to(k[..., None], (STEPS, share, LANES)).astype(BF16) for k in keep_dirs]
    xk_here = jnp.concatenate([x_mine, by_dir(keep_wide)], axis=2)
    xk_sent = jnp.concatenate([x_mine, by_other(keep_wide)], axis=2)
    xk_met = half_swap(xk_sent)
    w_in[0, 1] = input_piece(1)
    g_mine = lax.dynamic_slice_in_dim(grad_out, col * own_tokens, own_tokens, 0).reshape(share, STEPS, 2, model)
    g_dirs = (steps_first(g_mine[:, :, 0]), steps_first(g_mine[:, :, 1]))
    w_in, w_rec, xk_here, xk_met, g_dirs, places = after((w_in, w_rec, xk_here, xk_met, g_dirs, places))

    w_rec[1, 0] = over_chips(w_rec[0, 0], True)
    w_in[3, 0] = over_chips(w_in[1, 0], False)
    w_in[2, 1] = pair_swap(w_in[1, 0])
    for b in (1, 2):
        w_in[b, 2] = core_swap(w_in[b, 0])
    w_rec[0, 1], w_in[0, 2], w_in[0, 3] = recurrent_piece(1), input_piece(2), input_piece(3)
    xk = in_run(jnp.concatenate([xk_here, xk_met], axis=1))
    x_run, keep_run = xk[..., :model], xk[..., model:].astype(F32)
    x_flat = x_run.reshape(STEPS * rows, model)
    w_in, w_rec, x_flat, keep_run, g_dirs, places = after((w_in, w_rec, x_flat, keep_run, g_dirs, places))

    gates_of = lambda b: input_gates(x_flat, [w_in[b, part] for part in range(PARTS)])
    turn_of = lambda b: turn([w_rec[b, part] for part in range(PARTS)])
    w_in[1, 1] = over_chips(w_in[0, 1], True)
    w_rec[3, 0] = over_chips(w_rec[1, 0], False)
    w_in[3, 1] = pair_swap(w_in[3, 0])
    w_rec[1, 2], w_in[3, 2] = core_swap(w_rec[1, 0]), core_swap(w_in[3, 0])
    w_rec[0, 2], w_rec[0, 3] = recurrent_piece(2), recurrent_piece(3)
    px, turned = {0: gates_of(0)}, {}
    w_in, w_rec, px, x_flat = after((w_in, w_rec, px, x_flat))

    w_rec[1, 1] = over_chips(w_rec[0, 1], True)
    w_rec[2, 0] = over_chips(w_rec[0, 0], False)
    w_rec[2, 1] = pair_swap(w_rec[1, 0])
    for b in (1, 2, 3):
        w_in[b, 3] = core_swap(w_in[b, 1])
    turned[0] = turn_of(0)
    for b in (1, 2, 3):
        px[b] = gates_of(b)
    w_in, w_rec, px, turned, x_flat = after((w_in, w_rec, px, turned, x_flat))

    last_half = w_rec[3, 0].shape[0] // 2
    last_piece = [pair_swap(w_rec[3, 0][:last_half]), over_chips(w_rec[1, 1][last_half:], False)]
    w_rec[1, 3], w_rec[2, 2] = core_swap(w_rec[1, 1]), core_swap(w_rec[2, 0])
    w_rec[2, 3], w_rec[3, 2] = core_swap(w_rec[2, 1]), core_swap(w_rec[3, 0])
    x_met = core_swap(x_flat)
    turned[1], turned[2] = turn_of(1), turn_of(2)
    w_rec, turned, last_piece, x_met = after((w_rec, turned, last_piece, x_met))

    w_rec[3, 1] = jnp.concatenate(last_piece, axis=0)
    w_rec[3, 3] = core_swap(w_rec[3, 1])
    turned[3] = turn_of(3)
    x_turned = turn_rows(x_flat, x_met)
    g_sent = by_other(g_dirs)
    w_rec, turned, x_turned, g_sent = after((w_rec, turned, x_turned, g_sent))

    g_met = half_swap(g_sent)
    px = [px[b].reshape(STEPS, rows, PARTS * width) for b in range(BLOCKS)]
    pre, cell, emit_own, emit_far, raw, kept, hid = run_forward(
        px, keep_run, [w_rec[b, part] for b in range(BLOCKS) for part in range(PARTS)]
    )

    pre, cell, emit_own, emit_far, raw, kept, hid, g_met = after((pre, cell, emit_own, emit_far, raw, kept, hid, g_met))
    g_run = in_run(jnp.concatenate([by_dir(g_dirs), g_met], axis=1))

    flat = lambda value: value.reshape(STEPS * rows, value.shape[-1])
    hid_time = in_run(hid)
    hid_here, hid_there = hid_time[:, :share], half_swap(hid_time[:, share:])
    emit_met = core_swap(flat(emit_far))
    kept = flat(kept)
    kept_met = core_swap(kept)

    def over_cols(value, mask):
        return lax.ppermute(value, "cols", [(j, j ^ mask) for j in range(4)])

    slabs, draw, bias_sums = run_backward(
        pre,
        cell,
        raw,
        g_run,
        keep_run,
        [w for b in range(BLOCKS) for w in turned[b][0]],
        [p for b in range(BLOCKS) for p in turned[b][1]],
    )
    hid_here, hid_there, kept, kept_met, slabs, draw, bias_sums, emit_own, emit_met = after(
        (hid_here, hid_there, kept, kept_met, slabs, draw, bias_sums, emit_own, emit_met)
    )

    slabs = [[flat(value) for value in block] for block in slabs]
    emit_own, draw = flat(emit_own), flat(draw)
    bias_parts = jnp.sum(bias_sums, axis=0).reshape(BLOCKS, 4, 2, 2 * piece)
    bias_half = bias_parts[:, :, 0] + core_swap(bias_parts[:, :, 1])
    draw_met, far = core_swap(draw), {3: core_swap(slabs[3][1])}
    far[1] = core_swap(after((slabs[1][1], draw_met))[0])
    kept_turned, draw_turned = turn_rows(kept, kept_met), turn_rows(draw, draw_met)

    def grads(b):
        left = (x_turned, kept_turned, draw_turned)
        return block_grads(order, *left, slabs[b][0], far[b], emit_own, emit_met, b)

    def add(first, *others):
        total = first.astype(F32)
        for other in others:
            total = total + other.astype(F32)
        return total.astype(BF16)

    def flip(value):
        return jnp.concatenate([value[1:], value[:1]], axis=0)

    opposite = grads(3)
    far, opposite, kept_turned, draw_turned, slabs, bias_half = after(
        (far, opposite, kept_turned, draw_turned, slabs, bias_half)
    )

    relay_a, relay_b = over_chips(opposite[0], True), over_chips(opposite[1], False)
    met = pair_swap(opposite[3])
    far[2] = core_swap(slabs[2][1])
    bias_met = [over_chips(bias_half[1], True), over_chips(bias_half[2], False)]
    near = grads(1)
    other = grads(2)
    hid_both = jnp.concatenate([by_dir((hid_here, hid_there)), by_other((hid_here, hid_there))], axis=2)
    hid_both = steps_first(hid_both).reshape(own_tokens, 2 * model)
    far, relay_a, relay_b, met, near, other, slabs, bias_met, hid_both = after(
        (far, relay_a, relay_b, met, near, other, slabs, bias_met, hid_both)
    )

    near_a, other_b = over_chips(near[0], True), over_chips(other[1], False)
    other_met = pair_swap(near[3])
    far[0] = core_swap(slabs[0][1])
    bias_met = bias_met + [over_cols(bias_half[3], 3)]
    near_b, other_a = add(near[1], relay_b), add(other[0], relay_a)
    opposite1 = add(opposite[2], flip(met))
    own = grads(0)
    near1, other1, own0, own1 = near[2:], other[2:], own[:2], own[2:]
    near_a, other_b, other_met, opposite1, near_b, other_a, other1, own0, own1, slabs, bias_met = after(
        (near_a, other_b, other_met, opposite1, near_b, other_a, other1, own0, own1, slabs, bias_met)
    )

    near_b, other_a = over_chips(near_b, True), over_chips(other_a, False)
    near_met = pair_swap(other1[1])
    wide = None
    for b in range(BLOCKS):
        wide = add_input_grad(slabs[b], [w_in[b, part] for part in range(PARTS)], wide)
    bias_half = bias_half[0] + bias_met[0] + bias_met[1] + bias_met[2]
    bias_half = jnp.where(pair == 0, bias_half, jnp.concatenate([bias_half[:, piece:], bias_half[:, :piece]], axis=1))
    bias_met = pair_swap(bias_half)
    own0 = [add(own0[0], near_a), add(own0[1], other_b)]
    other_a1, other_b1 = add(other1[0][0], other_met[1]), add(other1[0][1], other_met[0])
    dx = in_run(wide.reshape(STEPS, rows, model))
    dx, dx_sent = dx[:, :share], dx[:, share:].astype(BF16)
    near_b, other_a, near_met, dx, dx_sent, own0, own1, bias_met, other_a1, other_b1 = after(
        (near_b, other_a, near_met, dx, dx_sent, own0, own1, bias_met, other_a1, other_b1)
    )

    relay_a, relay_b = over_chips(opposite1[0], True), over_chips(opposite1[1], False)
    near_a1, near_b1 = add(near1[0][0], near_met[1]), add(near1[0][1], near_met[0])
    near_a1, other_b1 = over_chips(near_a1, True), over_chips(other_b1, False)
    count = own0[0].shape[0] // 2
    sums0_met = pair_swap(jnp.stack([add(own0[0][count:], other_a[count:]), add(own0[1][count:], near_b[count:])]))
    sums0 = [add(own0[0][:count], other_a[:count]), add(own0[1][:count], near_b[:count])]
    bias_half = bias_half + bias_met
    lines, rest = [], bias_half
    for _ in range(3):
        lines.append(lax.reduce_precision(rest, 8, 7))
        rest = rest - lines[-1]
    lines = jnp.concatenate(lines + [jnp.zeros_like(rest)], axis=0).astype(BF16)
    dx_met = half_swap(jnp.concatenate([dx_sent.reshape(own_tokens, model), lines], axis=0))
    near_a1, near_b1, other_a1, other_b1, relay_a, relay_b, sums0, sums0_met, dx, dx_met, own1, bias_half = after(
        (near_a1, near_b1, other_a1, other_b1, relay_a, relay_b, sums0, sums0_met, dx, dx_met, own1, bias_half)
    )

    near_b1, other_a1 = over_chips(add(near_b1, relay_b), True), over_chips(add(other_a1, relay_a), False)
    own_met = pair_swap(own1[1])
    sums0_sent = jnp.stack([add(sums0[n][2:], sums0_met[1 - n][2:]) for n in range(2)])
    there0 = half_swap(sums0_sent)
    here0 = jnp.stack([add(sums0[n][:2], sums0_met[1 - n][:2]) for n in range(2)])
    bias_there = dx_met[own_tokens:].astype(F32).reshape(4, 4, 2 * piece)
    bias_there = bias_there[0] + bias_there[1] + bias_there[2]
    bias_half = jnp.stack([by_dir((bias_half, bias_there)), by_other((bias_half, bias_there))])
    dx_met = dx_met[:own_tokens].reshape(STEPS, share, model)
    dx = dx + dx_met.astype(F32) + g_dirs[0].astype(F32) + g_dirs[1].astype(F32)
    dx = steps_first(dx.astype(BF16)).reshape(own_tokens, model)
    share_width = model // 4
    slice_for = lambda mask: lax.dynamic_slice_in_dim(dx, (col ^ mask) * share_width, share_width, 1)
    outgoing = [jnp.concatenate([hid_both, slice_for(mask)], axis=1) for mask in range(4)]
    incoming = [outgoing[0], None, None, over_cols(outgoing[3], 3)]
    own_a1, own_b1 = add(own1[0][0], near_a1), add(own1[0][1], other_b1)
    near_b1, other_a1, own_met, here0, there0, own_a1, own_b1, incoming[0], incoming[3], outgoing, bias_half = after(
        (near_b1, other_a1, own_met, here0, there0, own_a1, own_b1, incoming[0], incoming[3], outgoing, bias_half)
    )

    parts1 = ((own_a1, own_met[1], other_a1), (own_b1, own_met[0], near_b1))
    there1 = half_swap(jnp.stack([add(*(value[2:] for value in parts)) for parts in parts1]))
    here1 = jnp.stack([add(*(value[:2] for value in parts)) for parts in parts1])

    def two_directions(here, there):
        both = jnp.stack([here, there])
        return both[:, :, 0], both[:, :, 1]

    kept0, sent0 = two_directions(here0, there0)
    met0 = core_swap(sent0)
    incoming[1], incoming[2] = over_cols(outgoing[1], 1), over_cols(outgoing[2], 2)
    block_out = layer_sum(col, inputs, [value[:, : 2 * model] for value in incoming])
    input_grad = jnp.zeros((BLOCKS * own_tokens, share_width), BF16)
    for mask, value in enumerate(incoming):
        input_grad = lax.dynamic_update_slice(input_grad, value[:, 2 * model :], ((col ^ mask) * own_tokens, 0))
    bias_total = jnp.concatenate(by_side(bias_half, core_swap(bias_half)), axis=2)
    here1, there1, kept0, met0, block_out, input_grad, bias_total = after(
        (here1, there1, kept0, met0, block_out, input_grad, bias_total)
    )

    kept1, sent1 = two_directions(here1, there1)
    met1 = core_swap(sent1)
    weight_share, proj_share = assemble(order, kept0, kept1, met0, met1, 2 * model // 8)
    proj_share = jnp.swapaxes(proj_share, 1, 2)
    return (block_out, input_grad, weight_share, bias_total, proj_share)


def solution(mesh):
    placed = (
        P("rows", None),
        P("rows"),
        P(None, None, None, "cols"),
        P(None, None, "cols"),
        P(None, "cols", None),
        P("rows", None, None),
    )
    plan = one_direction if (mesh.shape["rows"], mesh.shape["cols"]) == (8, 4) else shared_cells
    return jax.shard_map(
        plan,
        mesh=mesh,
        in_specs=placed,
        out_specs=(
            P("rows", None, None),
            P("rows", "cols"),
            P(None, "rows", None, "cols"),
            P(None, None, "cols"),
            P(None, "cols", "rows"),
        ),
        check_vma=False,
    )
```

```python
import functools

import jax
import jax.numpy as jnp
from jax import lax
from jax.experimental import pallas as pl
from jax.experimental.pallas import tpu as pltpu
from jax.sharding import PartitionSpec as P

STEPS = 20
BF16 = jnp.bfloat16
F32 = jnp.float32
THIRD = 1.0 / 3.0
LANES = 128
BLOCKS = 4
LIGHT = pl.CostEstimate(flops=1, bytes_accessed=1, transcendentals=0)
PARTS = 4


def soft_clip(amount):
    return 3.0 * jnp.tanh(amount / 3.0)


def clip_slope(amount):
    tangent = jnp.tanh(amount / 3.0)
    return 1.0 - tangent * tangent


def shared_cells(inputs, reset_flags, gate_weight, gate_bias, proj_weight, grad_out):
    tok_rows, model_width = inputs.shape
    windows = tok_rows // STEPS
    cell_cols = gate_weight.shape[3]
    gate_width = 4 * cell_cols
    share_width = model_width // lax.axis_size("cols")
    column = lax.axis_index("cols") * share_width
    weight = gate_weight.reshape(2, 2 * model_width, gate_width)
    w_input = weight[:, :model_width]
    w_recur = weight[:, model_width:]
    bias_row = gate_bias.reshape(2, 1, gate_width)
    sequence = jnp.swapaxes(inputs.reshape(windows, STEPS, model_width), 0, 1)
    x_stack = jnp.stack([sequence, sequence[::-1]], axis=1)
    flag_grid = jnp.swapaxes(reset_flags.reshape(windows, STEPS), 0, 1).astype(jnp.float32)
    position = lax.broadcasted_iota(jnp.int32, (STEPS, windows), 0)
    keep_ahead = jnp.where(position > 0, 1.0 - flag_grid, 0.0)
    next_flags = jnp.concatenate([flag_grid[1:], jnp.zeros((1, windows), jnp.float32)], axis=0)
    keep_behind = jnp.where(position < STEPS - 1, 1.0 - next_flags, 0.0)
    keep_stack = jnp.stack([keep_ahead, keep_behind[::-1]], axis=1)[..., None]
    input_gates = jnp.einsum("sdwh,dhg->sdwg", x_stack, w_input, preferred_element_type=jnp.float32)

    def forward_step(state_pair, pieces):
        hidden, cell_prev = state_pair
        gates_in, keep_step = pieces
        kept_hidden = hidden * keep_step.astype(jnp.bfloat16)
        gate_pre = (
            gates_in
            + jnp.einsum("dwh,dhg->dwg", kept_hidden, w_recur, preferred_element_type=jnp.float32)
            + bias_row
        )
        in_gate = jax.nn.sigmoid(gate_pre[..., :cell_cols])
        forget = jax.nn.sigmoid(gate_pre[..., cell_cols : 2 * cell_cols])
        update = jnp.tanh(gate_pre[..., 2 * cell_cols : 3 * cell_cols])
        out_gate = jax.nn.sigmoid(gate_pre[..., 3 * cell_cols :])
        kept_cell = cell_prev * keep_step
        cell_new = soft_clip(forget * kept_cell + in_gate * update)
        cell_output = (out_gate * jnp.tanh(cell_new)).astype(jnp.bfloat16)
        partial_raw = jnp.einsum(
            "dwc,dch->dwh", cell_output, proj_weight, preferred_element_type=jnp.float32
        )
        proj_raw = lax.psum(partial_raw, "cols")
        new_hidden = soft_clip(proj_raw).astype(jnp.bfloat16)
        return (
            (new_hidden, cell_new),
            (kept_hidden, gate_pre, kept_cell, cell_new, cell_output, proj_raw, new_hidden),
        )

    init_state = (
        jnp.zeros((2, windows, model_width), jnp.bfloat16),
        jnp.zeros((2, windows, cell_cols), jnp.float32),
    )
    _, fwd_saved = lax.scan(forward_step, init_state, (input_gates, keep_stack))
    kept_all, pre_all, kept_cells, cell_states, cell_outputs, proj_raws, hiddens = fwd_saved
    ahead_hidden = hiddens[:, 0]
    behind_hidden = hiddens[::-1, 1]
    both_outputs = jnp.stack([ahead_hidden, behind_hidden], axis=2).astype(jnp.float32) + sequence[
        :, :, None, :
    ].astype(jnp.float32)
    block_out = (
        jnp.swapaxes(both_outputs, 0, 1).reshape(tok_rows, 2, model_width).astype(jnp.bfloat16)
    )
    out_grid = jnp.transpose(grad_out.reshape(windows, STEPS, 2, model_width), (1, 2, 0, 3))
    grad_stack = jnp.stack([out_grid[:, 0], out_grid[::-1, 1]], axis=1)

    def backward_step(state_pair, pieces):
        recur_part, cell_grad = state_pair
        gate_pre, kept_cell, cell_new, cell_output, proj_raw, grad_step, keep_step = pieces
        recur_sum = lax.psum(recur_part, "cols")
        hidden_grad = grad_step.astype(jnp.float32) + recur_sum
        raw_grad = (hidden_grad * clip_slope(proj_raw)).astype(jnp.bfloat16)
        emit_grad = jnp.einsum(
            "dwh,dch->dwc", raw_grad, proj_weight, preferred_element_type=jnp.float32
        )
        in_gate = jax.nn.sigmoid(gate_pre[..., :cell_cols])
        forget = jax.nn.sigmoid(gate_pre[..., cell_cols : 2 * cell_cols])
        update = jnp.tanh(gate_pre[..., 2 * cell_cols : 3 * cell_cols])
        out_gate = jax.nn.sigmoid(gate_pre[..., 3 * cell_cols :])
        tanh_cell = jnp.tanh(cell_new)
        cell_total = cell_grad + emit_grad * out_gate * (1.0 - tanh_cell * tanh_cell)
        cell_third = cell_new / 3.0
        cell_raw_grad = cell_total * (1.0 - cell_third * cell_third)
        pre_grad = jnp.concatenate(
            [
                cell_raw_grad * update * in_gate * (1.0 - in_gate),
                cell_raw_grad * kept_cell * forget * (1.0 - forget),
                cell_raw_grad * in_gate * (1.0 - update * update),
                emit_grad * tanh_cell * out_gate * (1.0 - out_gate),
            ],
            axis=-1,
        ).astype(jnp.bfloat16)
        recur_next = (
            jnp.einsum("dwg,dhg->dwh", pre_grad, w_recur, preferred_element_type=jnp.float32)
            * keep_step
        )
        cell_next = cell_raw_grad * forget * keep_step
        return ((recur_next, cell_next), (pre_grad, raw_grad))

    zero_state = (
        jnp.zeros((2, windows, model_width), jnp.float32),
        jnp.zeros((2, windows, cell_cols), jnp.float32),
    )
    _, back_saved = lax.scan(
        backward_step,
        zero_state,
        (pre_all, kept_cells, cell_states, cell_outputs, proj_raws, grad_stack, keep_stack),
        reverse=True,
    )
    pre_grads, raw_grads = back_saved
    input_part = jnp.einsum(
        "sdwg,dhg->sdwh", pre_grads, w_input, preferred_element_type=jnp.float32
    )
    input_sum = jnp.swapaxes(input_part[:, 0] + input_part[::-1, 1], 0, 1).reshape(
        tok_rows, model_width
    )
    input_share = lax.psum_scatter(
        input_sum.astype(jnp.bfloat16), "cols", scatter_dimension=1, tiled=True
    ).astype(jnp.float32)
    residual_grad = grad_out[:, 0].astype(jnp.float32) + grad_out[:, 1].astype(jnp.float32)
    input_grad = (
        input_share + lax.dynamic_slice_in_dim(residual_grad, column, share_width, 1)
    ).astype(jnp.bfloat16)
    input_weight_grad = jnp.einsum(
        "sdwh,sdwg->dhg", x_stack, pre_grads, preferred_element_type=jnp.float32
    )
    recur_weight_grad = jnp.einsum(
        "sdwh,sdwg->dhg", kept_all, pre_grads, preferred_element_type=jnp.float32
    )
    weight_grad = jnp.concatenate([input_weight_grad, recur_weight_grad], axis=1).reshape(
        2, 2 * model_width, 4, cell_cols
    )
    proj_grad = jnp.einsum(
        "sdwc,sdwh->dch", cell_outputs, raw_grads, preferred_element_type=jnp.float32
    )
    bias_grad = jnp.sum(pre_grads, axis=(0, 2), dtype=jnp.float32).reshape(2, 4, cell_cols)
    weight_share, proj_share = (
        lax.psum_scatter(
            weight_grad.astype(jnp.bfloat16), "rows", scatter_dimension=1, tiled=True
        ).astype(jnp.float32),
        lax.psum_scatter(
            proj_grad.astype(jnp.bfloat16), "rows", scatter_dimension=2, tiled=True
        ).astype(jnp.float32),
    )
    bias_total = lax.psum(bias_grad, "rows")
    return (block_out, input_grad, weight_share, bias_total, proj_share)


def sigmoid(amount):
    return 0.5 * jnp.tanh(0.5 * amount) + 0.5


def whole(shape):
    return pl.BlockSpec(shape, lambda *_: (0,) * len(shape), pipeline_mode=pl.Buffered(1))


def matmul(a, b):
    return jnp.dot(a, b, preferred_element_type=F32)


def own_piece_kernel(order_ref, w_ref, extra_ref, out_ref):
    step = pl.program_id(0)
    lines = w_ref.shape[1]
    model, width = extra_ref.shape[-1] if extra_ref.shape[1] > 4 else None, out_ref.shape[1]
    for u in range(2):
        for q in range(4):
            to = (u * 4 + q) * LANES
            out_ref[pl.ds(step * lines, lines), to : to + LANES] = w_ref[0, :, q, u * LANES : (u + 1) * LANES]
    base = width // 2

    @pl.when(step == 0)
    def _():
        if model is None:
            rest = jnp.concatenate(
                [extra_ref[0, q : q + 1, u * LANES : (u + 1) * LANES] for u in range(2) for q in range(4)], axis=1
            )
            parts = []
            for _ in range(3):
                parts.append(rest.astype(BF16).astype(F32))
                rest = rest - parts[-1]
            parts.append(jnp.zeros((13, width), F32))
            out_ref[base:, :] = jnp.concatenate(parts, axis=0).astype(BF16)
        else:
            half = extra_ref.shape[1] // 2
            out_ref[base:, :model] = extra_ref[0, :half, :]
            out_ref[base:, model:] = extra_ref[0, half:, :]


def own_piece(place, gate_weight, extra, recurrent, memory=16):
    model, piece = gate_weight.shape[1] // 2, gate_weight.shape[3] // PARTS
    cut = model // 4
    first = 4 if recurrent else 0
    if recurrent:
        extra_spec = pl.BlockSpec((1, piece, model), lambda n, p: (p[0], p[1], 0))
    else:
        extra_spec = pl.BlockSpec((1, 4, piece), lambda n, p: (p[0], 0, p[1]))
    lines = model + (piece // 2 if recurrent else 16)
    return pl.pallas_call(
        own_piece_kernel,
        grid_spec=pltpu.PrefetchScalarGridSpec(
            num_scalar_prefetch=1,
            grid=(4,),
            in_specs=[pl.BlockSpec((1, cut, 4, piece), lambda n, p: (p[0], n + first, 0, p[1])), extra_spec],
            out_specs=pl.BlockSpec((lines, 4 * piece), lambda n, p: (0, 0)),
        ),
        out_shape=jax.ShapeDtypeStruct((lines, 4 * piece), BF16),
        compiler_params=pltpu.CompilerParams(vmem_limit_bytes=memory * 2**20, dimension_semantics=("arbitrary",)),
        cost_estimate=LIGHT,
        name="own_piece",
    )(place, gate_weight, extra)


def input_kernel(x_ref, w0, w1, w2, w3, out_ref):
    model, width = x_ref.shape[1], w0.shape[1]
    for n, w_ref in enumerate((w0, w1, w2, w3)):
        bias = jnp.sum(w_ref[model:, :].astype(F32), axis=0, keepdims=True)
        out_ref[:, n * width : (n + 1) * width] = (matmul(x_ref[...], w_ref[:model, :]) + bias).astype(BF16)


def input_gates(x, weights):
    rows, model = x.shape
    width = weights[0].shape[1]
    tile = rows // 2
    return pl.pallas_call(
        input_kernel,
        grid=(2,),
        out_shape=jax.ShapeDtypeStruct((rows, PARTS * width), BF16),
        in_specs=[pl.BlockSpec((tile, model), lambda n: (n, 0))] + [whole(w.shape) for w in weights],
        out_specs=pl.BlockSpec((tile, PARTS * width), lambda n: (n, 0)),
        compiler_params=pltpu.CompilerParams(vmem_limit_bytes=20 * 2**20),
        cost_estimate=LIGHT,
        name="input_gates",
    )(x, *weights)


def forward_kernel(*refs):
    px_refs, keep_ref = refs[:BLOCKS], refs[BLOCKS]
    w_refs = refs[BLOCKS + 1 : BLOCKS + 1 + BLOCKS * PARTS]
    pre_out, cell_out, emit_own, emit_far, raw_out, kept_out, hid_out, c_scr, h_scr = refs[BLOCKS + 1 + BLOCKS * PARTS :]
    step = pl.program_id(0)
    width = w_refs[0].shape[1]
    hidden = width // 2
    piece = width // 4
    cells = piece * PARTS
    tiles = piece // LANES
    half = cells // 2
    rows = keep_ref.shape[1]

    @pl.when(step == 0)
    def _():
        c_scr[...] = jnp.zeros_like(c_scr)
        h_scr[...] = jnp.zeros_like(h_scr)

    keep = keep_ref[0][:, :1]
    kept = (h_scr[...] * keep).astype(BF16)
    kept_out[0] = kept
    raw = jnp.zeros((rows, hidden), F32)
    def products(b):
        parts, proj = [], []
        for s in range(PARTS):
            w_ref = w_refs[b * PARTS + s]
            pre = px_refs[b][0, :, s * width : (s + 1) * width].astype(F32) + matmul(kept, w_ref[:hidden, :])
            at = b * 4 * cells + s * width
            pre_out[0, :, at : at + width] = pre.astype(BF16)
            parts.append(pre)
            proj += [w_ref[hidden:, :hidden], w_ref[hidden:, hidden:]]
        return parts, proj

    following = products(0)
    for b in range(BLOCKS):
        parts, proj = following
        if b + 1 < BLOCKS:
            following = products(b + 1)
        gates = [
            jnp.concatenate(
                [part[:, (u * 4 + q) * LANES : (u * 4 + q + 1) * LANES] for part in parts for u in range(tiles)], axis=1
            )
            for q in range(4)
        ]
        i, f, u, o = sigmoid(gates[0]), sigmoid(gates[1]), jnp.tanh(gates[2]), sigmoid(gates[3])
        at = b * cells
        kept_cell = c_scr[:, at : at + cells] * keep
        cell = 3.0 * jnp.tanh((f * kept_cell + i * u) * THIRD)
        emit = (o * jnp.tanh(cell)).astype(BF16)
        c_scr[:, at : at + cells] = cell
        cell_out[0, :, at : at + cells] = cell
        emit_own[0, :, b * half : (b + 1) * half] = emit[:, :half]
        emit_far[0, :, b * half : (b + 1) * half] = emit[:, half:]
        raw = raw + matmul(emit, jnp.concatenate(proj, axis=0))
    raw_out[0] = raw
    hid = 3.0 * jnp.tanh(raw * THIRD)
    h_scr[...] = hid.astype(BF16).astype(F32)
    hid_out[0] = hid.astype(BF16)


def run_forward(px, keep, weights):
    steps, rows, wide = px[0].shape
    hidden = weights[0].shape[1] // 2
    total = BLOCKS * wide // 4
    block = lambda n: pl.BlockSpec((1, rows, n), lambda t: (t, 0, 0))
    sizes = (4 * total, total, total // 2, total // 2, hidden, hidden, hidden)
    kinds = (BF16, F32, BF16, BF16, F32, BF16, BF16)
    return pl.pallas_call(
        forward_kernel,
        grid=(steps,),
        out_shape=tuple(jax.ShapeDtypeStruct((steps, rows, n), kind) for n, kind in zip(sizes, kinds)),
        in_specs=[block(wide)] * BLOCKS + [block(LANES)] + [whole(w.shape) for w in weights],
        out_specs=tuple(block(n) for n in sizes),
        scratch_shapes=[pltpu.VMEM((rows, total), F32), pltpu.VMEM((rows, hidden), F32)],
        compiler_params=pltpu.CompilerParams(vmem_limit_bytes=48 * 2**20, dimension_semantics=("arbitrary",)),
        cost_estimate=pl.CostEstimate(
            flops=2 * steps * rows * hidden * 5 * total * 8,
            bytes_accessed=steps * rows * total * 24 + 10 * total * hidden,
            transcendentals=steps * rows * total * 6,
        ),
        name="forward_chain",
    )(*px, keep, *weights)


def backward_kernel(*refs):
    pre_ref, cell_ref, before_ref, raw_ref, grad_ref, keep_ref = refs[:6]
    wt_refs, pt_refs = refs[6 : 6 + BLOCKS * PARTS], refs[6 + BLOCKS * PARTS : 6 + 2 * BLOCKS * PARTS]
    outs = refs[6 + 2 * BLOCKS * PARTS :]
    slabs, draw_out, bias_out, dc_scr, dk_scr = outs[: 2 * BLOCKS], *outs[2 * BLOCKS :]
    step = pl.program_id(0)
    hidden, piece = pt_refs[0].shape
    cells = piece * PARTS
    tiles = piece // LANES
    width = 4 * piece
    chunk = 4 * LANES
    rows = keep_ref.shape[1]

    @pl.when(step == 0)
    def _():
        dc_scr[...] = jnp.zeros_like(dc_scr)
        dk_scr[...] = jnp.zeros_like(dk_scr)
        bias_out[...] = jnp.zeros_like(bias_out)

    keep = keep_ref[0][:, :1]
    tangent = jnp.tanh(raw_ref[0] * THIRD)
    draw = ((grad_ref[0].astype(F32) + dk_scr[...]) * (1.0 - tangent * tangent)).astype(BF16)
    draw_out[0] = draw
    dk = jnp.zeros((rows, hidden), F32)
    emitted = lambda b: matmul(draw, jnp.concatenate([pt_refs[b * PARTS + s][...] for s in range(PARTS)], axis=1))
    following = emitted(0)
    for b in range(BLOCKS):
        at = b * cells
        demit = following
        if b + 1 < BLOCKS:
            following = emitted(b + 1)
        gates = [
            jnp.concatenate(
                [
                    pre_ref[0, :, 4 * at + s * width + (u * 4 + q) * LANES : 4 * at + s * width + (u * 4 + q + 1) * LANES]
                    for s in range(PARTS)
                    for u in range(tiles)
                ],
                axis=1,
            ).astype(F32)
            for q in range(4)
        ]
        i, f, u, o = sigmoid(gates[0]), sigmoid(gates[1]), jnp.tanh(gates[2]), sigmoid(gates[3])
        cell = cell_ref[0, :, at : at + cells]
        kept_cell = before_ref[0, :, at : at + cells] * keep
        tanh_cell = jnp.tanh(cell)
        third = cell * THIRD
        dcell = (dc_scr[:, at : at + cells] + demit * o * (1.0 - tanh_cell * tanh_cell)) * (1.0 - third * third)
        dgates = (
            dcell * u * i * (1.0 - i),
            dcell * kept_cell * f * (1.0 - f),
            dcell * i * (1.0 - u * u),
            demit * tanh_cell * o * (1.0 - o),
        )
        dc_scr[:, at : at + cells] = dcell * f * keep
        for q in range(4):
            folded = dgates[q][:8]
            for r in range(8, rows, 8):
                folded = folded + dgates[q][r : r + 8]
            bias_out[:, (b * 4 + q) * cells : (b * 4 + q + 1) * cells] += folded
        dgates = [dgate.astype(BF16) for dgate in dgates]
        for s in range(PARTS):
            part = jnp.concatenate(
                [
                    dgates[q][:, s * piece + u * LANES : s * piece + (u + 1) * LANES]
                    for u in range(tiles)
                    for q in range(4)
                ],
                axis=1,
            )
            side, quarter = s // 2, s % 2
            for u in range(tiles):
                to = (u * 2 + quarter) * chunk
                slabs[b * 2 + side][0, :, to : to + chunk] = part[:, u * chunk : (u + 1) * chunk]
            dk = dk + matmul(part, wt_refs[b * PARTS + s][...])
    dk_scr[...] = dk * keep


def run_backward(pre, cell, raw, grad, keep, weights, projs):
    steps, rows, gates = pre.shape
    total = gates // 4
    hidden, piece = projs[0].shape
    half = PARTS * piece * 2
    block = lambda n: pl.BlockSpec((1, rows, n), lambda s: (steps - 1 - s, 0, 0))
    before = pl.BlockSpec((1, rows, total), lambda s: (jnp.maximum(steps - 2 - s, 0), 0, 0))
    shape = lambda n: jax.ShapeDtypeStruct((steps, rows, n), BF16)
    out = pl.pallas_call(
        backward_kernel,
        grid=(steps,),
        out_shape=tuple([shape(half)] * (2 * BLOCKS) + [shape(hidden), jax.ShapeDtypeStruct((8, gates), F32)]),
        in_specs=[block(gates), block(total), before, block(hidden), block(hidden), block(LANES)]
        + [whole(w.shape) for w in [*weights, *projs]],
        out_specs=tuple([block(half)] * (2 * BLOCKS) + [block(hidden), pl.BlockSpec((8, gates), lambda s: (0, 0))]),
        scratch_shapes=[pltpu.VMEM((rows, total), F32), pltpu.VMEM((rows, hidden), F32)],
        compiler_params=pltpu.CompilerParams(vmem_limit_bytes=48 * 2**20, dimension_semantics=("arbitrary",)),
        cost_estimate=pl.CostEstimate(
            flops=2 * steps * rows * hidden * 5 * total * 8,
            bytes_accessed=steps * rows * total * 24 + 10 * total * hidden,
            transcendentals=steps * rows * total * 6,
        ),
        name="backward_chain",
    )(pre, cell, cell, raw, grad, keep, *weights, *projs)
    return [out[b * 2 : b * 2 + 2] for b in range(BLOCKS)], out[2 * BLOCKS], out[2 * BLOCKS + 1]


def block_kernel(order_ref, x_ref, kept_ref, draw_ref, own_ref, far_ref, own_emit, far_emit, *refs):
    first_a, first_b, second_here, second_there, right, emit = refs
    rows = own_ref.shape[0]
    tile, step = pl.program_id(0), pl.program_id(1)
    depth, lines = x_ref.shape[0] // 4, draw_ref.shape[0] // 8
    group = lines // 4
    chunk = 4 * LANES
    here = step ^ order_ref[2]

    @pl.when(step == 0)
    def _():
        right[:rows, :], right[rows:, :] = own_ref[...], far_ref[...]
        for u in range(2):

            @pl.when(tile == u)
            def _():
                for quarter in range(2):
                    to, at = quarter * LANES, (quarter * 2 + u) * LANES
                    emit[:rows, to : to + LANES] = own_emit[:, at : at + LANES]
                    emit[rows:, to : to + LANES] = far_emit[:, at : at + LANES]

    def body(outs):
        for half, left_ref in enumerate((x_ref, kept_ref)):
            left = left_ref[pl.ds(here * (2 * depth), 2 * depth), :]
            dp = matmul(draw_ref[pl.ds((half * 2 + here) * (2 * lines), 2 * lines), :], emit[...]).astype(BF16)
            for quarter, out in enumerate(outs):
                dw = matmul(left, right[:, quarter * chunk : (quarter + 1) * chunk]).astype(BF16)
                for side in range(2):
                    to = (half ^ order_ref[0]) * 2 + (side ^ order_ref[1])
                    out[to, :depth, :] = dw[side * depth : (side + 1) * depth]
                    for g in range(4):
                        at = side * lines + g * group
                        out[to, depth : depth + group, g * LANES : (g + 1) * LANES] = dp[
                            at : at + group, quarter * LANES : (quarter + 1) * LANES
                        ]

    pl.when(tile == 0)(lambda: body((first_a, first_b)))
    pl.when((tile == 1) & (step == 0))(lambda: body((second_here.at[0], second_here.at[1])))
    pl.when((tile == 1) & (step == 1))(lambda: body((second_there.at[0], second_there.at[1])))


def block_grads(order, x_turned, kept_turned, draw_turned, own, far, emit_own, emit_far, b):
    rows = own.shape[0]
    chunk = 4 * LANES
    depth, lines = x_turned.shape[0] // 4, draw_turned.shape[0] // 8
    high = depth + lines // 4
    emit = pl.BlockSpec((rows, 4 * LANES), lambda u, n, o: (0, b))
    slab = pl.BlockSpec((rows, 2 * chunk), lambda u, n, o: (0, u))
    left = pl.BlockSpec(memory_space=pltpu.VMEM)
    first = pl.BlockSpec((4, high, chunk), lambda u, n, o: (jnp.where(u == 0, n, 1), 0, 0))
    second = pl.BlockSpec((2, 4, high, chunk), lambda u, n, o: (0, 0, 0, 0))
    return pl.pallas_call(
        block_kernel,
        grid_spec=pltpu.PrefetchScalarGridSpec(
            num_scalar_prefetch=1,
            grid=(2, 2),
            in_specs=[left, left, left, slab, slab, emit, emit],
            out_specs=[first, first, second, second],
            scratch_shapes=[pltpu.VMEM((2 * rows, 2 * chunk), BF16), pltpu.VMEM((2 * rows, 2 * LANES), BF16)],
        ),
        out_shape=[jax.ShapeDtypeStruct((8, high, chunk), BF16)] * 2
        + [jax.ShapeDtypeStruct((2, 4, high, chunk), BF16)] * 2,
        compiler_params=pltpu.CompilerParams(vmem_limit_bytes=54 * 2**20, dimension_semantics=("arbitrary",) * 2),
        cost_estimate=LIGHT,
        name="weight_gradients",
    )(order, x_turned, kept_turned, draw_turned, own, far, emit_own, emit_far)


def layer_kernel(col_ref, x_ref, *refs):
    hid_refs, out_ref = refs[:4], refs[4]
    model = x_ref.shape[1]
    mask = pl.program_id(0) ^ col_ref[0]
    x = x_ref[...].astype(F32)

    def body(hid_ref):
        for d in range(2):
            out_ref[:, d, :] = (x + hid_ref[:, d * model : (d + 1) * model].astype(F32)).astype(BF16)

    for n in range(4):
        pl.when(mask == n)(functools.partial(body, hid_refs[n]))


def layer_sum(col, x, hiddens):
    rows, wide = hiddens[0].shape
    model = x.shape[1]
    return pl.pallas_call(
        layer_kernel,
        grid_spec=pltpu.PrefetchScalarGridSpec(
            num_scalar_prefetch=1,
            grid=(4,),
            in_specs=[pl.BlockSpec((rows, model), lambda n, c: (n, 0))] + [whole((rows, wide))] * 4,
            out_specs=pl.BlockSpec((rows, 2, model), lambda n, c: (n, 0, 0)),
        ),
        out_shape=jax.ShapeDtypeStruct((x.shape[0], 2, model), BF16),
        compiler_params=pltpu.CompilerParams(vmem_limit_bytes=16 * 2**20),
        cost_estimate=LIGHT,
        name="layer_sum",
    )(col.reshape(1).astype(jnp.int32), x, *hiddens)


def turn_rows_kernel(own_ref, met_ref, out_ref):
    rows = own_ref.shape[0]
    out_ref[:, :rows] = jnp.swapaxes(own_ref[...], 0, 1)
    out_ref[:, rows:] = jnp.swapaxes(met_ref[...], 0, 1)


def turn_rows(own, met):
    rows, wide = own.shape
    return pl.pallas_call(
        turn_rows_kernel,
        grid=(2,),
        out_shape=jax.ShapeDtypeStruct((wide, 2 * rows), BF16),
        in_specs=[pl.BlockSpec((rows, wide // 2), lambda n: (0, n))] * 2,
        out_specs=pl.BlockSpec((wide // 2, 2 * rows), lambda n: (n, 0)),
        compiler_params=pltpu.CompilerParams(vmem_limit_bytes=16 * 2**20),
        cost_estimate=LIGHT,
        name="turn_rows",
    )(own, met)


def turn_kernel(*refs):
    w_refs, p_refs, wt_refs, pt_refs = (refs[n * PARTS : (n + 1) * PARTS] for n in range(4))
    for source, target in zip(w_refs, wt_refs):
        target[...] = jnp.swapaxes(source[...], 0, 1)

    @pl.when(pl.program_id(0) == 0)
    def _():
        for source, target in zip(p_refs, pt_refs):
            lines, hidden = source.shape[0], source.shape[1] // 2
            target[:, :lines] = jnp.swapaxes(source[:, :hidden], 0, 1)
            target[:, lines:] = jnp.swapaxes(source[:, hidden:], 0, 1)


def turn(pieces):
    width = pieces[0].shape[1]
    hidden, piece = width // 2, width // 4
    cut = width // 4
    results = pl.pallas_call(
        turn_kernel,
        grid=(4,),
        out_shape=[jax.ShapeDtypeStruct((width, hidden), BF16)] * PARTS
        + [jax.ShapeDtypeStruct((hidden, piece), BF16)] * PARTS,
        in_specs=[pl.BlockSpec((hidden, cut), lambda n: (0, n))] * PARTS
        + [pl.BlockSpec((piece // 2, width), lambda n: (2 * hidden // piece, 0))] * PARTS,
        out_specs=[pl.BlockSpec((cut, hidden), lambda n: (n, 0))] * PARTS
        + [pl.BlockSpec((hidden, piece), lambda n: (0, 0))] * PARTS,
        compiler_params=pltpu.CompilerParams(vmem_limit_bytes=20 * 2**20, dimension_semantics=("arbitrary",)),
        cost_estimate=LIGHT,
        name="turn_pieces",
    )(*pieces, *pieces)
    return results[:PARTS], results[PARTS:]


def assemble_kernel(order_ref, *refs):
    weight_out, proj_out = refs[4:]
    depth = weight_out.shape[1]
    group = refs[0].shape[-2] - depth

    def body(tiles):
        for u, tile_ref in enumerate(tiles):
            value = tile_ref[0, 0].astype(F32)
            lanes = slice(u * LANES, (u + 1) * LANES)
            for q in range(4):
                columns = slice(q * LANES, (q + 1) * LANES)
                weight_out[0, :, q, lanes] = value[:depth, columns]
                proj_out[0, q * group : (q + 1) * group, lanes] = value[depth:, columns]

    far = (pl.program_id(1) // 2) ^ order_ref[1]
    pl.when(far == 0)(lambda: body(refs[:2]))
    pl.when(far == 1)(lambda: body(refs[2:4]))


def assemble(order, own0, own1, far0, far1, depth):
    lines = own0.shape[2]
    group = lines - depth
    cells = 8 * LANES
    piece = pl.BlockSpec((1, 1, lines, 4 * LANES), lambda d, n, o: (d ^ o[0], (n % 2) ^ o[2], 0, 0))
    return pl.pallas_call(
        assemble_kernel,
        grid_spec=pltpu.PrefetchScalarGridSpec(
            num_scalar_prefetch=1,
            grid=(2, 4),
            in_specs=[piece] * 4,
            out_specs=[
                pl.BlockSpec((1, depth, 4, 2 * LANES), lambda d, n, o: (d, 0, 0, n)),
                pl.BlockSpec((1, 4 * group, 2 * LANES), lambda d, n, o: (d, 0, n)),
            ],
        ),
        out_shape=[
            jax.ShapeDtypeStruct((2, depth, 4, cells), F32),
            jax.ShapeDtypeStruct((2, 4 * group, cells), F32),
        ],
        compiler_params=pltpu.CompilerParams(vmem_limit_bytes=16 * 2**20),
        cost_estimate=LIGHT,
        name="assemble_gradients",
    )(order, own0, own1, far0, far1)


def input_grad_kernel(has_sum, *refs):
    slab_refs, w_refs, out_ref = refs[:2], refs[2:6], refs[-1]
    chunk = 4 * LANES
    model = out_ref.shape[1]
    total = refs[6][...] if has_sum else None
    for side in range(2):
        for u in range(2):
            for quarter in range(2):
                at = (u * 2 + quarter) * chunk
                part = lax.dot_general(
                    slab_refs[side][:, at : at + chunk],
                    w_refs[side * 2 + quarter][:model, u * chunk : (u + 1) * chunk],
                    (((1,), (1,)), ((), ())),
                    preferred_element_type=F32,
                )
                total = part if total is None else total + part
    out_ref[...] = total


def add_input_grad(slabs, weights, total):
    rows, half = slabs[0].shape
    model = weights[0].shape[1] // 2
    tile = rows // 2
    operands = [*slabs, *weights] + ([] if total is None else [total])
    lines = lambda n: pl.BlockSpec((tile, n), lambda s: (s, 0))
    return pl.pallas_call(
        functools.partial(input_grad_kernel, total is not None),
        grid=(2,),
        out_shape=jax.ShapeDtypeStruct((rows, model), F32),
        in_specs=[lines(half)] * 2
        + [whole(w.shape) for w in weights]
        + ([] if total is None else [lines(model)]),
        out_specs=lines(model),
        compiler_params=pltpu.CompilerParams(vmem_limit_bytes=24 * 2**20),
        cost_estimate=LIGHT,
        name="input_gradient",
    )(*operands)


def after(values):
    return lax.optimization_barrier(values)


def one_direction(inputs, reset_flags, gate_weight, gate_bias, proj_weight, grad_out):
    row, col = lax.axis_index("rows"), lax.axis_index("cols")
    layer, core = row // 2, row % 2
    direction, pair = layer // 2, layer % 2
    model = inputs.shape[1]
    local = inputs.shape[0] // STEPS
    share = local // 4
    rows = 2 * share
    cells = gate_weight.shape[3]
    piece = cells // PARTS
    width = 4 * piece
    tiles = piece // LANES

    def mask_of(r, near):
        odd = (r // 2) % 2
        return (2 if odd else 1) if near else (1 if odd else 2)

    def over_chips(value, near):
        pairs = [(r * 4 + j, r * 4 + (j ^ mask_of(r, near))) for r in range(8) for j in range(4)]
        return lax.ppermute(value, ("rows", "cols"), pairs)

    def over_rows(value, mask):
        return lax.ppermute(value, "rows", [(r, r ^ mask) for r in range(8)])

    core_swap = functools.partial(over_rows, mask=1)
    pair_swap = functools.partial(over_rows, mask=2)
    half_swap = functools.partial(over_rows, mask=4)
    near_mask = jnp.where(pair == 0, 1, 2)
    block_at = [col, col ^ near_mask, col ^ (3 - near_mask), col ^ 3]
    by_dir = lambda pair_of: jnp.where(direction == 0, pair_of[0], pair_of[1])
    by_other = lambda pair_of: jnp.where(direction == 0, pair_of[1], pair_of[0])
    in_run = lambda value: jnp.where(direction == 0, value, value[::-1])

    order = jnp.stack([direction, core, pair]).astype(jnp.int32)

    def place_of(part):
        return jnp.stack([direction, (core ^ (part // 2)) * 2 + (pair ^ (part % 2))]).astype(jnp.int32)

    places = [place_of(part) for part in range(PARTS)]
    input_piece = lambda part: own_piece(places[part], gate_weight, gate_bias, False)
    recurrent_piece = lambda part: own_piece(places[part], gate_weight, proj_weight, True)

    local_windows = lambda value: lax.dynamic_slice_in_dim(value, col * share, share, 0)
    steps_first = lambda value: jnp.swapaxes(value, 0, 1)
    by_side = lambda k, there: [jnp.where(core == which, k, there) for which in range(2)]

    w_in = {(0, 0): own_piece(places[0], gate_weight, gate_bias, False, memory=60)}
    w_rec = {}
    w_in[1, 0] = over_chips(w_in[0, 0], True)
    w_in[2, 0] = over_chips(w_in[0, 0], False)
    w_rec[0, 0] = recurrent_piece(0)

    keep_grid = local_windows(reset_flags.reshape(local, STEPS)).astype(F32)
    position = lax.broadcasted_iota(jnp.int32, (share, STEPS), 1)
    keep_ahead = jnp.where(position > 0, 1.0 - keep_grid, 0.0)
    next_flags = jnp.concatenate([keep_grid[:, 1:], jnp.zeros((share, 1), F32)], axis=1)
    keep_behind = jnp.where(position < STEPS - 1, 1.0 - next_flags, 0.0)
    own_tokens = share * STEPS
    x_mine = lax.dynamic_slice_in_dim(inputs, col * own_tokens, own_tokens, 0).reshape(share, STEPS, model)
    x_mine = steps_first(x_mine)
    keep_dirs = (steps_first(keep_ahead), steps_first(keep_behind))
    keep_wide = [jnp.broadcast_to(k[..., None], (STEPS, share, LANES)).astype(BF16) for k in keep_dirs]
    xk_here = jnp.concatenate([x_mine, by_dir(keep_wide)], axis=2)
    xk_sent = jnp.concatenate([x_mine, by_other(keep_wide)], axis=2)
    xk_met = half_swap(xk_sent)
    w_in[0, 1] = input_piece(1)
    g_mine = lax.dynamic_slice_in_dim(grad_out, col * own_tokens, own_tokens, 0).reshape(share, STEPS, 2, model)
    g_dirs = (steps_first(g_mine[:, :, 0]), steps_first(g_mine[:, :, 1]))
    w_in, w_rec, xk_here, xk_met, g_dirs, places = after((w_in, w_rec, xk_here, xk_met, g_dirs, places))

    w_rec[1, 0] = over_chips(w_rec[0, 0], True)
    w_in[3, 0] = over_chips(w_in[1, 0], False)
    w_in[2, 1] = pair_swap(w_in[1, 0])
    for b in (1, 2):
        w_in[b, 2] = core_swap(w_in[b, 0])
    w_rec[0, 1], w_in[0, 2], w_in[0, 3] = recurrent_piece(1), input_piece(2), input_piece(3)
    xk = in_run(jnp.concatenate([xk_here, xk_met], axis=1))
    x_run, keep_run = xk[..., :model], xk[..., model:].astype(F32)
    x_flat = x_run.reshape(STEPS * rows, model)
    w_in, w_rec, x_flat, keep_run, g_dirs, places = after((w_in, w_rec, x_flat, keep_run, g_dirs, places))

    gates_of = lambda b: input_gates(x_flat, [w_in[b, part] for part in range(PARTS)])
    turn_of = lambda b: turn([w_rec[b, part] for part in range(PARTS)])
    w_in[1, 1] = over_chips(w_in[0, 1], True)
    w_rec[3, 0] = over_chips(w_rec[1, 0], False)
    w_in[3, 1] = pair_swap(w_in[3, 0])
    w_rec[1, 2], w_in[3, 2] = core_swap(w_rec[1, 0]), core_swap(w_in[3, 0])
    w_rec[0, 2], w_rec[0, 3] = recurrent_piece(2), recurrent_piece(3)
    px, turned = {0: gates_of(0)}, {}
    w_in, w_rec, px, x_flat = after((w_in, w_rec, px, x_flat))

    w_rec[1, 1] = over_chips(w_rec[0, 1], True)
    w_rec[2, 0] = over_chips(w_rec[0, 0], False)
    w_rec[2, 1] = pair_swap(w_rec[1, 0])
    for b in (1, 2, 3):
        w_in[b, 3] = core_swap(w_in[b, 1])
    turned[0] = turn_of(0)
    for b in (1, 2, 3):
        px[b] = gates_of(b)
    w_in, w_rec, px, turned, x_flat = after((w_in, w_rec, px, turned, x_flat))

    last_half = w_rec[3, 0].shape[0] // 2
    last_piece = [pair_swap(w_rec[3, 0][:last_half]), over_chips(w_rec[1, 1][last_half:], False)]
    w_rec[1, 3], w_rec[2, 2] = core_swap(w_rec[1, 1]), core_swap(w_rec[2, 0])
    w_rec[2, 3], w_rec[3, 2] = core_swap(w_rec[2, 1]), core_swap(w_rec[3, 0])
    x_met = core_swap(x_flat)
    turned[1], turned[2] = turn_of(1), turn_of(2)
    w_rec, turned, last_piece, x_met = after((w_rec, turned, last_piece, x_met))

    w_rec[3, 1] = jnp.concatenate(last_piece, axis=0)
    w_rec[3, 3] = core_swap(w_rec[3, 1])
    turned[3] = turn_of(3)
    x_turned = turn_rows(x_flat, x_met)
    g_sent = by_other(g_dirs)
    w_rec, turned, x_turned, g_sent = after((w_rec, turned, x_turned, g_sent))

    g_met = half_swap(g_sent)
    px = [px[b].reshape(STEPS, rows, PARTS * width) for b in range(BLOCKS)]
    pre, cell, emit_own, emit_far, raw, kept, hid = run_forward(
        px, keep_run, [w_rec[b, part] for b in range(BLOCKS) for part in range(PARTS)]
    )

    pre, cell, emit_own, emit_far, raw, kept, hid, g_met = after((pre, cell, emit_own, emit_far, raw, kept, hid, g_met))
    g_run = in_run(jnp.concatenate([by_dir(g_dirs), g_met], axis=1))

    flat = lambda value: value.reshape(STEPS * rows, value.shape[-1])
    hid_time = in_run(hid)
    hid_here, hid_there = hid_time[:, :share], half_swap(hid_time[:, share:])
    emit_met = core_swap(flat(emit_far))
    kept = flat(kept)
    kept_met = core_swap(kept)

    def over_cols(value, mask):
        return lax.ppermute(value, "cols", [(j, j ^ mask) for j in range(4)])

    slabs, draw, bias_sums = run_backward(
        pre,
        cell,
        raw,
        g_run,
        keep_run,
        [w for b in range(BLOCKS) for w in turned[b][0]],
        [p for b in range(BLOCKS) for p in turned[b][1]],
    )
    hid_here, hid_there, kept, kept_met, slabs, draw, bias_sums, emit_own, emit_met = after(
        (hid_here, hid_there, kept, kept_met, slabs, draw, bias_sums, emit_own, emit_met)
    )

    slabs = [[flat(value) for value in block] for block in slabs]
    emit_own, draw = flat(emit_own), flat(draw)
    bias_parts = jnp.sum(bias_sums, axis=0).reshape(BLOCKS, 4, 2, 2 * piece)
    bias_half = bias_parts[:, :, 0] + core_swap(bias_parts[:, :, 1])
    draw_met, far = core_swap(draw), {3: core_swap(slabs[3][1])}
    far[1] = core_swap(after((slabs[1][1], draw_met))[0])
    kept_turned, draw_turned = turn_rows(kept, kept_met), turn_rows(draw, draw_met)

    def grads(b):
        left = (x_turned, kept_turned, draw_turned)
        return block_grads(order, *left, slabs[b][0], far[b], emit_own, emit_met, b)

    def add(first, *others):
        total = first.astype(F32)
        for other in others:
            total = total + other.astype(F32)
        return total.astype(BF16)

    def flip(value):
        return jnp.concatenate([value[1:], value[:1]], axis=0)

    opposite = grads(3)
    far, opposite, kept_turned, draw_turned, slabs, bias_half = after(
        (far, opposite, kept_turned, draw_turned, slabs, bias_half)
    )

    relay_a, relay_b = over_chips(opposite[0], True), over_chips(opposite[1], False)
    met = pair_swap(opposite[3])
    far[2] = core_swap(slabs[2][1])
    bias_met = [over_chips(bias_half[1], True), over_chips(bias_half[2], False)]
    near = grads(1)
    other = grads(2)
    hid_both = jnp.concatenate([by_dir((hid_here, hid_there)), by_other((hid_here, hid_there))], axis=2)
    hid_both = steps_first(hid_both).reshape(own_tokens, 2 * model)
    far, relay_a, relay_b, met, near, other, slabs, bias_met, hid_both = after(
        (far, relay_a, relay_b, met, near, other, slabs, bias_met, hid_both)
    )

    near_a, other_b = over_chips(near[0], True), over_chips(other[1], False)
    other_met = pair_swap(near[3])
    far[0] = core_swap(slabs[0][1])
    bias_met = bias_met + [over_cols(bias_half[3], 3)]
    near_b, other_a = add(near[1], relay_b), add(other[0], relay_a)
    opposite1 = add(opposite[2], flip(met))
    own = grads(0)
    near1, other1, own0, own1 = near[2:], other[2:], own[:2], own[2:]
    near_a, other_b, other_met, opposite1, near_b, other_a, other1, own0, own1, slabs, bias_met = after(
        (near_a, other_b, other_met, opposite1, near_b, other_a, other1, own0, own1, slabs, bias_met)
    )

    near_b, other_a = over_chips(near_b, True), over_chips(other_a, False)
    near_met = pair_swap(other1[1])
    wide = None
    for b in range(BLOCKS):
        wide = add_input_grad(slabs[b], [w_in[b, part] for part in range(PARTS)], wide)
    bias_half = bias_half[0] + bias_met[0] + bias_met[1] + bias_met[2]
    bias_half = jnp.where(pair == 0, bias_half, jnp.concatenate([bias_half[:, piece:], bias_half[:, :piece]], axis=1))
    bias_met = pair_swap(bias_half)
    own0 = [add(own0[0], near_a), add(own0[1], other_b)]
    other_a1, other_b1 = add(other1[0][0], other_met[1]), add(other1[0][1], other_met[0])
    dx = in_run(wide.reshape(STEPS, rows, model))
    dx, dx_sent = dx[:, :share], dx[:, share:].astype(BF16)
    near_b, other_a, near_met, dx, dx_sent, own0, own1, bias_met, other_a1, other_b1 = after(
        (near_b, other_a, near_met, dx, dx_sent, own0, own1, bias_met, other_a1, other_b1)
    )

    relay_a, relay_b = over_chips(opposite1[0], True), over_chips(opposite1[1], False)
    near_a1, near_b1 = add(near1[0][0], near_met[1]), add(near1[0][1], near_met[0])
    near_a1, other_b1 = over_chips(near_a1, True), over_chips(other_b1, False)
    count = own0[0].shape[0] // 2
    sums0_met = pair_swap(jnp.stack([add(own0[0][count:], other_a[count:]), add(own0[1][count:], near_b[count:])]))
    sums0 = [add(own0[0][:count], other_a[:count]), add(own0[1][:count], near_b[:count])]
    bias_half = bias_half + bias_met
    lines, rest = [], bias_half
    for _ in range(3):
        lines.append(lax.reduce_precision(rest, 8, 7))
        rest = rest - lines[-1]
    lines = jnp.concatenate(lines + [jnp.zeros_like(rest)], axis=0).astype(BF16)
    dx_met = half_swap(jnp.concatenate([dx_sent.reshape(own_tokens, model), lines], axis=0))
    near_a1, near_b1, other_a1, other_b1, relay_a, relay_b, sums0, sums0_met, dx, dx_met, own1, bias_half = after(
        (near_a1, near_b1, other_a1, other_b1, relay_a, relay_b, sums0, sums0_met, dx, dx_met, own1, bias_half)
    )

    near_b1, other_a1 = over_chips(add(near_b1, relay_b), True), over_chips(add(other_a1, relay_a), False)
    own_met = pair_swap(own1[1])
    sums0_sent = jnp.stack([add(sums0[n][2:], sums0_met[1 - n][2:]) for n in range(2)])
    there0 = half_swap(sums0_sent)
    here0 = jnp.stack([add(sums0[n][:2], sums0_met[1 - n][:2]) for n in range(2)])
    bias_there = dx_met[own_tokens:].astype(F32).reshape(4, 4, 2 * piece)
    bias_there = bias_there[0] + bias_there[1] + bias_there[2]
    bias_half = jnp.stack([by_dir((bias_half, bias_there)), by_other((bias_half, bias_there))])
    dx_met = dx_met[:own_tokens].reshape(STEPS, share, model)
    dx = dx + dx_met.astype(F32) + g_dirs[0].astype(F32) + g_dirs[1].astype(F32)
    dx = steps_first(dx.astype(BF16)).reshape(own_tokens, model)
    share_width = model // 4
    slice_for = lambda mask: lax.dynamic_slice_in_dim(dx, (col ^ mask) * share_width, share_width, 1)
    outgoing = [jnp.concatenate([hid_both, slice_for(mask)], axis=1) for mask in range(4)]
    incoming = [outgoing[0], None, None, over_cols(outgoing[3], 3)]
    own_a1, own_b1 = add(own1[0][0], near_a1), add(own1[0][1], other_b1)
    near_b1, other_a1, own_met, here0, there0, own_a1, own_b1, incoming[0], incoming[3], outgoing, bias_half = after(
        (near_b1, other_a1, own_met, here0, there0, own_a1, own_b1, incoming[0], incoming[3], outgoing, bias_half)
    )

    parts1 = ((own_a1, own_met[1], other_a1), (own_b1, own_met[0], near_b1))
    there1 = half_swap(jnp.stack([add(*(value[2:] for value in parts)) for parts in parts1]))
    here1 = jnp.stack([add(*(value[:2] for value in parts)) for parts in parts1])

    def two_directions(here, there):
        both = jnp.stack([here, there])
        return both[:, :, 0], both[:, :, 1]

    kept0, sent0 = two_directions(here0, there0)
    met0 = core_swap(sent0)
    incoming[1], incoming[2] = over_cols(outgoing[1], 1), over_cols(outgoing[2], 2)
    block_out = layer_sum(col, inputs, [value[:, : 2 * model] for value in incoming])
    input_grad = jnp.zeros((BLOCKS * own_tokens, share_width), BF16)
    for mask, value in enumerate(incoming):
        input_grad = lax.dynamic_update_slice(input_grad, value[:, 2 * model :], ((col ^ mask) * own_tokens, 0))
    bias_total = jnp.concatenate(by_side(bias_half, core_swap(bias_half)), axis=2)
    here1, there1, kept0, met0, block_out, input_grad, bias_total = after(
        (here1, there1, kept0, met0, block_out, input_grad, bias_total)
    )

    kept1, sent1 = two_directions(here1, there1)
    met1 = core_swap(sent1)
    weight_share, proj_share = assemble(order, kept0, kept1, met0, met1, 2 * model // 8)
    proj_share = jnp.swapaxes(proj_share, 1, 2)
    return (block_out, input_grad, weight_share, bias_total, proj_share)


def solution(mesh):
    placed = (
        P("rows", None),
        P("rows"),
        P(None, None, None, "cols"),
        P(None, None, "cols"),
        P(None, "cols", None),
        P("rows", None, None),
    )
    plan = one_direction if (mesh.shape["rows"], mesh.shape["cols"]) == (8, 4) else shared_cells
    return jax.shard_map(
        plan,
        mesh=mesh,
        in_specs=placed,
        out_specs=(
            P("rows", None, None),
            P("rows", "cols"),
            P(None, "rows", None, "cols"),
            P(None, None, "cols"),
            P(None, "cols", "rows"),
        ),
        check_vma=False,
    )
```

```python
import functools

import jax
import jax.numpy as jnp
from jax import lax
from jax.experimental import pallas as pl
from jax.experimental.pallas import tpu as pltpu
from jax.sharding import PartitionSpec as P

STEPS = 20
BF16 = jnp.bfloat16
F32 = jnp.float32
THIRD = 1.0 / 3.0
LANES = 128
BLOCKS = 4
LIGHT = pl.CostEstimate(flops=1, bytes_accessed=1, transcendentals=0)
PARTS = 4


def soft_clip(amount):
    return 3.0 * jnp.tanh(amount / 3.0)


def clip_slope(amount):
    tangent = jnp.tanh(amount / 3.0)
    return 1.0 - tangent * tangent


def shared_cells(inputs, reset_flags, gate_weight, gate_bias, proj_weight, grad_out):
    tok_rows, model_width = inputs.shape
    windows = tok_rows // STEPS
    cell_cols = gate_weight.shape[3]
    gate_width = 4 * cell_cols
    share_width = model_width // lax.axis_size("cols")
    column = lax.axis_index("cols") * share_width
    weight = gate_weight.reshape(2, 2 * model_width, gate_width)
    w_input = weight[:, :model_width]
    w_recur = weight[:, model_width:]
    bias_row = gate_bias.reshape(2, 1, gate_width)
    sequence = jnp.swapaxes(inputs.reshape(windows, STEPS, model_width), 0, 1)
    x_stack = jnp.stack([sequence, sequence[::-1]], axis=1)
    flag_grid = jnp.swapaxes(reset_flags.reshape(windows, STEPS), 0, 1).astype(jnp.float32)
    position = lax.broadcasted_iota(jnp.int32, (STEPS, windows), 0)
    keep_ahead = jnp.where(position > 0, 1.0 - flag_grid, 0.0)
    next_flags = jnp.concatenate([flag_grid[1:], jnp.zeros((1, windows), jnp.float32)], axis=0)
    keep_behind = jnp.where(position < STEPS - 1, 1.0 - next_flags, 0.0)
    keep_stack = jnp.stack([keep_ahead, keep_behind[::-1]], axis=1)[..., None]
    input_gates = jnp.einsum("sdwh,dhg->sdwg", x_stack, w_input, preferred_element_type=jnp.float32)

    def forward_step(state_pair, pieces):
        hidden, cell_prev = state_pair
        gates_in, keep_step = pieces
        kept_hidden = hidden * keep_step.astype(jnp.bfloat16)
        gate_pre = (
            gates_in
            + jnp.einsum("dwh,dhg->dwg", kept_hidden, w_recur, preferred_element_type=jnp.float32)
            + bias_row
        )
        in_gate = jax.nn.sigmoid(gate_pre[..., :cell_cols])
        forget = jax.nn.sigmoid(gate_pre[..., cell_cols : 2 * cell_cols])
        update = jnp.tanh(gate_pre[..., 2 * cell_cols : 3 * cell_cols])
        out_gate = jax.nn.sigmoid(gate_pre[..., 3 * cell_cols :])
        kept_cell = cell_prev * keep_step
        cell_new = soft_clip(forget * kept_cell + in_gate * update)
        cell_output = (out_gate * jnp.tanh(cell_new)).astype(jnp.bfloat16)
        partial_raw = jnp.einsum(
            "dwc,dch->dwh", cell_output, proj_weight, preferred_element_type=jnp.float32
        )
        proj_raw = lax.psum(partial_raw, "cols")
        new_hidden = soft_clip(proj_raw).astype(jnp.bfloat16)
        return (
            (new_hidden, cell_new),
            (kept_hidden, gate_pre, kept_cell, cell_new, cell_output, proj_raw, new_hidden),
        )

    init_state = (
        jnp.zeros((2, windows, model_width), jnp.bfloat16),
        jnp.zeros((2, windows, cell_cols), jnp.float32),
    )
    _, fwd_saved = lax.scan(forward_step, init_state, (input_gates, keep_stack))
    kept_all, pre_all, kept_cells, cell_states, cell_outputs, proj_raws, hiddens = fwd_saved
    ahead_hidden = hiddens[:, 0]
    behind_hidden = hiddens[::-1, 1]
    both_outputs = jnp.stack([ahead_hidden, behind_hidden], axis=2).astype(jnp.float32) + sequence[
        :, :, None, :
    ].astype(jnp.float32)
    block_out = (
        jnp.swapaxes(both_outputs, 0, 1).reshape(tok_rows, 2, model_width).astype(jnp.bfloat16)
    )
    out_grid = jnp.transpose(grad_out.reshape(windows, STEPS, 2, model_width), (1, 2, 0, 3))
    grad_stack = jnp.stack([out_grid[:, 0], out_grid[::-1, 1]], axis=1)

    def backward_step(state_pair, pieces):
        recur_part, cell_grad = state_pair
        gate_pre, kept_cell, cell_new, cell_output, proj_raw, grad_step, keep_step = pieces
        recur_sum = lax.psum(recur_part, "cols")
        hidden_grad = grad_step.astype(jnp.float32) + recur_sum
        raw_grad = (hidden_grad * clip_slope(proj_raw)).astype(jnp.bfloat16)
        emit_grad = jnp.einsum(
            "dwh,dch->dwc", raw_grad, proj_weight, preferred_element_type=jnp.float32
        )
        in_gate = jax.nn.sigmoid(gate_pre[..., :cell_cols])
        forget = jax.nn.sigmoid(gate_pre[..., cell_cols : 2 * cell_cols])
        update = jnp.tanh(gate_pre[..., 2 * cell_cols : 3 * cell_cols])
        out_gate = jax.nn.sigmoid(gate_pre[..., 3 * cell_cols :])
        tanh_cell = jnp.tanh(cell_new)
        cell_total = cell_grad + emit_grad * out_gate * (1.0 - tanh_cell * tanh_cell)
        cell_third = cell_new / 3.0
        cell_raw_grad = cell_total * (1.0 - cell_third * cell_third)
        pre_grad = jnp.concatenate(
            [
                cell_raw_grad * update * in_gate * (1.0 - in_gate),
                cell_raw_grad * kept_cell * forget * (1.0 - forget),
                cell_raw_grad * in_gate * (1.0 - update * update),
                emit_grad * tanh_cell * out_gate * (1.0 - out_gate),
            ],
            axis=-1,
        ).astype(jnp.bfloat16)
        recur_next = (
            jnp.einsum("dwg,dhg->dwh", pre_grad, w_recur, preferred_element_type=jnp.float32)
            * keep_step
        )
        cell_next = cell_raw_grad * forget * keep_step
        return ((recur_next, cell_next), (pre_grad, raw_grad))

    zero_state = (
        jnp.zeros((2, windows, model_width), jnp.float32),
        jnp.zeros((2, windows, cell_cols), jnp.float32),
    )
    _, back_saved = lax.scan(
        backward_step,
        zero_state,
        (pre_all, kept_cells, cell_states, cell_outputs, proj_raws, grad_stack, keep_stack),
        reverse=True,
    )
    pre_grads, raw_grads = back_saved
    input_part = jnp.einsum(
        "sdwg,dhg->sdwh", pre_grads, w_input, preferred_element_type=jnp.float32
    )
    input_sum = jnp.swapaxes(input_part[:, 0] + input_part[::-1, 1], 0, 1).reshape(
        tok_rows, model_width
    )
    input_share = lax.psum_scatter(
        input_sum.astype(jnp.bfloat16), "cols", scatter_dimension=1, tiled=True
    ).astype(jnp.float32)
    residual_grad = grad_out[:, 0].astype(jnp.float32) + grad_out[:, 1].astype(jnp.float32)
    input_grad = (
        input_share + lax.dynamic_slice_in_dim(residual_grad, column, share_width, 1)
    ).astype(jnp.bfloat16)
    input_weight_grad = jnp.einsum(
        "sdwh,sdwg->dhg", x_stack, pre_grads, preferred_element_type=jnp.float32
    )
    recur_weight_grad = jnp.einsum(
        "sdwh,sdwg->dhg", kept_all, pre_grads, preferred_element_type=jnp.float32
    )
    weight_grad = jnp.concatenate([input_weight_grad, recur_weight_grad], axis=1).reshape(
        2, 2 * model_width, 4, cell_cols
    )
    proj_grad = jnp.einsum(
        "sdwc,sdwh->dch", cell_outputs, raw_grads, preferred_element_type=jnp.float32
    )
    bias_grad = jnp.sum(pre_grads, axis=(0, 2), dtype=jnp.float32).reshape(2, 4, cell_cols)
    weight_share, proj_share = (
        lax.psum_scatter(
            weight_grad.astype(jnp.bfloat16), "rows", scatter_dimension=1, tiled=True
        ).astype(jnp.float32),
        lax.psum_scatter(
            proj_grad.astype(jnp.bfloat16), "rows", scatter_dimension=2, tiled=True
        ).astype(jnp.float32),
    )
    bias_total = lax.psum(bias_grad, "rows")
    return (block_out, input_grad, weight_share, bias_total, proj_share)


def sigmoid(amount):
    return 0.5 * jnp.tanh(0.5 * amount) + 0.5


def whole(shape):
    return pl.BlockSpec(shape, lambda *_: (0,) * len(shape), pipeline_mode=pl.Buffered(1))


def matmul(a, b):
    return jnp.dot(a, b, preferred_element_type=F32)


def own_piece_kernel(order_ref, w_ref, extra_ref, out_ref):
    step = pl.program_id(0)
    lines = w_ref.shape[1]
    model, width = extra_ref.shape[-1] if extra_ref.shape[1] > 4 else None, out_ref.shape[1]
    for u in range(2):
        for q in range(4):
            to = (u * 4 + q) * LANES
            out_ref[pl.ds(step * lines, lines), to : to + LANES] = w_ref[0, :, q, u * LANES : (u + 1) * LANES]
    base = width // 2

    @pl.when(step == 0)
    def _():
        if model is None:
            rest = jnp.concatenate(
                [extra_ref[0, q : q + 1, u * LANES : (u + 1) * LANES] for u in range(2) for q in range(4)], axis=1
            )
            parts = []
            for _ in range(3):
                parts.append(rest.astype(BF16).astype(F32))
                rest = rest - parts[-1]
            parts.append(jnp.zeros((13, width), F32))
            out_ref[base:, :] = jnp.concatenate(parts, axis=0).astype(BF16)
        else:
            half = extra_ref.shape[1] // 2
            out_ref[base:, :model] = extra_ref[0, :half, :]
            out_ref[base:, model:] = extra_ref[0, half:, :]


def own_piece(place, gate_weight, extra, recurrent, memory=16):
    model, piece = gate_weight.shape[1] // 2, gate_weight.shape[3] // PARTS
    cut = model // 4
    first = 4 if recurrent else 0
    if recurrent:
        extra_spec = pl.BlockSpec((1, piece, model), lambda n, p: (p[0], p[1], 0))
    else:
        extra_spec = pl.BlockSpec((1, 4, piece), lambda n, p: (p[0], 0, p[1]))
    lines = model + (piece // 2 if recurrent else 16)
    return pl.pallas_call(
        own_piece_kernel,
        grid_spec=pltpu.PrefetchScalarGridSpec(
            num_scalar_prefetch=1,
            grid=(4,),
            in_specs=[pl.BlockSpec((1, cut, 4, piece), lambda n, p: (p[0], n + first, 0, p[1])), extra_spec],
            out_specs=pl.BlockSpec((lines, 4 * piece), lambda n, p: (0, 0)),
        ),
        out_shape=jax.ShapeDtypeStruct((lines, 4 * piece), BF16),
        compiler_params=pltpu.CompilerParams(vmem_limit_bytes=memory * 2**20, dimension_semantics=("arbitrary",)),
        cost_estimate=LIGHT,
        name="own_piece",
    )(place, gate_weight, extra)


def input_kernel(x_ref, w0, w1, w2, w3, out_ref):
    model, width = x_ref.shape[1], w0.shape[1]
    for n, w_ref in enumerate((w0, w1, w2, w3)):
        bias = jnp.sum(w_ref[model:, :].astype(F32), axis=0, keepdims=True)
        out_ref[:, n * width : (n + 1) * width] = (matmul(x_ref[...], w_ref[:model, :]) + bias).astype(BF16)


def input_gates(x, weights):
    rows, model = x.shape
    width = weights[0].shape[1]
    tile = rows // 2
    return pl.pallas_call(
        input_kernel,
        grid=(2,),
        out_shape=jax.ShapeDtypeStruct((rows, PARTS * width), BF16),
        in_specs=[pl.BlockSpec((tile, model), lambda n: (n, 0))] + [whole(w.shape) for w in weights],
        out_specs=pl.BlockSpec((tile, PARTS * width), lambda n: (n, 0)),
        compiler_params=pltpu.CompilerParams(vmem_limit_bytes=20 * 2**20),
        cost_estimate=LIGHT,
        name="input_gates",
    )(x, *weights)


def forward_kernel(*refs):
    px_refs, keep_ref = refs[:BLOCKS], refs[BLOCKS]
    w_refs = refs[BLOCKS + 1 : BLOCKS + 1 + BLOCKS * PARTS]
    pre_out, cell_out, emit_own, emit_far, raw_out, kept_out, hid_out, c_scr, h_scr = refs[BLOCKS + 1 + BLOCKS * PARTS :]
    step = pl.program_id(0)
    width = w_refs[0].shape[1]
    hidden = width // 2
    piece = width // 4
    cells = piece * PARTS
    tiles = piece // LANES
    half = cells // 2
    rows = keep_ref.shape[1]

    @pl.when(step == 0)
    def _():
        c_scr[...] = jnp.zeros_like(c_scr)
        h_scr[...] = jnp.zeros_like(h_scr)

    keep = keep_ref[0][:, :1]
    kept = (h_scr[...] * keep).astype(BF16)
    kept_out[0] = kept
    raw = jnp.zeros((rows, hidden), F32)
    def products(b):
        parts, proj = [], []
        for s in range(PARTS):
            w_ref = w_refs[b * PARTS + s]
            pre = px_refs[b][0, :, s * width : (s + 1) * width].astype(F32) + matmul(kept, w_ref[:hidden, :])
            at = b * 4 * cells + s * width
            pre_out[0, :, at : at + width] = pre.astype(BF16)
            parts.append(pre)
            proj += [w_ref[hidden:, :hidden], w_ref[hidden:, hidden:]]
        return parts, proj

    following = products(0)
    for b in range(BLOCKS):
        parts, proj = following
        if b + 1 < BLOCKS:
            following = products(b + 1)
        gates = [
            jnp.concatenate(
                [part[:, (u * 4 + q) * LANES : (u * 4 + q + 1) * LANES] for part in parts for u in range(tiles)], axis=1
            )
            for q in range(4)
        ]
        i, f, u, o = sigmoid(gates[0]), sigmoid(gates[1]), jnp.tanh(gates[2]), sigmoid(gates[3])
        at = b * cells
        kept_cell = c_scr[:, at : at + cells] * keep
        cell = 3.0 * jnp.tanh((f * kept_cell + i * u) * THIRD)
        emit = (o * jnp.tanh(cell)).astype(BF16)
        c_scr[:, at : at + cells] = cell
        cell_out[0, :, at : at + cells] = cell
        emit_own[0, :, b * half : (b + 1) * half] = emit[:, :half]
        emit_far[0, :, b * half : (b + 1) * half] = emit[:, half:]
        raw = raw + matmul(emit, jnp.concatenate(proj, axis=0))
    raw_out[0] = raw
    hid = 3.0 * jnp.tanh(raw * THIRD)
    h_scr[...] = hid.astype(BF16).astype(F32)
    hid_out[0] = hid.astype(BF16)


def run_forward(px, keep, weights):
    steps, rows, wide = px[0].shape
    hidden = weights[0].shape[1] // 2
    total = BLOCKS * wide // 4
    block = lambda n: pl.BlockSpec((1, rows, n), lambda t: (t, 0, 0))
    sizes = (4 * total, total, total // 2, total // 2, hidden, hidden, hidden)
    kinds = (BF16, F32, BF16, BF16, F32, BF16, BF16)
    return pl.pallas_call(
        forward_kernel,
        grid=(steps,),
        out_shape=tuple(jax.ShapeDtypeStruct((steps, rows, n), kind) for n, kind in zip(sizes, kinds)),
        in_specs=[block(wide)] * BLOCKS + [block(LANES)] + [whole(w.shape) for w in weights],
        out_specs=tuple(block(n) for n in sizes),
        scratch_shapes=[pltpu.VMEM((rows, total), F32), pltpu.VMEM((rows, hidden), F32)],
        compiler_params=pltpu.CompilerParams(vmem_limit_bytes=48 * 2**20, dimension_semantics=("arbitrary",)),
        cost_estimate=pl.CostEstimate(
            flops=2 * steps * rows * hidden * 5 * total * 8,
            bytes_accessed=steps * rows * total * 24 + 10 * total * hidden,
            transcendentals=steps * rows * total * 6,
        ),
        name="forward_chain",
    )(*px, keep, *weights)


def backward_kernel(*refs):
    pre_ref, cell_ref, before_ref, raw_ref, grad_ref, keep_ref = refs[:6]
    wt_refs, pt_refs = refs[6 : 6 + BLOCKS * PARTS], refs[6 + BLOCKS * PARTS : 6 + 2 * BLOCKS * PARTS]
    outs = refs[6 + 2 * BLOCKS * PARTS :]
    slabs, draw_out, bias_out, dc_scr, dk_scr = outs[: 2 * BLOCKS], *outs[2 * BLOCKS :]
    step = pl.program_id(0)
    hidden, piece = pt_refs[0].shape
    cells = piece * PARTS
    tiles = piece // LANES
    width = 4 * piece
    chunk = 4 * LANES
    rows = keep_ref.shape[1]

    @pl.when(step == 0)
    def _():
        dc_scr[...] = jnp.zeros_like(dc_scr)
        dk_scr[...] = jnp.zeros_like(dk_scr)
        bias_out[...] = jnp.zeros_like(bias_out)

    keep = keep_ref[0][:, :1]
    tangent = jnp.tanh(raw_ref[0] * THIRD)
    draw = ((grad_ref[0].astype(F32) + dk_scr[...]) * (1.0 - tangent * tangent)).astype(BF16)
    draw_out[0] = draw
    dk = jnp.zeros((rows, hidden), F32)
    emitted = lambda b: matmul(draw, jnp.concatenate([pt_refs[b * PARTS + s][...] for s in range(PARTS)], axis=1))
    following = emitted(0)
    for b in range(BLOCKS):
        at = b * cells
        demit = following
        if b + 1 < BLOCKS:
            following = emitted(b + 1)
        gates = [
            jnp.concatenate(
                [
                    pre_ref[0, :, 4 * at + s * width + (u * 4 + q) * LANES : 4 * at + s * width + (u * 4 + q + 1) * LANES]
                    for s in range(PARTS)
                    for u in range(tiles)
                ],
                axis=1,
            ).astype(F32)
            for q in range(4)
        ]
        i, f, u, o = sigmoid(gates[0]), sigmoid(gates[1]), jnp.tanh(gates[2]), sigmoid(gates[3])
        cell = cell_ref[0, :, at : at + cells]
        kept_cell = before_ref[0, :, at : at + cells] * keep
        tanh_cell = jnp.tanh(cell)
        third = cell * THIRD
        dcell = (dc_scr[:, at : at + cells] + demit * o * (1.0 - tanh_cell * tanh_cell)) * (1.0 - third * third)
        dgates = (
            dcell * u * i * (1.0 - i),
            dcell * kept_cell * f * (1.0 - f),
            dcell * i * (1.0 - u * u),
            demit * tanh_cell * o * (1.0 - o),
        )
        dc_scr[:, at : at + cells] = dcell * f * keep
        for q in range(4):
            folded = dgates[q][:8]
            for r in range(8, rows, 8):
                folded = folded + dgates[q][r : r + 8]
            bias_out[:, (b * 4 + q) * cells : (b * 4 + q + 1) * cells] += folded
        dgates = [dgate.astype(BF16) for dgate in dgates]
        for s in range(PARTS):
            part = jnp.concatenate(
                [
                    dgates[q][:, s * piece + u * LANES : s * piece + (u + 1) * LANES]
                    for u in range(tiles)
                    for q in range(4)
                ],
                axis=1,
            )
            side, quarter = s // 2, s % 2
            for u in range(tiles):
                to = (u * 2 + quarter) * chunk
                slabs[b * 2 + side][0, :, to : to + chunk] = part[:, u * chunk : (u + 1) * chunk]
            dk = dk + matmul(part, wt_refs[b * PARTS + s][...])
    dk_scr[...] = dk * keep


def run_backward(pre, cell, raw, grad, keep, weights, projs):
    steps, rows, gates = pre.shape
    total = gates // 4
    hidden, piece = projs[0].shape
    half = PARTS * piece * 2
    block = lambda n: pl.BlockSpec((1, rows, n), lambda s: (steps - 1 - s, 0, 0))
    before = pl.BlockSpec((1, rows, total), lambda s: (jnp.maximum(steps - 2 - s, 0), 0, 0))
    shape = lambda n: jax.ShapeDtypeStruct((steps, rows, n), BF16)
    out = pl.pallas_call(
        backward_kernel,
        grid=(steps,),
        out_shape=tuple([shape(half)] * (2 * BLOCKS) + [shape(hidden), jax.ShapeDtypeStruct((8, gates), F32)]),
        in_specs=[block(gates), block(total), before, block(hidden), block(hidden), block(LANES)]
        + [whole(w.shape) for w in [*weights, *projs]],
        out_specs=tuple([block(half)] * (2 * BLOCKS) + [block(hidden), pl.BlockSpec((8, gates), lambda s: (0, 0))]),
        scratch_shapes=[pltpu.VMEM((rows, total), F32), pltpu.VMEM((rows, hidden), F32)],
        compiler_params=pltpu.CompilerParams(vmem_limit_bytes=48 * 2**20, dimension_semantics=("arbitrary",)),
        cost_estimate=pl.CostEstimate(
            flops=2 * steps * rows * hidden * 5 * total * 8,
            bytes_accessed=steps * rows * total * 24 + 10 * total * hidden,
            transcendentals=steps * rows * total * 6,
        ),
        name="backward_chain",
    )(pre, cell, cell, raw, grad, keep, *weights, *projs)
    return [out[b * 2 : b * 2 + 2] for b in range(BLOCKS)], out[2 * BLOCKS], out[2 * BLOCKS + 1]


def block_kernel(order_ref, x_ref, kept_ref, draw_ref, own_ref, far_ref, own_emit, far_emit, *refs):
    first_a, first_b, second_here, second_there, right, emit = refs
    rows = own_ref.shape[0]
    tile, step = pl.program_id(0), pl.program_id(1)
    depth, lines = x_ref.shape[0] // 4, draw_ref.shape[0] // 8
    group = lines // 4
    chunk = 4 * LANES
    here = step ^ order_ref[2]

    @pl.when(step == 0)
    def _():
        right[:rows, :], right[rows:, :] = own_ref[...], far_ref[...]
        for u in range(2):

            @pl.when(tile == u)
            def _():
                for quarter in range(2):
                    to, at = quarter * LANES, (quarter * 2 + u) * LANES
                    emit[:rows, to : to + LANES] = own_emit[:, at : at + LANES]
                    emit[rows:, to : to + LANES] = far_emit[:, at : at + LANES]

    def body(outs):
        for half, left_ref in enumerate((x_ref, kept_ref)):
            left = left_ref[pl.ds(here * (2 * depth), 2 * depth), :]
            dp = matmul(draw_ref[pl.ds((half * 2 + here) * (2 * lines), 2 * lines), :], emit[...]).astype(BF16)
            for quarter, out in enumerate(outs):
                dw = matmul(left, right[:, quarter * chunk : (quarter + 1) * chunk]).astype(BF16)
                for side in range(2):
                    to = (half ^ order_ref[0]) * 2 + (side ^ order_ref[1])
                    out[to, :depth, :] = dw[side * depth : (side + 1) * depth]
                    for g in range(4):
                        at = side * lines + g * group
                        out[to, depth : depth + group, g * LANES : (g + 1) * LANES] = dp[
                            at : at + group, quarter * LANES : (quarter + 1) * LANES
                        ]

    pl.when(tile == 0)(lambda: body((first_a, first_b)))
    pl.when((tile == 1) & (step == 0))(lambda: body((second_here.at[0], second_here.at[1])))
    pl.when((tile == 1) & (step == 1))(lambda: body((second_there.at[0], second_there.at[1])))


def block_grads(order, x_turned, kept_turned, draw_turned, own, far, emit_own, emit_far, b):
    rows = own.shape[0]
    chunk = 4 * LANES
    depth, lines = x_turned.shape[0] // 4, draw_turned.shape[0] // 8
    high = depth + lines // 4
    emit = pl.BlockSpec((rows, 4 * LANES), lambda u, n, o: (0, b))
    slab = pl.BlockSpec((rows, 2 * chunk), lambda u, n, o: (0, u))
    left = pl.BlockSpec(memory_space=pltpu.VMEM)
    first = pl.BlockSpec((4, high, chunk), lambda u, n, o: (jnp.where(u == 0, n, 1), 0, 0))
    second = pl.BlockSpec((2, 4, high, chunk), lambda u, n, o: (0, 0, 0, 0))
    return pl.pallas_call(
        block_kernel,
        grid_spec=pltpu.PrefetchScalarGridSpec(
            num_scalar_prefetch=1,
            grid=(2, 2),
            in_specs=[left, left, left, slab, slab, emit, emit],
            out_specs=[first, first, second, second],
            scratch_shapes=[pltpu.VMEM((2 * rows, 2 * chunk), BF16), pltpu.VMEM((2 * rows, 2 * LANES), BF16)],
        ),
        out_shape=[jax.ShapeDtypeStruct((8, high, chunk), BF16)] * 2
        + [jax.ShapeDtypeStruct((2, 4, high, chunk), BF16)] * 2,
        compiler_params=pltpu.CompilerParams(vmem_limit_bytes=54 * 2**20, dimension_semantics=("arbitrary",) * 2),
        cost_estimate=LIGHT,
        name="weight_gradients",
    )(order, x_turned, kept_turned, draw_turned, own, far, emit_own, emit_far)


def layer_kernel(col_ref, x_ref, *refs):
    hid_refs, out_ref = refs[:4], refs[4]
    model = x_ref.shape[1]
    mask = pl.program_id(0) ^ col_ref[0]
    x = x_ref[...].astype(F32)

    def body(hid_ref):
        for d in range(2):
            out_ref[:, d, :] = (x + hid_ref[:, d * model : (d + 1) * model].astype(F32)).astype(BF16)

    for n in range(4):
        pl.when(mask == n)(functools.partial(body, hid_refs[n]))


def layer_sum(col, x, hiddens):
    rows, wide = hiddens[0].shape
    model = x.shape[1]
    return pl.pallas_call(
        layer_kernel,
        grid_spec=pltpu.PrefetchScalarGridSpec(
            num_scalar_prefetch=1,
            grid=(4,),
            in_specs=[pl.BlockSpec((rows, model), lambda n, c: (n, 0))] + [whole((rows, wide))] * 4,
            out_specs=pl.BlockSpec((rows, 2, model), lambda n, c: (n, 0, 0)),
        ),
        out_shape=jax.ShapeDtypeStruct((x.shape[0], 2, model), BF16),
        compiler_params=pltpu.CompilerParams(vmem_limit_bytes=16 * 2**20),
        cost_estimate=LIGHT,
        name="layer_sum",
    )(col.reshape(1).astype(jnp.int32), x, *hiddens)


def turn_rows_kernel(own_ref, met_ref, out_ref):
    rows = own_ref.shape[0]
    out_ref[:, :rows] = jnp.swapaxes(own_ref[...], 0, 1)
    out_ref[:, rows:] = jnp.swapaxes(met_ref[...], 0, 1)


def turn_rows(own, met):
    rows, wide = own.shape
    return pl.pallas_call(
        turn_rows_kernel,
        grid=(2,),
        out_shape=jax.ShapeDtypeStruct((wide, 2 * rows), BF16),
        in_specs=[pl.BlockSpec((rows, wide // 2), lambda n: (0, n))] * 2,
        out_specs=pl.BlockSpec((wide // 2, 2 * rows), lambda n: (n, 0)),
        compiler_params=pltpu.CompilerParams(vmem_limit_bytes=16 * 2**20),
        cost_estimate=LIGHT,
        name="turn_rows",
    )(own, met)


def turn_kernel(*refs):
    w_refs, p_refs, wt_refs, pt_refs = (refs[n * PARTS : (n + 1) * PARTS] for n in range(4))
    for source, target in zip(w_refs, wt_refs):
        target[...] = jnp.swapaxes(source[...], 0, 1)

    @pl.when(pl.program_id(0) == 0)
    def _():
        for source, target in zip(p_refs, pt_refs):
            lines, hidden = source.shape[0], source.shape[1] // 2
            target[:, :lines] = jnp.swapaxes(source[:, :hidden], 0, 1)
            target[:, lines:] = jnp.swapaxes(source[:, hidden:], 0, 1)


def turn(pieces):
    width = pieces[0].shape[1]
    hidden, piece = width // 2, width // 4
    cut = width // 4
    results = pl.pallas_call(
        turn_kernel,
        grid=(4,),
        out_shape=[jax.ShapeDtypeStruct((width, hidden), BF16)] * PARTS
        + [jax.ShapeDtypeStruct((hidden, piece), BF16)] * PARTS,
        in_specs=[pl.BlockSpec((hidden, cut), lambda n: (0, n))] * PARTS
        + [pl.BlockSpec((piece // 2, width), lambda n: (2 * hidden // piece, 0))] * PARTS,
        out_specs=[pl.BlockSpec((cut, hidden), lambda n: (n, 0))] * PARTS
        + [pl.BlockSpec((hidden, piece), lambda n: (0, 0))] * PARTS,
        compiler_params=pltpu.CompilerParams(vmem_limit_bytes=20 * 2**20, dimension_semantics=("arbitrary",)),
        cost_estimate=LIGHT,
        name="turn_pieces",
    )(*pieces, *pieces)
    return results[:PARTS], results[PARTS:]


def assemble_kernel(order_ref, own_ref, far_ref, *refs):
    weight_out, proj_out = refs[-2:]
    depth = weight_out.shape[1]
    group = own_ref.shape[-2] - depth

    def body(tile_ref):
        value = tile_ref[0, 0].astype(F32)
        for q in range(4):
            columns = slice(q * LANES, (q + 1) * LANES)
            weight_out[0, :, q, :] = value[:depth, columns]
            proj_out[0, q * group : (q + 1) * group, :] = value[depth:, columns]

    far = (pl.program_id(1) // 2) ^ order_ref[1]
    pl.when(far == 0)(lambda: body(own_ref))
    pl.when(far == 1)(lambda: body(far_ref))


def assemble(order, own, far, u, depth, before=()):
    lines = own.shape[2]
    group = lines - depth
    cells = 8 * LANES
    piece = pl.BlockSpec((1, 1, lines, 4 * LANES), lambda d, n, o: (d ^ o[0], (n % 2) ^ o[2], 0, 0))
    return pl.pallas_call(
        assemble_kernel,
        grid_spec=pltpu.PrefetchScalarGridSpec(
            num_scalar_prefetch=1,
            grid=(2, 4),
            in_specs=[piece] * 2 + [pl.BlockSpec(memory_space=pl.ANY)] * len(before),
            out_specs=[
                pl.BlockSpec((1, depth, 4, LANES), lambda d, n, o: (d, 0, 0, n * 2 + u)),
                pl.BlockSpec((1, 4 * group, LANES), lambda d, n, o: (d, 0, n * 2 + u)),
            ],
        ),
        out_shape=[
            jax.ShapeDtypeStruct((2, depth, 4, cells), F32),
            jax.ShapeDtypeStruct((2, 4 * group, cells), F32),
        ],
        input_output_aliases={3 + n: n for n in range(len(before))},
        compiler_params=pltpu.CompilerParams(vmem_limit_bytes=16 * 2**20),
        cost_estimate=LIGHT,
        name="assemble_gradients",
    )(order, own, far, *before)


def input_grad_kernel(has_sum, *refs):
    slab_refs, w_refs, out_ref = refs[:2], refs[2:6], refs[-1]
    chunk = 4 * LANES
    model = out_ref.shape[1]
    total = refs[6][...] if has_sum else None
    for side in range(2):
        for u in range(2):
            for quarter in range(2):
                at = (u * 2 + quarter) * chunk
                part = lax.dot_general(
                    slab_refs[side][:, at : at + chunk],
                    w_refs[side * 2 + quarter][:model, u * chunk : (u + 1) * chunk],
                    (((1,), (1,)), ((), ())),
                    preferred_element_type=F32,
                )
                total = part if total is None else total + part
    out_ref[...] = total


def add_input_grad(slabs, weights, total):
    rows, half = slabs[0].shape
    model = weights[0].shape[1] // 2
    tile = rows // 2
    operands = [*slabs, *weights] + ([] if total is None else [total])
    lines = lambda n: pl.BlockSpec((tile, n), lambda s: (s, 0))
    return pl.pallas_call(
        functools.partial(input_grad_kernel, total is not None),
        grid=(2,),
        out_shape=jax.ShapeDtypeStruct((rows, model), F32),
        in_specs=[lines(half)] * 2
        + [whole(w.shape) for w in weights]
        + ([] if total is None else [lines(model)]),
        out_specs=lines(model),
        compiler_params=pltpu.CompilerParams(vmem_limit_bytes=24 * 2**20),
        cost_estimate=LIGHT,
        name="input_gradient",
    )(*operands)


def after(values):
    return lax.optimization_barrier(values)


def one_direction(inputs, reset_flags, gate_weight, gate_bias, proj_weight, grad_out):
    row, col = lax.axis_index("rows"), lax.axis_index("cols")
    layer, core = row // 2, row % 2
    direction, pair = layer // 2, layer % 2
    model = inputs.shape[1]
    local = inputs.shape[0] // STEPS
    share = local // 4
    rows = 2 * share
    cells = gate_weight.shape[3]
    piece = cells // PARTS
    width = 4 * piece
    tiles = piece // LANES

    def mask_of(r, near):
        odd = (r // 2) % 2
        return (2 if odd else 1) if near else (1 if odd else 2)

    def over_chips(value, near):
        pairs = [(r * 4 + j, r * 4 + (j ^ mask_of(r, near))) for r in range(8) for j in range(4)]
        return lax.ppermute(value, ("rows", "cols"), pairs)

    def over_rows(value, mask):
        return lax.ppermute(value, "rows", [(r, r ^ mask) for r in range(8)])

    core_swap = functools.partial(over_rows, mask=1)
    pair_swap = functools.partial(over_rows, mask=2)
    half_swap = functools.partial(over_rows, mask=4)
    near_mask = jnp.where(pair == 0, 1, 2)
    block_at = [col, col ^ near_mask, col ^ (3 - near_mask), col ^ 3]
    by_dir = lambda pair_of: jnp.where(direction == 0, pair_of[0], pair_of[1])
    by_other = lambda pair_of: jnp.where(direction == 0, pair_of[1], pair_of[0])
    in_run = lambda value: jnp.where(direction == 0, value, value[::-1])

    order = jnp.stack([direction, core, pair]).astype(jnp.int32)

    def place_of(part):
        return jnp.stack([direction, (core ^ (part // 2)) * 2 + (pair ^ (part % 2))]).astype(jnp.int32)

    places = [place_of(part) for part in range(PARTS)]
    input_piece = lambda part: own_piece(places[part], gate_weight, gate_bias, False)
    recurrent_piece = lambda part: own_piece(places[part], gate_weight, proj_weight, True)

    local_windows = lambda value: lax.dynamic_slice_in_dim(value, col * share, share, 0)
    steps_first = lambda value: jnp.swapaxes(value, 0, 1)
    by_side = lambda k, there: [jnp.where(core == which, k, there) for which in range(2)]

    w_in = {(0, 0): own_piece(places[0], gate_weight, gate_bias, False, memory=60)}
    w_rec = {}
    w_in[1, 0] = over_chips(w_in[0, 0], True)
    w_in[2, 0] = over_chips(w_in[0, 0], False)
    w_rec[0, 0] = recurrent_piece(0)

    keep_grid = local_windows(reset_flags.reshape(local, STEPS)).astype(F32)
    position = lax.broadcasted_iota(jnp.int32, (share, STEPS), 1)
    keep_ahead = jnp.where(position > 0, 1.0 - keep_grid, 0.0)
    next_flags = jnp.concatenate([keep_grid[:, 1:], jnp.zeros((share, 1), F32)], axis=1)
    keep_behind = jnp.where(position < STEPS - 1, 1.0 - next_flags, 0.0)
    own_tokens = share * STEPS
    x_mine = lax.dynamic_slice_in_dim(inputs, col * own_tokens, own_tokens, 0).reshape(share, STEPS, model)
    x_mine = steps_first(x_mine)
    keep_dirs = (steps_first(keep_ahead), steps_first(keep_behind))
    keep_wide = [jnp.broadcast_to(k[..., None], (STEPS, share, LANES)).astype(BF16) for k in keep_dirs]
    xk_here = jnp.concatenate([x_mine, by_dir(keep_wide)], axis=2)
    xk_sent = jnp.concatenate([x_mine, by_other(keep_wide)], axis=2)
    xk_met = half_swap(xk_sent)
    g_mine = lax.dynamic_slice_in_dim(grad_out, col * own_tokens, own_tokens, 0).reshape(share, STEPS, 2, model)
    g_dirs = (steps_first(g_mine[:, :, 0]), steps_first(g_mine[:, :, 1]))
    w_in, w_rec, xk_here, xk_met, g_dirs, places = after((w_in, w_rec, xk_here, xk_met, g_dirs, places))

    w_rec[1, 0] = over_chips(w_rec[0, 0], True)
    w_in[3, 0] = over_chips(w_in[1, 0], False)
    w_in[2, 1] = pair_swap(w_in[1, 0])
    for b in (1, 2):
        w_in[b, 2] = core_swap(w_in[b, 0])
    w_in[0, 1], w_rec[0, 1] = input_piece(1), recurrent_piece(1)
    w_in[0, 2], w_in[0, 3] = input_piece(2), input_piece(3)
    xk = in_run(jnp.concatenate([xk_here, xk_met], axis=1))
    x_run, keep_run = xk[..., :model], xk[..., model:].astype(F32)
    x_flat = x_run.reshape(STEPS * rows, model)
    w_in, w_rec, x_flat, keep_run, g_dirs, places = after((w_in, w_rec, x_flat, keep_run, g_dirs, places))

    gates_of = lambda b: input_gates(x_flat, [w_in[b, part] for part in range(PARTS)])
    turn_of = lambda b: turn([w_rec[b, part] for part in range(PARTS)])
    w_in[1, 1] = over_chips(w_in[0, 1], True)
    w_rec[3, 0] = over_chips(w_rec[1, 0], False)
    w_in[3, 1] = pair_swap(w_in[3, 0])
    w_rec[1, 2], w_in[3, 2] = core_swap(w_rec[1, 0]), core_swap(w_in[3, 0])
    w_rec[0, 2], w_rec[0, 3] = recurrent_piece(2), recurrent_piece(3)
    px, turned = {0: gates_of(0)}, {}
    w_in, w_rec, px, x_flat = after((w_in, w_rec, px, x_flat))

    w_rec[1, 1] = over_chips(w_rec[0, 1], True)
    w_rec[2, 0] = over_chips(w_rec[0, 0], False)
    w_rec[2, 1] = pair_swap(w_rec[1, 0])
    for b in (1, 2, 3):
        w_in[b, 3] = core_swap(w_in[b, 1])
    turned[0] = turn_of(0)
    for b in (1, 2, 3):
        px[b] = gates_of(b)
    w_in, w_rec, px, turned, x_flat = after((w_in, w_rec, px, turned, x_flat))

    last_half = w_rec[3, 0].shape[0] // 2
    last_piece = [pair_swap(w_rec[3, 0][:last_half]), over_chips(w_rec[1, 1][last_half:], False)]
    w_rec[1, 3], w_rec[2, 2] = core_swap(w_rec[1, 1]), core_swap(w_rec[2, 0])
    w_rec[2, 3], w_rec[3, 2] = core_swap(w_rec[2, 1]), core_swap(w_rec[3, 0])
    x_met = core_swap(x_flat)
    turned[1], turned[2] = turn_of(1), turn_of(2)
    w_rec, turned, last_piece, x_met = after((w_rec, turned, last_piece, x_met))

    w_rec[3, 1] = jnp.concatenate(last_piece, axis=0)
    w_rec[3, 3] = core_swap(w_rec[3, 1])
    turned[3] = turn_of(3)
    x_turned = turn_rows(x_flat, x_met)
    g_sent = by_other(g_dirs)
    w_rec, turned, x_turned, g_sent = after((w_rec, turned, x_turned, g_sent))

    g_met = half_swap(g_sent)
    px = [px[b].reshape(STEPS, rows, PARTS * width) for b in range(BLOCKS)]
    pre, cell, emit_own, emit_far, raw, kept, hid = run_forward(
        px, keep_run, [w_rec[b, part] for b in range(BLOCKS) for part in range(PARTS)]
    )

    pre, cell, emit_own, emit_far, raw, kept, hid, g_met = after((pre, cell, emit_own, emit_far, raw, kept, hid, g_met))
    g_run = in_run(jnp.concatenate([by_dir(g_dirs), g_met], axis=1))

    flat = lambda value: value.reshape(STEPS * rows, value.shape[-1])
    hid_time = in_run(hid)
    hid_here, hid_there = hid_time[:, :share], half_swap(hid_time[:, share:])
    emit_met = core_swap(flat(emit_far))
    kept = flat(kept)
    kept_met = core_swap(kept)

    def over_cols(value, mask):
        return lax.ppermute(value, "cols", [(j, j ^ mask) for j in range(4)])

    slabs, draw, bias_sums = run_backward(
        pre,
        cell,
        raw,
        g_run,
        keep_run,
        [w for b in range(BLOCKS) for w in turned[b][0]],
        [p for b in range(BLOCKS) for p in turned[b][1]],
    )
    hid_here, hid_there, kept, kept_met, slabs, draw, bias_sums, emit_own, emit_met = after(
        (hid_here, hid_there, kept, kept_met, slabs, draw, bias_sums, emit_own, emit_met)
    )

    slabs = [[flat(value) for value in block] for block in slabs]
    emit_own, draw = flat(emit_own), flat(draw)
    bias_parts = jnp.sum(bias_sums, axis=0).reshape(BLOCKS, 4, 2, 2 * piece)
    bias_half = bias_parts[:, :, 0] + core_swap(bias_parts[:, :, 1])
    draw_met, far = core_swap(draw), {3: core_swap(slabs[3][1])}
    far[1] = core_swap(after((slabs[1][1], draw_met))[0])
    kept_turned, draw_turned = turn_rows(kept, kept_met), turn_rows(draw, draw_met)

    def grads(b):
        left = (x_turned, kept_turned, draw_turned)
        return block_grads(order, *left, slabs[b][0], far[b], emit_own, emit_met, b)

    def add(first, *others):
        total = first.astype(F32)
        for other in others:
            total = total + other.astype(F32)
        return total.astype(BF16)

    def flip(value):
        return jnp.concatenate([value[1:], value[:1]], axis=0)

    opposite = grads(3)
    far, opposite, kept_turned, draw_turned, slabs, bias_half = after(
        (far, opposite, kept_turned, draw_turned, slabs, bias_half)
    )

    relay_a, relay_b = over_chips(opposite[0], True), over_chips(opposite[1], False)
    met = pair_swap(opposite[3])
    far[2] = core_swap(slabs[2][1])
    bias_met = [over_chips(bias_half[1], True), over_chips(bias_half[2], False)]
    near = grads(1)
    other = grads(2)
    hid_both = jnp.concatenate([by_dir((hid_here, hid_there)), by_other((hid_here, hid_there))], axis=2)
    hid_both = steps_first(hid_both).reshape(own_tokens, 2 * model)
    far, relay_a, relay_b, met, near, other, slabs, bias_met, hid_both = after(
        (far, relay_a, relay_b, met, near, other, slabs, bias_met, hid_both)
    )

    near_a, other_b = over_chips(near[0], True), over_chips(other[1], False)
    other_met = pair_swap(near[3])
    far[0] = core_swap(slabs[0][1])
    bias_met = bias_met + [over_cols(bias_half[3], 3)]
    near_b, other_a = add(near[1], relay_b), add(other[0], relay_a)
    opposite1 = add(opposite[2], flip(met))
    own = grads(0)
    near1, other1, own0, own1 = near[2:], other[2:], own[:2], own[2:]
    near_a, other_b, other_met, opposite1, near_b, other_a, other1, own0, own1, slabs, bias_met = after(
        (near_a, other_b, other_met, opposite1, near_b, other_a, other1, own0, own1, slabs, bias_met)
    )

    near_b, other_a = over_chips(near_b, True), over_chips(other_a, False)
    near_met = pair_swap(other1[1])
    wide = None
    for b in range(BLOCKS):
        wide = add_input_grad(slabs[b], [w_in[b, part] for part in range(PARTS)], wide)
    bias_half = bias_half[0] + bias_met[0] + bias_met[1] + bias_met[2]
    bias_half = jnp.where(pair == 0, bias_half, jnp.concatenate([bias_half[:, piece:], bias_half[:, :piece]], axis=1))
    bias_met = pair_swap(bias_half)
    own0 = [add(own0[0], near_a), add(own0[1], other_b)]
    other_a1, other_b1 = add(other1[0][0], other_met[1]), add(other1[0][1], other_met[0])
    dx = in_run(wide.reshape(STEPS, rows, model))
    dx, dx_sent = dx[:, :share], dx[:, share:].astype(BF16)
    near_b, other_a, near_met, dx, dx_sent, own0, own1, bias_met, other_a1, other_b1 = after(
        (near_b, other_a, near_met, dx, dx_sent, own0, own1, bias_met, other_a1, other_b1)
    )

    relay_a, relay_b = over_chips(opposite1[0], True), over_chips(opposite1[1], False)
    near_a1, near_b1 = add(near1[0][0], near_met[1]), add(near1[0][1], near_met[0])
    near_a1, other_b1 = over_chips(near_a1, True), over_chips(other_b1, False)
    count = own0[0].shape[0] // 2
    sums0_met = pair_swap(jnp.stack([add(own0[0][count:], other_a[count:]), add(own0[1][count:], near_b[count:])]))
    sums0 = [add(own0[0][:count], other_a[:count]), add(own0[1][:count], near_b[:count])]
    bias_half = bias_half + bias_met
    lines, rest = [], bias_half
    for _ in range(3):
        lines.append(lax.reduce_precision(rest, 8, 7))
        rest = rest - lines[-1]
    lines = jnp.concatenate(lines + [jnp.zeros_like(rest)], axis=0).astype(BF16)
    dx_met = half_swap(jnp.concatenate([dx_sent.reshape(own_tokens, model), lines], axis=0))
    near_a1, near_b1, other_a1, other_b1, relay_a, relay_b, sums0, sums0_met, dx, dx_met, own1, bias_half = after(
        (near_a1, near_b1, other_a1, other_b1, relay_a, relay_b, sums0, sums0_met, dx, dx_met, own1, bias_half)
    )

    near_b1, other_a1 = over_chips(add(near_b1, relay_b), True), over_chips(add(other_a1, relay_a), False)
    own_met = pair_swap(own1[1])
    sums0_sent = jnp.stack([add(sums0[n][2:], sums0_met[1 - n][2:]) for n in range(2)])
    there0 = half_swap(sums0_sent)
    here0 = jnp.stack([add(sums0[n][:2], sums0_met[1 - n][:2]) for n in range(2)])
    bias_there = dx_met[own_tokens:].astype(F32).reshape(4, 4, 2 * piece)
    bias_there = bias_there[0] + bias_there[1] + bias_there[2]
    bias_half = jnp.stack([by_dir((bias_half, bias_there)), by_other((bias_half, bias_there))])
    dx_met = dx_met[:own_tokens].reshape(STEPS, share, model)
    dx = dx + dx_met.astype(F32) + g_dirs[0].astype(F32) + g_dirs[1].astype(F32)
    dx = steps_first(dx.astype(BF16)).reshape(own_tokens, model)
    share_width = model // 4
    slice_for = lambda mask: lax.dynamic_slice_in_dim(dx, (col ^ mask) * share_width, share_width, 1)
    outgoing = [jnp.concatenate([hid_both, slice_for(mask)], axis=1) for mask in range(4)]
    incoming = [outgoing[0], None, None, over_cols(outgoing[3], 3)]
    own_a1, own_b1 = add(own1[0][0], near_a1), add(own1[0][1], other_b1)
    near_b1, other_a1, own_met, here0, there0, own_a1, own_b1, incoming[0], incoming[3], outgoing, bias_half = after(
        (near_b1, other_a1, own_met, here0, there0, own_a1, own_b1, incoming[0], incoming[3], outgoing, bias_half)
    )

    parts1 = ((own_a1, own_met[1], other_a1), (own_b1, own_met[0], near_b1))
    there1 = half_swap(jnp.stack([add(*(value[2:] for value in parts)) for parts in parts1]))
    here1 = jnp.stack([add(*(value[:2] for value in parts)) for parts in parts1])

    def two_directions(here, there):
        both = jnp.stack([here, there])
        return both[:, :, 0], both[:, :, 1]

    kept0, sent0 = two_directions(here0, there0)
    met0 = core_swap(sent0)
    incoming[1], incoming[2] = over_cols(outgoing[1], 1), over_cols(outgoing[2], 2)
    block_out = layer_sum(col, inputs, [value[:, : 2 * model] for value in incoming])
    input_grad = jnp.zeros((BLOCKS * own_tokens, share_width), BF16)
    for mask, value in enumerate(incoming):
        input_grad = lax.dynamic_update_slice(input_grad, value[:, 2 * model :], ((col ^ mask) * own_tokens, 0))
    bias_total = jnp.concatenate(by_side(bias_half, core_swap(bias_half)), axis=2)
    shares = assemble(order, kept0, met0, 0, 2 * model // 8)
    here1, there1, shares, block_out, input_grad, bias_total = after(
        (here1, there1, shares, block_out, input_grad, bias_total)
    )

    kept1, sent1 = two_directions(here1, there1)
    met1 = core_swap(sent1)
    weight_share, proj_share = assemble(order, kept1, met1, 1, 2 * model // 8, shares)
    proj_share = jnp.swapaxes(proj_share, 1, 2)
    return (block_out, input_grad, weight_share, bias_total, proj_share)


def solution(mesh):
    placed = (
        P("rows", None),
        P("rows"),
        P(None, None, None, "cols"),
        P(None, None, "cols"),
        P(None, "cols", None),
        P("rows", None, None),
    )
    plan = one_direction if (mesh.shape["rows"], mesh.shape["cols"]) == (8, 4) else shared_cells
    return jax.shard_map(
        plan,
        mesh=mesh,
        in_specs=placed,
        out_specs=(
            P("rows", None, None),
            P("rows", "cols"),
            P(None, "rows", None, "cols"),
            P(None, None, "cols"),
            P(None, "cols", "rows"),
        ),
        check_vma=False,
    )
```
